32 devices in a mesh: dp: 8 (over y, x, core), mp: 4 (over z).
Axes of the slice: x: 2, y: 2, z: 4, core: 2. Of those that a mesh axis runs over, the one named last changes fastest.
Arguments:
- tokens: bfloat16 [28672, 768], P(('dp', 'mp')), may hold values from -6 to 6
- clip_lengths: int32 [32, 8], P('dp'), may hold values from 1 to 256, 896 in all within a row
- gain_attn: bfloat16 [768], replicated, may hold values from 0.099609375 to 1.8984375
- shift_attn: bfloat16 [768], replicated, may hold values from -3 to 3
- w_qkv: bfloat16 [3, 768, 768], P(None, None, 'mp'), may hold values from -0.21875 to 0.21875
- bias_qv: bfloat16 [2, 768], P(None, 'mp'), may hold values from -3 to 3
- w_out: bfloat16 [768, 768], P('mp'), may hold values from -0.875 to 0.875
- bias_out: bfloat16 [768], replicated, may hold values from -2 to 2
- gain_mlp: bfloat16 [768], replicated, may hold values from 0.099609375 to 1.8984375
- shift_mlp: bfloat16 [768], replicated, may hold values from -3 to 3
- w_up: bfloat16 [768, 3072], P(None, 'mp'), may hold values from -0.21875 to 0.21875
- bias_up: bfloat16 [3072], P('mp'), may hold values from -3 to 3
- w_down: bfloat16 [3072, 768], P('mp'), may hold values from -0.109375 to 0.109375
- bias_down: bfloat16 [768], replicated, may hold values from -3 to 3
- cotangent: bfloat16 [28672, 768], P(('dp', 'mp')), may hold values from -6 to 6
Outputs:
- output: bfloat16 [28672, 768], P(('dp', 'mp'))
- grad_tokens: float32 [28672, 768], P(('dp', 'mp'))
- grad_gain_attn: float32 [768], P(('dp', 'mp'))
- grad_shift_attn: float32 [768], P(('dp', 'mp'))
- grad_w_qkv: float32 [3, 768, 768], P(None, 'dp', 'mp')
- grad_bias_qv: float32 [2, 768], P(None, ('mp', 'dp'))
- grad_w_out: float32 [768, 768], P('mp', 'dp')
- grad_bias_out: float32 [768], P(('dp', 'mp'))
- grad_gain_mlp: float32 [768], P(('dp', 'mp'))
- grad_shift_mlp: float32 [768], P(('dp', 'mp'))
- grad_w_up: float32 [768, 3072], P('dp', 'mp')
- grad_bias_up: float32 [3072], P(('mp', 'dp'))
- grad_w_down: float32 [3072, 768], P('mp', 'dp')
- grad_bias_down: float32 [768], P(('dp', 'mp'))
The draws below stay inside these ranges and needn't reach their ends.
Inputs may be any that keep to these rules, and one draw needn't show every extreme that they name: `clip_lengths`: each row's 8 lengths sum to 896, and its longest is exactly 256; the row's last clip is padding.
All inputs are finite; a program needn't handle non-finite values.
Results may differ from the reference program's by a relative error of at most 0.025.
Values may be sent and summed in bfloat16 or wider, within the bound.
No kernel may reach another device: no remote copies, remote signals or barrier semaphores. Data moves between devices by JAX's collectives and lax.ppermute only.
A program may use at most 192 MiB of HBM per device.

```python
import math
from functools import partial
import jax
import jax.numpy as jnp
import numpy as np
from jax import lax

D = 768
HEADS = 12
HEAD_DIM = 64
FF = 3072
SLOTS = 896
CLIPS = 8
MOST = 256
ROWS = 32
TOKENS = 28672


def strengthened(drawn, key, source, target, parts, factor):
    def block_of(position):
        return (jnp.arange(drawn.shape[position]) // (drawn.shape[position] // parts)).reshape((-1,) + (1,) * (drawn.ndim - 1 - position))

    one_side = jax.random.permutation(key, parts)[block_of(target)]
    second = (block_of(target) + parts // 2) % parts
    return jnp.where((block_of(source) == one_side) | (block_of(source) == second), factor * drawn, drawn)


def levels(key, shape, shards, smallest, top_value):
    gain, own = 1.0, jax.random.fold_in(key, 6)
    for axis_at, shards_of in shards:
        draws = jnp.exp(jax.random.uniform(jax.random.fold_in(own, axis_at), (shards_of,), jnp.float32, smallest / len(shards), top_value / len(shards)))
        gain = gain * jnp.repeat(draws, shape[axis_at] // shards_of).reshape([-1 if axis == axis_at else 1 for axis in range(len(shape))])
    return gain


def length_profile(amount, total, most, lean):
    weights = [(1 << 20) // math.isqrt(grade ** lean) + 1 for grade in range(2, amount + 1)]
    spare, given = total - most - (amount - 1), [1] * (amount - 1)
    while spare > 0:
        free = [i for i in range(amount - 1) if given[i] < most]
        pool, left = sum([weights[i] for i in free]), spare
        for i in free:
            more = min(most - given[i], max(1, left * weights[i] // pool), spare)
            given[i] = given[i] + more
            spare = spare - more
    return np.array([most] + given)


def ragged(rng, number_of, total, reach, slope):
    if number_of == 2:
        one = jax.random.randint(rng, (), max(1, total - reach), min(reach, total - 1) + 1)
        return jnp.stack([one, total - one])
    sizes = jnp.asarray(length_profile(number_of, total, reach, slope), jnp.int32)
    couples = (number_of - 1) // 2
    donor, taker = sizes[1:1 + 2 * couples:2], sizes[2:2 + 2 * couples:2]
    margin = jnp.minimum(donor - 1, reach - taker)
    passed = jax.random.randint(jax.random.fold_in(rng, 1), (couples,), 0, 1 << 20) % (margin + 1)
    sizes = sizes.at[1:1 + 2 * couples:2].set(donor - passed).at[2:2 + 2 * couples:2].set(taker + passed)
    return sizes[jax.random.permutation(jax.random.fold_in(rng, 2), number_of)]


def normal_values(stream_key, extent, deviation, most, split=(), kind=jnp.bfloat16):
    entries = jax.random.normal(stream_key, extent, jnp.float32) * deviation
    if len(split) > 0:
        entries = levels(stream_key, extent, split, -0.22, 0.18) * entries
    return jnp.clip(entries, min=-most, max=most).astype(kind)


def bell_draw_with(own_key, extent, width, limit, split, heavy, kind=jnp.bfloat16):
    values = width * jax.random.normal(own_key, extent, jnp.float32)
    if split:
        values = values * levels(own_key, extent, split, -0.22, 0.18)
    return jnp.clip(strengthened(values, jax.random.fold_in(own_key, 3), *heavy), -limit, limit).astype(kind)


def setup_inputs(seed: int = 0) -> dict:
    seeds = jax.random.split(jax.random.key(seed), 16)
    tokens = normal_values(seeds[0], (TOKENS, D), 1.0, 6.0, ((0, 32),))
    clip_lengths = jax.vmap(lambda own: ragged(own, CLIPS, SLOTS, MOST, 2))(jax.random.split(seeds[1], ROWS)).reshape((ROWS, CLIPS)).astype(jnp.int32)
    gain_attn = jnp.clip(1.0 + 0.18 * jax.random.normal(seeds[2], (D,), jnp.float32), 0.099609375, 1.8984375).astype(jnp.bfloat16)
    shift_attn = normal_values(seeds[3], (D,), 0.5, 3.0)
    w_qkv = normal_values(seeds[4], (3, D, D), D ** -0.5, 0.21875, ((2, 4),))
    bias_qv = normal_values(seeds[5], (2, D), 0.5, 3.0, ((1, 4),))
    w_out = normal_values(seeds[6], (D, D), (D // 16) ** -0.5, 0.875, ((0, 4),))
    bias_out = normal_values(seeds[7], (D,), 0.3, 2.0)
    gain_mlp = jnp.clip(1.0 + 0.18 * jax.random.normal(seeds[8], (D,), jnp.float32), 0.099609375, 1.8984375).astype(jnp.bfloat16)
    shift_mlp = normal_values(seeds[9], (D,), 0.5, 3.0)
    w_up = normal_values(seeds[10], (D, FF), D ** -0.5, 0.21875, ((1, 4),))
    bias_up = normal_values(seeds[11], (FF,), 0.5, 3.0, ((0, 4),))
    w_down = normal_values(seeds[12], (FF, D), FF ** -0.5, 0.109375, ((0, 4),))
    bias_down = normal_values(seeds[13], (D,), 0.5, 3.0)
    cotangent = bell_draw_with(seeds[14], (TOKENS, D), 1.0, 6.0, ((0, 32),), (0, 1, 32, 2.75))
    return {"tokens": tokens, "clip_lengths": clip_lengths, "gain_attn": gain_attn, "shift_attn": shift_attn, "w_qkv": w_qkv, "bias_qv": bias_qv, "w_out": w_out, "bias_out": bias_out, "gain_mlp": gain_mlp, "shift_mlp": shift_mlp, "w_up": w_up, "bias_up": bias_up, "w_down": w_down, "bias_down": bias_down, "cotangent": cotangent}


@jax.custom_vjp
def low(v):
    return lax.optimization_barrier(v.astype(jnp.bfloat16)).astype(jnp.float32)

@jax.custom_vjp
def low_back(v):
    return v

def low_keep(v):
    return (low(v), None)

def low_pass(kept, grad):
    return (grad,)

def back_keep(v):
    return (v, None)

def back_low(kept, grad):
    return (low(grad),)
low.defvjp(low_keep, low_pass)
low_back.defvjp(back_keep, back_low)
EPSILON = 1e-06
MASKED = -1e+30
PRECISE = lax.Precision.HIGHEST

def normalize(values_in, gain_row, shift_row):
    centre = lax.optimization_barrier(jnp.mean(values_in, axis=1, keepdims=True))
    centred = values_in - centre
    inverse = lax.rsqrt(lax.optimization_barrier(jnp.mean(centred * centred, axis=1, keepdims=True)) + EPSILON)
    return centred * inverse * gain_row + shift_row

def allowed_pairs(lengths, slot_count):
    clip_ends = jnp.cumsum(lengths)
    places = lax.broadcasted_iota(jnp.int32, (slot_count,), 0)
    segment = lax.optimization_barrier(jnp.sum((clip_ends[None, :] <= places[:, None]).astype(jnp.int32), axis=1))
    padding = segment == lengths.shape[0] - 1
    same_clip = segment[:, None] == segment[None, :]
    return same_clip & (jnp.logical_not(padding)[None, :] | (places[:, None] == places[None, :]))

def attend_row(inputs):
    queries, keys_row, values_row, lengths = inputs
    allowed = allowed_pairs(lengths, queries.shape[0])
    score_scale = queries.shape[2] ** (-0.5)
    scores = low_back(jnp.einsum('ihd,jhd->hij', queries, keys_row, precision=PRECISE) * score_scale)
    scores = jnp.where(allowed[None], scores, MASKED)
    highest = lax.optimization_barrier(jnp.max(scores, axis=2, keepdims=True))
    exponent = jnp.exp(scores - highest)
    totals = lax.optimization_barrier(jnp.sum(exponent, axis=2, keepdims=True))
    weights = low(exponent / totals)
    return jnp.einsum('hij,jhd->ihd', weights, values_row, precision=PRECISE)

def layer(tokens, gain_attn, shift_attn, w_qkv, bias_qv, w_out, bias_out, gain_mlp, shift_mlp, w_up, bias_up, w_down, bias_down, clip_lengths):
    count_rows = clip_lengths.shape[0]
    head_shape = (count_rows, SLOTS, HEADS, HEAD_DIM)
    norm_one = low(normalize(tokens, gain_attn, shift_attn))
    projected = jnp.einsum('td,cde->cte', norm_one, w_qkv, precision=PRECISE)
    queries = low(low_back(projected[0] + bias_qv[0])).reshape(head_shape)
    keys_all = low(low_back(projected[1])).reshape(head_shape)
    values_all = low(low_back(projected[2] + bias_qv[1])).reshape(head_shape)
    attended = lax.map(jax.checkpoint(attend_row), (queries, keys_all, values_all, clip_lengths))
    attended = low(low_back(attended.reshape(count_rows * SLOTS, D)))
    mixed = tokens + low_back(jnp.dot(attended, w_out, precision=PRECISE)) + bias_out
    norm_two = low(normalize(mixed, gain_mlp, shift_mlp))
    hidden_pre = low_back(jnp.dot(norm_two, w_up, precision=PRECISE) + bias_up)
    hidden = low(jax.nn.gelu(hidden_pre, approximate=False))
    return mixed + low_back(jnp.dot(hidden, w_down, precision=PRECISE)) + bias_down

def reference(tokens, clip_lengths, gain_attn, shift_attn, w_qkv, bias_qv, w_out, bias_out, gain_mlp, shift_mlp, w_up, bias_up, w_down, bias_down, cotangent):
    params = tuple((item.astype(jnp.float32) for item in (tokens, gain_attn, shift_attn, w_qkv, bias_qv, w_out, bias_out, gain_mlp, shift_mlp, w_up, bias_up, w_down, bias_down)))
    result, pullback = jax.vjp(partial(layer, clip_lengths=clip_lengths), *params)
    grads = pullback(cotangent.astype(jnp.float32))
    return (result.astype(jnp.bfloat16), grads[0], grads[1], grads[2], grads[3], grads[4], grads[5], grads[6], grads[7], grads[8], grads[9], grads[10], grads[11], grads[12])
```

```python
from functools import partial

import jax
import jax.numpy as jnp
import numpy as np
from jax import lax
from jax.experimental import pallas as pl
from jax.experimental.pallas import tpu as pltpu
from jax.sharding import PartitionSpec as P

F32, BF = jnp.float32, jnp.bfloat16
HEAD_DIM = 64
MOST = 256
EPSILON = 1e-06
MASKED = -1e30
LOG2E = 1.4426950408889634
ROOT_HALF = 0.7071067811865476
RSQRT_2PI = 0.3989422804014327
PARTS = 8
KEY_BLOCK = 128
HIDDEN_BLOCK = 768
VMEM, SMEM, ANY = pltpu.VMEM, pltpu.SMEM, pl.ANY
SDS = jax.ShapeDtypeStruct


def _dot(a, b, i, j):
    return lax.dot_general(a, b, (((i,), (j,)), ((), ())), preferred_element_type=F32)


def nn(a, b):
    return _dot(a, b, 1, 0)


def nt(a, b):
    return _dot(a, b, 1, 1)


def tn(a, b):
    return _dot(a, b, 0, 0)


def tt(a, b):
    return _dot(a, b, 0, 1)


def vm():
    return pl.BlockSpec(memory_space=VMEM)


def cost(us):
    return pl.CostEstimate(flops=int(us * 1.0e9), bytes_accessed=1 << 20, transcendentals=0)


def windows(slots, width=256):
    out = []
    for q0 in range(0, slots, width):
        qn = min(width, slots - q0)
        lo = max(0, (q0 - MOST + 1) // 128 * 128)
        hi = min(slots, -(-(q0 + qn + MOST - 1) // 128) * 128)
        out.append((q0, qn, lo, hi - lo))
    return out


def segments(info, clips, shape, axis):
    place = lax.broadcasted_iota(jnp.int32, shape, axis)
    seg = jnp.zeros(shape, jnp.int32)
    for c in range(clips):
        seg = seg + jnp.where(place >= info[c], 1, 0)
    return jnp.where(seg == clips - 1, place + clips, seg)


def fill_mask(bias_sc, segc, segr, q0, qn, k0, w):
    for b in range(0, w, KEY_BLOCK):
        same = segc[k0 + b : k0 + b + KEY_BLOCK, :] == segr[:, q0 : q0 + qn]
        bias_sc[b : b + KEY_BLOCK, :qn] = jnp.where(same, 0.0, MASKED)


def fold(x, f):
    return f(x.reshape(x.shape[0] // 8, 8, x.shape[1]), axis=0)


def attend(tl, heads, scale, qkvT, kn, segc, segr, oT, lse, bias_sc, s_sc, p_sc):
    e, hd = heads * HEAD_DIM, HEAD_DIM
    for q0, qn, k0, w in tl:
        fill_mask(bias_sc, segc, segr, q0, qn, k0, w)
        for h in range(heads):
            q = qkvT[h * hd : (h + 1) * hd, q0 : q0 + qn]
            m = None
            for b in range(0, w, KEY_BLOCK):
                s = nn(kn[h, k0 + b : k0 + b + KEY_BLOCK, :], q) * scale + bias_sc[b : b + KEY_BLOCK, :qn]
                s_sc[b : b + KEY_BLOCK, :qn] = s
                mb = fold(s, jnp.max)
                m = mb if m is None else jnp.maximum(m, mb)
            m = jnp.max(m, axis=0, keepdims=True)
            total = None
            for b in range(0, w, KEY_BLOCK):
                p = jnp.exp2(s_sc[b : b + KEY_BLOCK, :qn] - m)
                p_sc[b : b + KEY_BLOCK, :qn] = p.astype(BF)
                lb = fold(p, jnp.sum)
                total = lb if total is None else total + lb
            total = jnp.sum(total, axis=0, keepdims=True)
            o = nn(qkvT[2 * e + h * hd : 2 * e + (h + 1) * hd, k0 : k0 + w], p_sc[:w, :qn])
            oT[h * hd : (h + 1) * hd, q0 : q0 + qn] = (o * (1.0 / total)).astype(BF)
            lse[h : h + 1, q0 : q0 + qn] = m + jnp.log2(total)


def unit(x):
    y = x - jnp.mean(x, axis=1, keepdims=True)
    inverse = lax.rsqrt(jnp.mean(y * y, axis=1, keepdims=True) + EPSILON)
    return y * inverse, inverse


def unit_back(up, n, inverse, gain):
    g = up * gain
    return inverse * (g - jnp.mean(g, axis=1, keepdims=True) - n * jnp.mean(g * n, axis=1, keepdims=True))


def normal(u):
    x = jnp.clip(u * ROOT_HALF, -3.832506856900711, 3.832506856900711)
    z = x * x
    a = 0.00022905065861350646
    for c in (0.0034082910107109506, 0.050955695062380861, 0.18520832239976145, 1.128379143519084):
        a = a * z + c
    b = -1.1791602954361697e-7
    for c in (
        0.000023547966471313185,
        0.0010179625278914885,
        0.014070470171167667,
        0.11098505178285362,
        0.49746925110067538,
        1.0,
    ):
        b = b * z + c
    return 0.5 + 0.5 * (x * a / b), jnp.exp2(u * u * (-0.5 * LOG2E)) * RSQRT_2PI


def pieces_in(info, at, refs, target, sem):
    copies = []
    for i, ref in enumerate(refs):
        for dst, src in target(ref, info[at + i]):
            copies.append(pltpu.make_async_copy(src, dst, sem))
    for c in copies:
        c.start()
    return copies


def blocks_out(info, at, source, place, keep, send, sem):
    n = source.shape[0] // PARTS
    copies = []
    for j in range(PARTS):
        dst = keep if j < PARTS // 2 else send
        row = pl.multiple_of(info[at + j] * n, n)
        copies.append(
            pltpu.make_async_copy(source.at[pl.ds(row, n)], dst.at[j % (PARTS // 2), pl.ds(place, n)], sem)
        )
    for c in copies:
        c.start()
    return copies


def weights_kernel(info, w_qkv, w_out, w0, piece):
    e = w_out.shape[0]
    for c in range(3):
        w0[c * e : (c + 1) * e, :] = w_qkv[c].T
    w0[3 * e :, :] = w_out[...]
    n = w0.shape[0] // PARTS
    piece[...] = w0[pl.ds(pl.multiple_of(info[24] * n, n), n), :]


def project_attend(clips, tl, heads, scale, r, info, n1, w, b, qkvT, oT, lse, kn, bias_sc, s_sc, p_sc):
    e = heads * HEAD_DIM
    slots = n1.shape[0]
    segc = segments(info, clips, (slots, 1), 0)
    segr = segments(info, clips, (1, slots), 1)
    for c in (1, 0, 2):
        t = (nt(w[c * e : (c + 1) * e, :], n1[...]) + b[c * e : (c + 1) * e, r : r + 1]).astype(BF)
        qkvT[c * e : (c + 1) * e, :] = t
        if c == 1:
            for h in range(heads):
                kn[h] = t[h * HEAD_DIM : (h + 1) * HEAD_DIM, :].T
    attend(tl, heads, scale, qkvT, kn, segc, segr, oT, lse, bias_sc, s_sc, p_sc)


def first_kernel(clips, tl, heads, scale, info, x, gain, shift, w, b, n1, qkvT, oT, lse, *scratch):
    rows = 128
    for i in range(0, x.shape[0], rows):
        n, _ = unit(x[i : i + rows, :].astype(F32))
        n1[i : i + rows, :] = (n * gain[...] + shift[...]).astype(BF)
    project_attend(clips, tl, heads, scale, 0, info, n1, w, b, qkvT, oT, lse, *scratch)


def attn_kernel(clips, tl, heads, scale, r, info, n1, b, *refs):
    pieces, (w, qkvT, oT, lse), scratch, sem = refs[:PARTS], refs[PARTS : PARTS + 4], refs[PARTS + 4 : -1], refs[-1]
    n = w.shape[0] // PARTS

    def target(ref, slot):
        return [(w.at[pl.ds(pl.multiple_of(slot * n, n), n)], ref)]

    for c in pieces_in(info, 8, pieces, target, sem):
        c.wait()
    project_attend(clips, tl, heads, scale, r, info, n1, w, b, qkvT, oT, lse, *scratch)


def mlp_chunk(info, n2, cot, wup, wdn, bup, out_acc, g_acc, keep, send, gb, hid, gp, up_sc, dn_sc, sem, fresh):
    H = wup.shape[1]
    n = n2.shape[1] // PARTS
    cuts = [slice(h, h + HIDDEN_BLOCK) for h in range(0, H, HIDDEN_BLOCK)]
    for s in cuts:
        u = nn(n2[...], wup[:, s]) + bup[:, s]
        ga = nt(cot[...], wdn[s, :])
        dist, dens = normal(u)
        hid[:, s] = (u * dist).astype(BF)
        g = (ga * (dist + u * dens)).astype(BF)
        gp[:, s] = g
        gb[:, s] = jnp.sum(g.astype(F32), axis=0, keepdims=True)
    dn_sc[...] = tn(cot[...], hid[...]).astype(BF)
    copies = blocks_out(info, 16, dn_sc, n, keep, send, sem)
    up_sc[...] = tn(n2[...], gp[...]).astype(BF)
    copies += blocks_out(info, 16, up_sc, 0, keep, send, sem)
    o, g = nn(hid[...], wdn[...]), nt(gp[...], wup[...])
    if fresh:
        out_acc[...] = o
        g_acc[...] = g
    else:
        out_acc[...] += o
        g_acc[...] += g
    return copies


def mid_kernel(info, x, bias_out, gain, shift, cot, o0, o1, o2, o3, w0, w1, w2, w3, wup, wdn, bup, *refs):
    mixed, n2, out_acc, g_acc, keep, send, gb, hid, gp, up_sc, dn_sc, sem = refs
    at = 3 * o0.shape[0]
    mixed[...] = x[...].astype(F32) + bias_out[...] + tn(o0[...], w0[at:, :])
    for o, w in ((o1, w1), (o2, w2), (o3, w3)):
        mixed[...] += tn(o[...], w[at:, :])
    rows = 128
    for i in range(0, x.shape[0], rows):
        n, _ = unit(mixed[i : i + rows, :])
        n2[i : i + rows, :] = (n * gain[...] + shift[...]).astype(BF)
    for c in mlp_chunk(info, n2, cot, wup, wdn, bup, out_acc, g_acc, keep, send, gb, hid, gp, up_sc, dn_sc, sem, True):
        c.wait()


def mlp_kernel(last, info, n2, cot, bup, out_in, g_in, *refs):
    if last:
        mixed, bias_down, gain = refs[:3]
        refs = refs[3:]
    pieces, refs = refs[:PARTS], refs[PARTS:]
    if last:
        result, grad_mixed, branch, vecs = refs[:4]
        refs = refs[4:]
        keep, send, gb, hid, gp, up_sc, dn_sc, wup, wdn, sem_in, sem = refs
        out_acc, g_acc = out_in, g_in
    else:
        out_acc, g_acc, keep, send, gb, hid, gp, up_sc, dn_sc, wup, wdn, sem_in, sem = refs
    n = wup.shape[0] // PARTS

    def target(ref, slot):
        row = pl.ds(pl.multiple_of(slot * n, n), n)
        return [(wup.at[row], ref.at[pl.ds(0, n)]), (wdn.at[row], ref.at[pl.ds(n, n)])]

    for c in pieces_in(info, 8, pieces, target, sem_in):
        c.wait()
    if not last:
        out_acc[...] = out_in[...]
        g_acc[...] = g_in[...]
    copies = mlp_chunk(info, n2, cot, wup, wdn, bup, out_acc, g_acc, keep, send, gb, hid, gp, up_sc, dn_sc, sem, False)
    if last:
        rows = 128
        sums = [0.0] * 4
        for i in range(0, n2.shape[0], rows):
            k = slice(i, i + rows)
            up, mid, c = g_acc[k, :], mixed[k, :], cot[k, :].astype(F32)
            result[k, :] = (mid + out_acc[k, :] + bias_down[...]).astype(BF)
            m, inverse = unit(mid)
            gm = c + unit_back(up, m, inverse, gain[...])
            grad_mixed[k, :] = gm
            branch[k, :] = gm.astype(BF)
            for j, v in enumerate((gm, up * m, up, c)):
                sums[j] = sums[j] + fold(v, jnp.sum)
        for j in range(4):
            vecs[j : j + 1, :] = jnp.sum(sums[j], axis=0, keepdims=True)
    for c in copies:
        c.wait()


def back_kernel(clips, tl, heads, scale, part, info, qkvT, w, gb, oT, n1, lse, dT, keep, send, small, *scratch):
    kn, vn, ga, bias_sc, p_sc, t_sc, pb_sc, ds_sc, dk, dv, acc, sem = scratch
    e, hd = heads * HEAD_DIM, HEAD_DIM
    slots = n1.shape[0]
    segc = segments(info, clips, (slots, 1), 0)
    segr = segments(info, clips, (1, slots), 1)
    ga[...] = nt(w[3 * e : 4 * e, :], gb[...]).astype(BF)
    for h in range(heads):
        kn[h] = qkvT[e + h * hd : e + (h + 1) * hd, :].T
        vn[h] = qkvT[2 * e + h * hd : 2 * e + (h + 1) * hd, :].T
    dk[...] = jnp.zeros_like(dk)
    dv[...] = jnp.zeros_like(dv)
    for q0, qn, k0, wide in tl:
        fill_mask(bias_sc, segc, segr, q0, qn, k0, wide)
        for h in range(heads):
            hs = slice(h * hd, (h + 1) * hd)
            q, go = qkvT[hs, q0 : q0 + qn], ga[hs, q0 : q0 + qn]
            total = lse[h : h + 1, q0 : q0 + qn]
            centre = None
            for b in range(0, wide, KEY_BLOCK):
                k, v = slice(b, b + KEY_BLOCK), slice(k0 + b, k0 + b + KEY_BLOCK)
                p = jnp.exp2(nn(kn[h, v, :], q) * scale + bias_sc[k, :qn] - total)
                t = p * nn(vn[h, v, :], go)
                p_sc[k, :qn] = p
                t_sc[k, :qn] = t
                pb_sc[k, :qn] = p.astype(BF)
                cb = fold(t, jnp.sum)
                centre = cb if centre is None else centre + cb
            centre = jnp.sum(centre, axis=0, keepdims=True)
            for b in range(0, wide, KEY_BLOCK):
                k = slice(b, b + KEY_BLOCK)
                ds_sc[k, :qn] = (t_sc[k, :qn] - p_sc[k, :qn] * centre).astype(BF)
            ds = ds_sc[:wide, :qn]
            dT[hs, q0 : q0 + qn] = (nn(qkvT[e + h * hd : e + (h + 1) * hd, k0 : k0 + wide], ds) * part).astype(BF)
            dk[hs, k0 : k0 + wide] += nt(q, ds)
            dv[hs, k0 : k0 + wide] += nt(go, pb_sc[:wide, :qn])
    dT[e : 2 * e, :] = (dk[...] * part).astype(BF)
    dT[2 * e : 3 * e, :] = dv[...].astype(BF)
    small[0:e, :] = jnp.sum(dT[0:e, :].astype(F32), axis=1, keepdims=True)
    small[e : 2 * e, :] = jnp.sum(dT[2 * e : 3 * e, :].astype(F32), axis=1, keepdims=True)
    acc[:, 0 : 3 * e] = tt(n1[...], dT[...]).astype(BF)
    acc[:, 3 * e : 4 * e] = tt(gb[...], oT[...]).astype(BF)
    for c in blocks_out(info, 16, acc, 0, keep, send, sem):
        c.wait()


def last_kernel(x, gain, grad_mixed, d0, d1, d2, d3, w0, w1, w2, w3, grad_tokens, vecs, g_sc):
    at = d0.shape[0]
    g_sc[...] = tn(d0[...], w0[:at, :])
    for dr, w in ((d1, w1), (d2, w2), (d3, w3)):
        g_sc[...] += tn(dr[...], w[:at, :])
    rows = 128
    sums = [0.0] * 2
    for i in range(0, x.shape[0], rows):
        k = slice(i, i + rows)
        up = g_sc[k, :]
        m, inverse = unit(x[k, :].astype(F32))
        grad_tokens[k, :] = grad_mixed[k, :] + unit_back(up, m, inverse, gain[...])
        for j, v in enumerate((up * m, up)):
            sums[j] = sums[j] + fold(v, jnp.sum)
    for j in range(2):
        vecs[j : j + 1, :] = jnp.sum(sums[j], axis=0, keepdims=True)


def on_device(
    places,
    planes,
    tokens,
    clip_lengths,
    gain_attn,
    shift_attn,
    w_qkv,
    bias_qv,
    w_out,
    bias_out,
    gain_mlp,
    shift_mlp,
    w_up,
    bias_up,
    w_down,
    bias_down,
    cotangent,
):
    T, D = tokens.shape
    clips = clip_lengths.shape[1]
    e = w_out.shape[0]
    heads = e // HEAD_DIM
    H = w_up.shape[1]
    n = D // PARTS
    rest = places // PARTS
    d, z = lax.axis_index("dp"), lax.axis_index("mp")
    hi = d // rest
    row = lambda v: v.astype(F32).reshape(1, -1)
    limit = lambda mb: pltpu.CompilerParams(vmem_limit_bytes=mb << 20)

    core = hi % 2
    first, second = jnp.where(core == 0, 2, 4), jnp.where(core == 0, 4, 2)
    both = lambda a, f, s: [a, a ^ f, a ^ s, a ^ 6]
    gathered = both(hi, first, second) + both(hi ^ 1, second, first)
    order = lambda a, f, s: [a, a ^ s, a ^ f, a ^ 6]
    exchanged = order(hi, first, second) + order(hi ^ 1, second, first)
    ends = jnp.cumsum(lax.dynamic_index_in_dim(clip_lengths, z, 0, keepdims=False))
    ends = jnp.concatenate([ends, jnp.zeros((8 - clips,), jnp.int32)])
    info = jnp.concatenate([ends, jnp.stack(gathered + exchanged + [hi]).astype(jnp.int32)])

    def over_plane(v, flip):
        return lax.ppermute(v, "dp", [(a, (((a // rest) ^ flip((a // rest) % 2)) * rest + a % rest)) for a in range(places)])

    to_core = lambda v: over_plane(v, lambda c: 1)
    to_first = lambda v: over_plane(v, lambda c: 4 if c else 2)
    to_second = lambda v: over_plane(v, lambda c: 2 if c else 4)

    def from_plane(v, r):
        return lax.ppermute(v, "mp", [(a, (a - r) % planes) for a in range(planes)])

    def to_plane(v, r):
        return lax.ppermute(v, "mp", [(a, (a + r) % planes) for a in range(planes)])

    far = [1, 3, 2]

    def spread(b):
        s1 = to_first(b)
        mine = [b, s1, to_second(b), to_second(s1)]
        return mine + [to_core(v) for v in mine]

    w0, piece = pl.pallas_call(
        weights_kernel,
        out_shape=(SDS((4 * e, D), BF), SDS((n, D), BF)),
        in_specs=[pl.BlockSpec(memory_space=SMEM), vm(), vm()],
        compiler_params=limit(16),
        cost_estimate=cost(2),
        name="weights",
    )(info, w_qkv, w_out)
    small_in = jnp.concatenate([bias_qv.reshape(-1), bias_up])
    got = {0: small_in}
    heads_from, units_from = {}, {}
    for r in far:
        heads_from[r] = from_plane(piece, r)
    for r in far:
        got[r] = from_plane(small_in, r)
    heads_in = {r: spread(heads_from[r]) for r in far}
    unit_piece = jnp.concatenate(
        [lax.dynamic_slice_in_dim(w_up, hi * n, n, 0), lax.dynamic_slice_in_dim(w_down, hi * n, n, 0)]
    )
    for r in far:
        units_from[r] = from_plane(unit_piece, r)
    units_in = {r: spread(units_from[r]) for r in far}
    biases = jnp.stack([got[r] for r in range(planes)]).astype(F32)
    cols = jnp.concatenate([biases[:, :e], jnp.zeros((planes, e), F32), biases[:, e : 2 * e]], axis=1).T
    bups = [biases[r : r + 1, 2 * e :] for r in range(planes)]

    tl = windows(T)
    wm, qm = max(t[3] for t in tl), max(t[1] for t in tl)
    scale = HEAD_DIM**-0.5 * LOG2E
    smem = pl.BlockSpec(memory_space=SMEM)
    anywhere = pl.BlockSpec(memory_space=ANY)
    attn_out = (SDS((3 * e, T), BF), SDS((e, T), BF), SDS((8, T), F32))
    attn_sc = [VMEM((heads, T, HEAD_DIM), BF), VMEM((wm, qm), F32), VMEM((wm, qm), F32), VMEM((wm, qm), BF)]
    n1, q0, o0, l0 = pl.pallas_call(
        partial(first_kernel, clips, tl, heads, scale),
        out_shape=(SDS((T, D), BF),) + attn_out,
        in_specs=[smem] + [vm()] * 5,
        scratch_shapes=attn_sc,
        compiler_params=limit(24),
        cost_estimate=cost(8),
        name="first",
    )(info, tokens, row(gain_attn), row(shift_attn), w0, cols)
    ws, qs, os, ls = {0: w0}, {0: q0}, {0: o0}, {0: l0}
    for r in far:
        ws[r], qs[r], os[r], ls[r] = pl.pallas_call(
            partial(attn_kernel, clips, tl, heads, scale, r),
            out_shape=(SDS((4 * e, D), BF),) + attn_out,
            in_specs=[smem, vm(), vm()] + [anywhere] * PARTS,
            scratch_shapes=attn_sc + [pltpu.SemaphoreType.DMA],
            compiler_params=limit(24),
            cost_estimate=cost(6),
            name=f"attn{r}",
        )(info, n1, cols, *heads_in[r])

    mlp_sc = [VMEM((T, H), BF)] * 2 + [VMEM((D, H), BF)] * 2
    grads_out = (SDS((PARTS // 2, 2 * n, H), BF),) * 2
    acc_out = (SDS((T, D), F32),) * 2
    keeps, sends, gbs = {}, {}, {}
    mixed, n2, out_acc, g_acc, keeps[0], sends[0], gbs[0] = pl.pallas_call(
        mid_kernel,
        out_shape=(SDS((T, D), F32), SDS((T, D), BF)) + acc_out + grads_out + (SDS((1, H), F32),),
        in_specs=[smem] + [vm()] * 16,
        out_specs=(vm(), vm(), vm(), vm(), anywhere, anywhere, vm()),
        scratch_shapes=mlp_sc + [pltpu.SemaphoreType.DMA],
        compiler_params=limit(40),
        cost_estimate=cost(14),
        name="mid",
    )(
        info,
        tokens,
        row(bias_out),
        row(gain_mlp),
        row(shift_mlp),
        cotangent,
        *(os[r] for r in range(planes)),
        *(ws[r] for r in range(planes)),
        w_up,
        w_down,
        bups[0],
    )
    for r in far:
        last = r == far[-1]
        extra = (mixed, row(bias_down), row(gain_mlp)) if last else ()
        extra_out = (SDS((T, D), BF), SDS((T, D), F32), SDS((T, D), BF), SDS((4, D), F32)) if last else acc_out
        res = pl.pallas_call(
            partial(mlp_kernel, last),
            out_shape=extra_out + grads_out + (SDS((1, H), F32),),
            in_specs=[smem] + [vm()] * (5 + len(extra)) + [anywhere] * PARTS,
            out_specs=(vm(),) * len(extra_out) + (anywhere, anywhere, vm()),
            scratch_shapes=mlp_sc
            + [VMEM((D, H), BF), VMEM((H, D), BF), pltpu.SemaphoreType.DMA, pltpu.SemaphoreType.DMA],
            compiler_params=limit(40),
            cost_estimate=cost(14 if last else 10),
            name=f"mlp{r}",
        )(info, n2, cotangent, bups[r], out_acc, g_acc, *extra, *units_in[r])
        if last:
            result, grad_mixed, branch, vec_mlp = res[:4]
        else:
            out_acc, g_acc = res[:2]
        keeps[r], sends[r], gbs[r] = res[len(extra_out) :]

    f32 = lambda v: v.astype(F32)

    def reduce_plane(keep, send):
        k = f32(keep) + f32(to_core(send))
        k = k[:2] + f32(to_first(k[2:].astype(BF)))
        k = k[0] + f32(to_second(k[1].astype(BF)))
        if rest > 1:
            groups = [[a * rest + b for b in range(rest)] for a in range(PARTS)]
            k = k.reshape(-1, n, k.shape[-1])
            k = lax.psum_scatter(k, "dp", scatter_dimension=1, axis_index_groups=groups, tiled=True)
            k = k.reshape(-1, k.shape[-1])
        return k

    def reduce_planes(parts):
        total = parts[0]
        for r in range(1, planes):
            total = total + f32(to_plane(parts[r].astype(BF), r))
        return total

    unit_grads = {r: reduce_plane(keeps[r], sends[r]) for r in [0] + far}

    V = VMEM
    back_sc = (
        [V((heads, T, HEAD_DIM), BF)] * 2
        + [V((e, T), BF)]
        + [V((wm, qm), F32)] * 3
        + [V((wm, qm), BF)] * 2
        + [V((e, T), F32)] * 2
        + [V((D, 4 * e), BF), pltpu.SemaphoreType.DMA]
    )
    ds, head_grads, smalls = {}, {}, {}
    for r in far + [0]:
        ds[r], keep, send, smalls[r] = pl.pallas_call(
            partial(back_kernel, clips, tl, heads, scale, HEAD_DIM**-0.5),
            out_shape=(SDS((3 * e, T), BF),) + (SDS((PARTS // 2, n, 4 * e), BF),) * 2 + (SDS((2 * e, 1), F32),),
            in_specs=[smem] + [vm()] * 6,
            out_specs=(vm(), anywhere, anywhere, vm()),
            scratch_shapes=back_sc,
            compiler_params=limit(32),
            cost_estimate=cost(11),
            name=f"back{r}",
        )(info, qs[r], ws[r], branch, os[r], n1, ls[r])
        head_grads[r] = reduce_plane(keep, send)

    grad_tokens, vec_attn = pl.pallas_call(
        last_kernel,
        out_shape=(SDS((T, D), F32), SDS((2, D), F32)),
        in_specs=[vm()] * 11,
        out_specs=(vm(), vm()),
        scratch_shapes=[VMEM((T, D), F32)],
        compiler_params=limit(32),
        cost_estimate=cost(7),
        name="last",
    )(
        tokens,
        row(gain_attn),
        grad_mixed,
        *(ds[r] for r in range(planes)),
        *(ws[r] for r in range(planes)),
    )

    vecs = jnp.concatenate([vec_mlp, vec_attn]).reshape(1, -1)
    per = jnp.concatenate(
        [jnp.concatenate([gbs[r], smalls[r].reshape(1, -1)], axis=1) for r in range(planes)], axis=1
    )
    small = jnp.concatenate([per, vecs], axis=1)
    step = 1
    while step < places:
        small = small + lax.ppermute(small, "dp", [(a, a ^ step) for a in range(places)])
        step *= 2
    width = H + 2 * e
    vecs = small[:, planes * width :]
    per = [small[:, r * width : (r + 1) * width] for r in range(planes)]
    own = jnp.concatenate([per[0], vecs], axis=1)
    total = own
    for r in range(1, planes):
        total = total + to_plane(jnp.concatenate([per[r], vecs], axis=1), r)
    total = total[0]
    cut = lambda v, at, size: lax.dynamic_slice_in_dim(v, at, size, v.ndim - 1)
    grad_bias_up = cut(total[:H], d * (H // places), H // places)
    grad_bias_qv = cut(total[H:width].reshape(2, e), d * (e // places), e // places)
    piece_of = D // (places * planes)
    g_bo, g_gm, g_sm, g_bd, g_ga, g_sa = cut(total[width:].reshape(6, D), (d * planes + z) * piece_of, piece_of)

    units = reduce_planes(unit_grads)
    m = D // places
    grad_w_up, grad_w_down = units[:m], units[m:].T
    hd = reduce_planes(head_grads)
    grad_w_qkv = hd[:, : 3 * e].reshape(m, 3, e).transpose(1, 0, 2)
    grad_w_out = hd[:, 3 * e :].T
    return (
        result,
        grad_tokens,
        g_ga,
        g_sa,
        grad_w_qkv,
        grad_bias_qv,
        grad_w_out,
        g_bo,
        g_gm,
        g_sm,
        grad_w_up,
        grad_bias_up,
        grad_w_down,
        g_bd,
    )


def solution(mesh):
    return jax.shard_map(
        partial(on_device, mesh.shape["dp"], mesh.shape["mp"]),
        mesh=mesh,
        in_specs=(
            P(("dp", "mp"), None),
            P("dp", None),
            P(),
            P(),
            P(None, None, "mp"),
            P(None, "mp"),
            P("mp", None),
            P(),
            P(),
            P(),
            P(None, "mp"),
            P("mp"),
            P("mp", None),
            P(),
            P(("dp", "mp"), None),
        ),
        out_specs=(
            P(("dp", "mp"), None),
            P(("dp", "mp"), None),
            P(("dp", "mp")),
            P(("dp", "mp")),
            P(None, "dp", "mp"),
            P(None, ("mp", "dp")),
            P("mp", "dp"),
            P(("dp", "mp")),
            P(("dp", "mp")),
            P(("dp", "mp")),
            P("dp", "mp"),
            P(("mp", "dp")),
            P("mp", "dp"),
            P(("dp", "mp")),
        ),
        check_vma=False,
    )
```

```python
from functools import partial

import jax
import jax.numpy as jnp
import numpy as np
from jax import lax
from jax.experimental import pallas as pl
from jax.experimental.pallas import tpu as pltpu
from jax.sharding import PartitionSpec as P

F32, BF = jnp.float32, jnp.bfloat16
HEAD_DIM = 64
MOST = 256
EPSILON = 1e-06
MASKED = -1e30
LOG2E = 1.4426950408889634
ROOT_HALF = 0.7071067811865476
RSQRT_2PI = 0.3989422804014327
PARTS = 8
KEY_BLOCK = 128
TAIL = 16
GATHERED, EXCHANGED, PLACE = 8, 16, 24
VMEM, SMEM, HBM = pltpu.VMEM, pltpu.SMEM, pltpu.HBM
LANES = 128
SDS = jax.ShapeDtypeStruct


def _dot(a, b, i, j):
    return lax.dot_general(a, b, (((i,), (j,)), ((), ())), preferred_element_type=F32)


def nn(a, b):
    return _dot(a, b, 1, 0)


def nt(a, b):
    return _dot(a, b, 1, 1)


def tn(a, b):
    return _dot(a, b, 0, 0)


def tt(a, b):
    return _dot(a, b, 0, 1)


def call(body, name, us, megabytes, ins, outs, scratch, after=()):
    count, skip = len(ins), len(ins) + len(after)

    def kernel(*refs):
        body(*refs[:count], *refs[skip:])

    return pl.pallas_call(
        kernel,
        out_shape=tuple(o[0] for o in outs),
        in_specs=[pl.BlockSpec(memory_space=m) for _, m in ins] + [pl.BlockSpec(memory_space=HBM)] * len(after),
        out_specs=tuple(pl.BlockSpec(memory_space=m) for _, m in outs),
        scratch_shapes=scratch,
        compiler_params=pltpu.CompilerParams(vmem_limit_bytes=megabytes << 20),
        cost_estimate=pl.CostEstimate(flops=int(us * 1.0e9), bytes_accessed=1 << 20, transcendentals=0),
        name=name,
    )(*(a for a, _ in ins), *after)


class Mover:
    def __init__(self, sems):
        self.sems, self.used = sems, 0

    def __call__(self, src, dst):
        c = pltpu.make_async_copy(src, dst, self.sems.at[self.used])
        self.used += 1
        c.start()
        return c


def wait(*copies):
    for c in copies:
        c.wait()


def windows(slots, width=256):
    out = []
    for q0 in range(0, slots, width):
        qn = min(width, slots - q0)
        lo = max(0, (q0 - MOST + 1) // 128 * 128)
        hi = min(slots, -(-(q0 + qn + MOST - 1) // 128) * 128)
        out.append((q0, qn, lo, hi - lo))
    return out


def segments(info, clips, shape, axis):
    place = lax.broadcasted_iota(jnp.int32, shape, axis)
    seg = jnp.zeros(shape, jnp.int32)
    for c in range(clips):
        seg = seg + jnp.where(place >= info[c], 1, 0)
    return jnp.where(seg == clips - 1, place + clips, seg)


def fill_mask(bias_sc, segc, segr, q0, qn, k0, w):
    for b in range(0, w, KEY_BLOCK):
        same = segc[k0 + b : k0 + b + KEY_BLOCK, :] == segr[:, q0 : q0 + qn]
        bias_sc[b : b + KEY_BLOCK, :qn] = jnp.where(same, 0.0, MASKED)


def fold(x, f):
    return f(x.reshape(x.shape[0] // 8, 8, x.shape[1]), axis=0)


def attend(tl, heads, scale, qkvT, kn, segc, segr, oT, lse, bias_sc, s_sc, p_sc):
    e, hd = heads * HEAD_DIM, HEAD_DIM
    for q0, qn, k0, w in tl:
        fill_mask(bias_sc, segc, segr, q0, qn, k0, w)
        for h in range(heads):
            q = qkvT[h * hd : (h + 1) * hd, q0 : q0 + qn]
            m = None
            for b in range(0, w, KEY_BLOCK):
                s = nn(kn[h, k0 + b : k0 + b + KEY_BLOCK, :], q) * scale + bias_sc[b : b + KEY_BLOCK, :qn]
                s_sc[b : b + KEY_BLOCK, :qn] = s
                mb = fold(s, jnp.max)
                m = mb if m is None else jnp.maximum(m, mb)
            m = jnp.max(m, axis=0, keepdims=True)
            total = None
            for b in range(0, w, KEY_BLOCK):
                p = jnp.exp2(s_sc[b : b + KEY_BLOCK, :qn] - m)
                p_sc[b : b + KEY_BLOCK, :qn] = p.astype(BF)
                lb = fold(p, jnp.sum)
                total = lb if total is None else total + lb
            total = jnp.sum(total, axis=0, keepdims=True)
            o = nn(qkvT[2 * e + h * hd : 2 * e + (h + 1) * hd, k0 : k0 + w], p_sc[:w, :qn])
            oT[h * hd : (h + 1) * hd, q0 : q0 + qn] = (o * (1.0 / total)).astype(BF)
            lse[h : h + 1, q0 : q0 + qn] = m + jnp.log2(total)


def unit(x):
    y = x - jnp.mean(x, axis=1, keepdims=True)
    inverse = lax.rsqrt(jnp.mean(y * y, axis=1, keepdims=True) + EPSILON)
    return y * inverse, inverse


def unit_back(up, n, inverse, gain):
    g = up * gain
    return inverse * (g - jnp.mean(g, axis=1, keepdims=True) - n * jnp.mean(g * n, axis=1, keepdims=True))


def normal(u):
    x = jnp.clip(u * ROOT_HALF, -3.832506856900711, 3.832506856900711)
    z = x * x
    a = 0.00022905065861350646
    for c in (0.0034082910107109506, 0.050955695062380861, 0.18520832239976145, 1.128379143519084):
        a = a * z + c
    b = -1.1791602954361697e-7
    for c in (
        0.000023547966471313185,
        0.0010179625278914885,
        0.014070470171167667,
        0.11098505178285362,
        0.49746925110067538,
        1.0,
    ):
        b = b * z + c
    return 0.5 + 0.5 * (x * a / b), jnp.exp2(u * u * (-0.5 * LOG2E)) * RSQRT_2PI


def gather_rows(move, info, at, blocks, target, n):
    return [
        move(ref.at[pl.ds(row, n)], target.at[pl.ds(pl.multiple_of(info[at + i] * n, n), n)])
        for i, (ref, row) in enumerate(blocks)
    ]


def blocks_out(move, info, source, place, keep, send):
    n, half = source.shape[0] // PARTS, PARTS // 2
    return [
        move(
            source.at[pl.ds(pl.multiple_of(info[EXCHANGED + j] * n, n), n)],
            (keep if j < half else send).at[j % half, pl.ds(place, n)],
        )
        for j in range(PARTS)
    ]


def cut_kernel(info, w_heads, w_out, w_up, w_down, bias_qv, bias_up, w0, piece, units, tail_s, sems):
    e, H = w_out.shape[0], bias_up.shape[1]
    n = units.shape[0] // 2
    move = Mover(sems)
    row = pl.ds(pl.multiple_of(info[PLACE] * n, n), n)
    tail = piece.at[pl.ds(n, TAIL)]
    tail_s[...] = jnp.zeros_like(tail_s)
    tail_s[0:1, :H] = bias_up[...].astype(F32)
    for i in range(2):
        tail_s[1:2, 256 * i : 256 * i + e] = bias_qv[i : i + 1, :].astype(F32)
    tail[...] = tail_s[...].astype(BF)
    done = [move(w_up.at[row], units.at[pl.ds(0, n)]), move(w_down.at[row], units.at[pl.ds(n, n)])]
    done += [move(w_heads, w0.at[pl.ds(0, 3 * e)]), move(w_out, w0.at[pl.ds(3 * e, e)])]
    wait(*done)
    piece[pl.ds(0, n), :] = w0[row, :]


def project_attend(clips, tl, heads, scale, info, n1, w, piece, qkvT, oT, lse, kn, bias_sc, s_sc, p_sc):
    e = heads * HEAD_DIM
    slots = n1.shape[0]
    n = piece.shape[0] - TAIL
    segc = segments(info, clips, (slots, 1), 0)
    segr = segments(info, clips, (1, slots), 1)
    biases = piece[n : n + TAIL, :512].astype(F32)[1:2, :]
    for c in (1, 0, 2):
        t = nt(w[c * e : (c + 1) * e, :], n1[...])
        if c != 1:
            at = 128 * c
            t = t + jnp.broadcast_to(biases[:, at : at + 256], (LANES, 256)).T[:e, :1]
        t = t.astype(BF)
        qkvT[c * e : (c + 1) * e, :] = t
        if c == 1:
            for h in range(heads):
                kn[h] = t[h * HEAD_DIM : (h + 1) * HEAD_DIM, :].T
    attend(tl, heads, scale, qkvT, kn, segc, segr, oT, lse, bias_sc, s_sc, p_sc)


def first_kernel(clips, tl, heads, scale, info, x, gain, shift, w, piece, n1, qkvT, oT, lse, *scratch):
    for i in range(0, x.shape[0], LANES):
        n, _ = unit(x[i : i + LANES, :].astype(F32))
        n1[i : i + LANES, :] = (n * gain[...].astype(F32) + shift[...].astype(F32)).astype(BF)
    project_attend(clips, tl, heads, scale, info, n1, w, piece, qkvT, oT, lse, *scratch)


def attn_kernel(clips, tl, heads, scale, info, n1, piece, p4, r4, w, qkvT, oT, lse, *scratch):
    n = w.shape[0] // PARTS
    for i in range(PARTS):
        ref = (p4, r4)[i // 4]
        w[pl.ds(pl.multiple_of(info[GATHERED + i] * n, n), n), :] = ref[i % 4 * n : (i % 4 + 1) * n, :]
    project_attend(clips, tl, heads, scale, info, n1, w, piece, qkvT, oT, lse, *scratch)


def chunk_front(n2, cot, wup, wdn, piece, hid, gp, gb):
    n = piece.shape[0] - TAIL
    u = nn(n2[...], wup[...]) + piece[n : n + TAIL, :].astype(F32)[0:1, : wup.shape[1]]
    ga = nt(cot[...], wdn[...])
    dist, dens = normal(u)
    hid[...] = (u * dist).astype(BF)
    g = (ga * (dist + u * dens)).astype(BF)
    gp[...] = g
    gb[...] = jnp.sum(g.astype(F32), axis=0, keepdims=True)


def chunk_sums(hid, gp, wup, wdn, out_acc, g_acc, fresh):
    o = nn(hid[...], wdn[...])
    out_acc[...] = o if fresh else out_acc[...] + o
    g = nt(gp[...], wup[...])
    g_acc[...] = g if fresh else g_acc[...] + g


def chunk_grads(move, info, n2, cot, hid, gp, up_sc, dn_sc, k, keep, send):
    n = n2.shape[1] // PARTS
    dn_sc[...] = tn(cot[...], hid[...]).astype(BF)
    copies = blocks_out(move, info, dn_sc, (2 * k + 1) * n, keep, send)
    up_sc[...] = tn(n2[...], gp[...]).astype(BF)
    return copies + blocks_out(move, info, up_sc, 2 * k * n, keep, send)


def mid_kernel(x, bias_out, gain, shift, *refs):
    count = (len(refs) - 6) // 2
    o, w, refs = refs[:count], refs[count : 2 * count], refs[2 * count :]
    mixed, n2, o_s, wo_s, mixed_s, sems = refs
    e = o[0].shape[0]
    move = Mover(sems)
    for r in range(count):
        o_s[r * e : (r + 1) * e, :] = o[r][...]
        wo_s[r * e : (r + 1) * e, :] = w[r][3 * e : 4 * e, :]
    mixed_s[...] = tn(o_s[...], wo_s[...])
    done = []
    for i in range(0, x.shape[0], LANES):
        k = slice(i, i + LANES)
        m = mixed_s[k, :] + x[k, :].astype(F32) + bias_out[...].astype(F32)
        mixed_s[k, :] = m
        done.append(move(mixed_s.at[pl.ds(i, LANES)], mixed.at[pl.ds(i, LANES)]))
        n, _ = unit(m)
        n2[k, :] = (n * gain[...].astype(F32) + shift[...].astype(F32)).astype(BF)
    wait(*done)


def own_kernel(info, n2, cot, piece, wup, wdn, *refs):
    out, g, keep, send, gb = refs[:5]
    cot_s, wup_s, wdn_s, out_s, g_s, hid, gp, up_sc, dn_sc, sems = refs[5:]
    move = Mover(sems)
    loads = [move(wup, wup_s), move(cot, cot_s), move(wdn, wdn_s)]
    wait(*loads)
    chunk_front(n2, cot_s, wup_s, wdn_s, piece, hid, gp, gb)
    chunk_sums(hid, gp, wup_s, wdn_s, out_s, g_s, True)
    done = [move(out_s, out), move(g_s, g)]
    wait(*chunk_grads(move, info, n2, cot_s, hid, gp, up_sc, dn_sc, 0, keep, send), *done)


def mlp_kernel(count, info, n2, cot, out_in, g_in, p4, r4, *refs):
    small, refs = refs[:count], refs[count:]
    out, g, keep, send, gb = refs[:5]
    n2_s, cot_s, out_s, g_s, hid, gp, up_sc, dn_sc, sems = refs[5:14]
    wup_s, wdn_s = refs[14 : 14 + count], refs[14 + count :]
    move = Mover(sems)
    n = n2_s.shape[1] // PARTS
    front = [move(n2, n2_s), move(cot, cot_s)]
    ready = [units_here(move, info, p4, r4, wup_s[k], wdn_s[k], n, k, count) for k in range(count)]
    sums = [move(out_in, out_s), move(g_in, g_s)]
    wait(*front)
    done = []
    for k in range(count):
        wait(*ready[k])
        chunk_front(n2_s, cot_s, wup_s[k], wdn_s[k], small[k], hid, gp, gb.at[pl.ds(k, 1)])
        if k == 0:
            wait(*sums)
        chunk_sums(hid, gp, wup_s[k], wdn_s[k], out_s, g_s, False)
        wait(*done)
        done = []
        if k == count - 1:
            done = [move(out_s, out), move(g_s, g)]
        done += chunk_grads(move, info, n2_s, cot_s, hid, gp, up_sc, dn_sc, k, keep, send)
    wait(*done)


def units_here(move, info, p4, r4, wup, wdn, n, k, count):
    blocks = [(ref, (i * count + k) * 2 * n) for ref in (p4, r4) for i in range(PARTS // 2)]
    return gather_rows(move, info, GATHERED, blocks, wup, n) + gather_rows(
        move, info, GATHERED, [(ref, row + n) for ref, row in blocks], wdn, n
    )


def mlp_last_kernel(info, n2, cot, out_in, g_in, p4, r4, small, mixed, bias_down, gain, *refs):
    gbs, refs = refs[: len(refs) - 19], refs[len(refs) - 19 :]
    result, grad_mixed, branch, keep, send, sm = refs[:6]
    n2_s, cot_s, out_s, g_s, hid, gp, up_sc, dn_sc, wup_s, wdn_s, mixed_s, result_s, sems = refs[6:]
    move = Mover(sems)
    n = n2_s.shape[1] // PARTS
    front = [move(n2, n2_s), move(cot, cot_s)] + units_here(move, info, p4, r4, wup_s, wdn_s, n, 0, 1)
    sums = [move(out_in, out_s), move(g_in, g_s), move(mixed, mixed_s)]
    wait(*front)
    chunk_front(n2_s, cot_s, wup_s, wdn_s, small, hid, gp, sm.at[pl.ds(7, 1)])
    wait(*sums)
    chunk_sums(hid, gp, wup_s, wdn_s, out_s, g_s, False)
    vecs = [0.0] * 4
    for i in range(0, n2.shape[0], LANES):
        k = slice(i, i + LANES)
        up, mid, c = g_s[k, :], mixed_s[k, :], cot_s[k, :].astype(F32)
        result_s[k, :] = (mid + out_s[k, :] + bias_down[...].astype(F32)).astype(BF)
        m, inverse = unit(mid)
        gm = c + unit_back(up, m, inverse, gain[...].astype(F32))
        mixed_s[k, :] = gm
        branch[k, :] = gm.astype(BF)
        for j, v in enumerate((gm, up * m, up, c)):
            vecs[j] = vecs[j] + fold(v, jnp.sum)
    done = [move(mixed_s, grad_mixed), move(result_s, result)]
    for j in range(4):
        sm[j : j + 1, :] = jnp.sum(vecs[j], axis=0, keepdims=True)
    at = 4
    for ref in gbs:
        sm[at : at + ref.shape[0], :] = ref[...]
        at += ref.shape[0]
    done += chunk_grads(move, info, n2_s, cot_s, hid, gp, up_sc, dn_sc, 0, keep, send)
    wait(*done)


def riders(move, sm, low, keep, send, place):
    low[...] = sm[...].astype(BF)
    return [move(low, ref.at[j, pl.ds(place, TAIL)]) for ref in (keep, send) for j in range(PARTS // 2)]


def back_heads(clips, tl, heads, scale, part, info, gb, w, q_s, lse, d_s, scratch):
    kn, vn, ga, bias_sc, p_sc, t_sc, pb_sc, ds_sc, dk, dv = scratch
    e, hd = heads * HEAD_DIM, HEAD_DIM
    slots = gb.shape[0]
    segc = segments(info, clips, (slots, 1), 0)
    segr = segments(info, clips, (1, slots), 1)
    ga[...] = nt(w[3 * e : 4 * e, :], gb[...]).astype(BF)
    for h in range(heads):
        kn[h] = q_s[e + h * hd : e + (h + 1) * hd, :].T
        vn[h] = q_s[2 * e + h * hd : 2 * e + (h + 1) * hd, :].T
    dk[...] = jnp.zeros_like(dk)
    dv[...] = jnp.zeros_like(dv)
    for q0, qn, k0, wide in tl:
        fill_mask(bias_sc, segc, segr, q0, qn, k0, wide)
        for h in range(heads):
            hs = slice(h * hd, (h + 1) * hd)
            q, go = q_s[hs, q0 : q0 + qn], ga[hs, q0 : q0 + qn]
            total = lse[h : h + 1, q0 : q0 + qn]
            centre = None
            for b in range(0, wide, KEY_BLOCK):
                k, v = slice(b, b + KEY_BLOCK), slice(k0 + b, k0 + b + KEY_BLOCK)
                p = jnp.exp2(nn(kn[h, v, :], q) * scale + bias_sc[k, :qn] - total)
                t = p * nn(vn[h, v, :], go)
                p_sc[k, :qn] = p
                t_sc[k, :qn] = t
                pb_sc[k, :qn] = p.astype(BF)
                cb = fold(t, jnp.sum)
                centre = cb if centre is None else centre + cb
            centre = jnp.sum(centre, axis=0, keepdims=True)
            for b in range(0, wide, KEY_BLOCK):
                k = slice(b, b + KEY_BLOCK)
                ds_sc[k, :qn] = (t_sc[k, :qn] - p_sc[k, :qn] * centre).astype(BF)
            ds = ds_sc[:wide, :qn]
            d_s[hs, q0 : q0 + qn] = (nn(q_s[e + h * hd : e + (h + 1) * hd, k0 : k0 + wide], ds) * part).astype(BF)
            dk[hs, k0 : k0 + wide] += nt(q, ds)
            dv[hs, k0 : k0 + wide] += nt(go, pb_sc[:wide, :qn])
    d_s[e : 2 * e, :] = (dk[...] * part).astype(BF)
    d_s[2 * e : 3 * e, :] = dv[...].astype(BF)


def bias_rows(d_s, small, at, e):
    rows = nt(jnp.ones((8, d_s.shape[1]), BF), d_s[...])
    small[at : at + 1, 0:e] = rows[0:1, 0:e]
    small[at : at + 1, 256 : 256 + e] = rows[0:1, 2 * e : 3 * e]


def head_grads(move, info, gb, n1, oT, d_s, acc, keep, send):
    k = d_s.shape[0]
    acc[:, :k] = tt(n1[...], d_s[...]).astype(BF)
    acc[:, k:] = tt(gb[...], oT[...]).astype(BF)
    return blocks_out(move, info, acc, 0, keep, send)


def back_kernel(clips, tl, heads, scale, part, info, gb, n1, q, w, oT, lse, d, keep, send, small, acc, sems, *scratch):
    small[...] = jnp.zeros_like(small)
    back_heads(clips, tl, heads, scale, part, info, gb, w, q, lse, d, scratch)
    bias_rows(d, small, 0, heads * HEAD_DIM)
    wait(*head_grads(Mover(sems), info, gb, n1, oT, d, acc, keep, send))


def last_kernel(clips, tl, heads, scale, part, planes, info, gb_h, n1_h, q_h, w_h, oT_h, lse, x, gain, grad_mixed, sm1, *refs):
    count = planes - 1
    smalls, d, ws, refs = refs[:count], refs[count : 2 * count], refs[2 * count : 3 * count], refs[3 * count :]
    grad_tokens, keep, send, gb, n1, q, w, oT, acc, d0, x_s, gm_s, d_s, w_s, g_sc, sm, sm_low, sems = refs[:18]
    e = heads * HEAD_DIM
    rows = 3 * e
    move = Mover(sems)
    soon = [move(w_h, w), move(gb_h, gb), move(q_h, q)]
    grad_loads = [move(n1_h, n1), move(oT_h, oT)]
    loads = [[move(d[i], d_s.at[i]), move(ws[i].at[pl.ds(0, rows)], w_s.at[i])] for i in range(count)]
    later = [move(x, x_s), move(grad_mixed, gm_s)]
    sm[...] = jnp.zeros_like(sm)
    sm[6:14, :] = sm1[...]
    wait(*soon)
    back_heads(clips, tl, heads, scale, part, info, gb, w, q, lse, d0, refs[18:])
    bias_rows(d0, sm, 2, e)
    wait(*grad_loads)
    done = head_grads(move, info, gb, n1, oT, d0, acc, keep, send)
    g_sc[...] = tn(d0[...], w[:rows, :])
    for i in range(count):
        wait(*loads[i])
        g_sc[...] += tn(d_s[i], w_s[i])
        sm[3 + i : 4 + i, :512] = smalls[i][0:1, :]
    wait(*later)
    vecs = [0.0] * 2
    for i in range(0, x.shape[0], LANES):
        k = slice(i, i + LANES)
        up = g_sc[k, :]
        m, inverse = unit(x_s[k, :].astype(F32))
        gm_s[k, :] = gm_s[k, :] + unit_back(up, m, inverse, gain[...].astype(F32))
        done.append(move(gm_s.at[pl.ds(i, LANES)], grad_tokens.at[pl.ds(i, LANES)]))
        for j, v in enumerate((up * m, up)):
            vecs[j] = vecs[j] + fold(v, jnp.sum)
    for j in range(2):
        sm[j : j + 1, :] = jnp.sum(vecs[j], axis=0, keepdims=True)
    wait(*riders(move, sm, sm_low, keep, send, keep.shape[1] - TAIL), *done)


def on_device(
    places,
    planes,
    tokens,
    clip_lengths,
    gain_attn,
    shift_attn,
    w_qkv,
    bias_qv,
    w_out,
    bias_out,
    gain_mlp,
    shift_mlp,
    w_up,
    bias_up,
    w_down,
    bias_down,
    cotangent,
):
    T, D = tokens.shape
    clips = clip_lengths.shape[1]
    e = w_out.shape[0]
    heads = e // HEAD_DIM
    H = w_up.shape[1]
    n = D // PARTS
    rest = places // PARTS
    d, z = lax.axis_index("dp"), lax.axis_index("mp")
    hi = d // rest
    f32 = lambda v: v.astype(F32)
    row = lambda v: v.reshape(1, -1)

    core = hi % 2
    first, second = jnp.where(core == 0, 2, 4), jnp.where(core == 0, 4, 2)
    both = lambda a, f, s: [a, a ^ f, a ^ s, a ^ 6]
    order = lambda a, f, s: [a, a ^ s, a ^ f, a ^ 6]
    gathered = both(hi, first, second) + both(hi ^ 1, second, first)
    exchanged = order(hi, first, second) + order(hi ^ 1, second, first)
    ends = jnp.cumsum(lax.dynamic_index_in_dim(clip_lengths, z, 0, keepdims=False))
    ends = jnp.concatenate([ends, jnp.zeros((GATHERED - clips,), jnp.int32)])
    info = jnp.concatenate([ends, jnp.stack(gathered + exchanged + [hi]).astype(jnp.int32)])

    def over_plane(v, flip):
        to = lambda a: ((a // rest) ^ flip((a // rest) % 2)) * rest + a % rest
        return lax.ppermute(v, "dp", [(a, to(a)) for a in range(places)])

    to_core = lambda v: over_plane(v, lambda c: 1)
    to_first = lambda v: over_plane(v, lambda c: 4 if c else 2)
    to_second = lambda v: over_plane(v, lambda c: 2 if c else 4)
    shift = lambda v, r: lax.ppermute(v, "mp", [(a, (a + r) % planes) for a in range(planes)])
    from_plane = lambda v, r: shift(v, -r)
    to_plane = shift

    def now(*arrays):
        return lax.optimization_barrier(arrays)

    near, last_far = [1, 3], 2
    far = near + [last_far]

    sems = lambda k: pltpu.SemaphoreType.DMA((k,))
    w_heads = w_qkv.transpose(0, 2, 1).reshape(3 * e, D)
    w0, piece, unit_piece = call(
        cut_kernel,
        "cut",
        3,
        60,
        [(info, SMEM), (w_heads, HBM), (w_out, HBM), (w_up, HBM), (w_down, HBM), (bias_qv, VMEM), (row(bias_up), VMEM)],
        [(SDS((4 * e, D), BF), VMEM), (SDS((n + TAIL, D), BF), VMEM), (SDS((2 * n, D), BF), VMEM)],
        [VMEM((TAIL, D), F32), sems(4)],
    )
    pieces = {0: piece, **{r: from_plane(piece, r) for r in far}}

    tl = windows(T)
    wm, qm = max(t[3] for t in tl), max(t[1] for t in tl)
    scale = HEAD_DIM**-0.5 * LOG2E
    attn_out = [(SDS((3 * e, T), BF), VMEM), (SDS((e, T), BF), VMEM), (SDS((8, T), F32), VMEM)]
    attn_sc = [VMEM((heads, T, HEAD_DIM), BF), VMEM((wm, qm), F32), VMEM((wm, qm), F32), VMEM((wm, qm), BF)]
    n1, q0, o0, l0 = call(
        partial(first_kernel, clips, tl, heads, scale),
        "first",
        7,
        24,
        [(info, SMEM), (tokens, VMEM), (row(gain_attn), VMEM), (row(shift_attn), VMEM), (w0, VMEM), (piece, VMEM)],
        [(SDS((T, D), BF), VMEM)] + attn_out,
        attn_sc,
    )
    ws, qs, os, ls = {0: w0}, {0: q0}, {0: o0}, {0: l0}

    def spread(b, rows):
        f = to_first(b)
        c2 = jnp.concatenate([b[:rows], f[:rows]])
        c4 = jnp.concatenate([c2, to_second(c2)])
        return c4, to_core(c4)

    def join(*v):
        return jnp.concatenate(v)

    def attn(r, c4, r4, after):
        ws[r], qs[r], os[r], ls[r] = call(
            partial(attn_kernel, clips, tl, heads, scale),
            f"attn{r}",
            7,
            24,
            [(info, SMEM), (n1, VMEM), (pieces[r], VMEM), (c4, VMEM), (r4, VMEM)],
            [(SDS((4 * e, D), BF), VMEM)] + attn_out,
            attn_sc,
            after=after,
        )
        return ls[r]

    a1, a3, a2 = far
    _, p1, p3 = now(l0, pieces[a1], pieces[a3])
    p1, p3, f1, f3, p2 = now(p1, p3, to_first(p1), to_first(p3), pieces[a2])
    c1, c3 = join(p1[:n], f1[:n]), join(p3[:n], f3[:n])
    s1, s3, f2 = to_second(c1), to_second(c3), to_first(p2)
    c1 = join(c1, s1)
    core1, near_piece = to_core(c1), now(unit_piece, c1)[0]
    near_z = [from_plane(near_piece, r) for r in near]
    t = attn(a1, c1, core1, [])
    _, s3, f2, *near_z = now(t, s3, f2, *near_z)
    c3, c2, near_b = join(c3, s3), join(p2[:n], f2[:n]), join(*near_z)
    core3, s2, near_f = to_core(c3), to_second(c2), to_first(near_b)
    far_b = from_plane(now(unit_piece, near_b)[0], last_far)
    t = attn(a3, c3, core3, [c2, near_b])
    _, s2, near_f = now(t, s2, near_f)
    c2, near_b = join(c2, s2), join(near_b, near_f)
    core2, near_s = to_core(c2), to_second(near_b)
    t = attn(a2, c2, core2, [near_b])
    _, far_b = now(t, far_b)
    far_f = to_first(far_b)

    def block(i, keep, core, first):
        return f32(keep[i]) + f32(core[i]) + f32(first[i])

    def hop_first(keep, core):
        half = PARTS // 4
        return to_first((f32(keep[half:]) + f32(core[half:])).astype(BF))

    def hop_second(*had):
        return to_second(block(1, *had).astype(BF))

    def total(keep, core, first, second, riders=False):
        k, tail = block(0, keep, core, first) + f32(second), None
        if riders:
            k, tail = k[:-TAIL], k[-TAIL:]
        if rest > 1:
            groups = [[a * rest + b for b in range(rest)] for a in range(PARTS)]
            k = k.reshape(-1, n, k.shape[-1])
            k = lax.psum_scatter(k, "dp", scatter_dimension=1, axis_index_groups=groups, tiled=True)
            k = k.reshape(-1, k.shape[-1])
            if riders:
                tail = lax.psum(tail, "dp", axis_index_groups=groups)
        return (k, tail) if riders else k

    half = PARTS // 2
    acts = [VMEM((T, D), BF)] * 2 + [VMEM((T, D), F32)] * 2 + [VMEM((T, H), BF)] * 2 + [VMEM((D, H), BF)] * 2
    grads = lambda k: [(SDS((half, k * 2 * n, H), BF), HBM)] * 2
    sums = [(SDS((T, D), F32), HBM)] * 2
    mixed, n2 = call(
        mid_kernel,
        "mid",
        6,
        24,
        [(tokens, VMEM), (row(bias_out), VMEM), (row(gain_mlp), VMEM), (row(shift_mlp), VMEM)]
        + [(os[r], VMEM) for r in range(planes)]
        + [(ws[r], VMEM) for r in range(planes)],
        [(SDS((T, D), F32), HBM), (SDS((T, D), BF), VMEM)],
        [VMEM((planes * e, T), BF), VMEM((planes * e, D), BF), VMEM((T, D), F32), sems(8)],
        after=[far_b],
    )
    n2, near_s, far_f = now(n2, near_s, far_f)
    near_b, far_b = join(near_b, near_s), join(far_b, far_f)
    near_r, far_s = to_core(near_b), to_second(far_b)
    out_acc, g_acc, u0_keep, u0_send, gb0 = call(
        own_kernel,
        "own",
        12,
        50,
        [(info, SMEM), (n2, VMEM), (cotangent, HBM), (piece, VMEM), (w_up, HBM), (w_down, HBM)],
        sums + grads(1) + [(SDS((1, H), F32), VMEM)],
        [acts[0], VMEM((D, H), BF), VMEM((H, D), BF)] + acts[2:] + [sems(24)],
        after=[near_b, far_b],
    )
    gb0, near_r, far_s = now(gb0, near_r, far_s)
    far_b = join(far_b, far_s)
    far_r, u0_core = to_core(far_b), to_core(u0_send)
    k = len(near)
    out_acc, g_acc, u13_keep, u13_send, gb13 = call(
        partial(mlp_kernel, k),
        "mlp",
        22,
        58,
        [(info, SMEM), (n2, HBM), (cotangent, HBM), (out_acc, HBM), (g_acc, HBM), (near_b, HBM), (near_r, HBM)]
        + [(pieces[r], VMEM) for r in near],
        sums + grads(k) + [(SDS((k, H), F32), VMEM)],
        acts + [sems(80)] + [VMEM((D, H), BF)] * k + [VMEM((H, D), BF)] * k,
        after=[far_b],
    )
    gb13, far_r, u0_core = now(gb13, far_r, u0_core)
    u0_first, u13_core = hop_first(u0_keep, u0_core), to_core(u13_send)
    result, grad_mixed, branch, u2_keep, u2_send, sm1 = call(
        mlp_last_kernel,
        "mlplast",
        15,
        58,
        [(info, SMEM), (n2, HBM), (cotangent, HBM), (out_acc, HBM), (g_acc, HBM), (far_b, HBM), (far_r, HBM)]
        + [(pieces[last_far], VMEM), (mixed, HBM), (row(bias_down), VMEM), (row(gain_mlp), VMEM), (gb0, VMEM), (gb13, VMEM)],
        [(SDS((T, D), BF), HBM), (SDS((T, D), F32), HBM), (SDS((T, D), BF), VMEM)]
        + grads(1)
        + [(SDS((8, H), F32), VMEM)],
        acts + [VMEM((D, H), BF), VMEM((H, D), BF), VMEM((T, D), F32), VMEM((T, D), BF), sems(56)],
    )

    back_sc = (
        [VMEM((heads, T, HEAD_DIM), BF)] * 2
        + [VMEM((e, T), BF)]
        + [VMEM((wm, qm), F32)] * 3
        + [VMEM((wm, qm), BF)] * 2
        + [VMEM((e, T), F32)] * 2
    )
    spec = (clips, tl, heads, scale, HEAD_DIM**-0.5)
    ins = lambda r: [(v, VMEM) for v in (branch, n1, qs[r], ws[r], os[r], ls[r])]
    ds, smalls = {}, {}

    def back(r, after):
        ds[r], keep, send, smalls[r] = call(
            partial(back_kernel, *spec),
            f"back{r}",
            11,
            30,
            [(info, SMEM)] + ins(r),
            [(SDS((3 * e, T), BF), VMEM)] + [(SDS((half, n, 4 * e), BF), HBM)] * 2 + [(SDS((1, 512), F32), VMEM)],
            [VMEM((D, 4 * e), BF), sems(8)] + back_sc,
            after=after,
        )
        return keep, send

    r2, r1, r3 = last_far, *near
    sm1, u0_first, u13_core = now(sm1, u0_first, u13_core)
    u0 = u0_keep, u0_core, u0_first
    u0_second, u13_first, u2_core = hop_second(*u0), hop_first(u13_keep, u13_core), to_core(u2_send)
    h2_keep, h2_send = back(r2, [sm1])
    t, u0_second, u13_first, u2_core = now(smalls[r2], u0_second, u13_first, u2_core)
    u13 = u13_keep, u13_core, u13_first
    u13_second, u2_first, h2_core = hop_second(*u13), hop_first(u2_keep, u2_core), to_core(h2_send)
    h1_keep, h1_send = back(r1, [u0_second, t])
    t, u13_second, u2_first, h2_core = now(smalls[r1], u13_second, u2_first, h2_core)
    u2 = u2_keep, u2_core, u2_first
    units_of = {0: total(*u0, u0_second)}
    pair = total(*u13, u13_second)
    rows = pair.shape[0] // len(near)
    for i, r in enumerate(near):
        units_of[r] = to_plane(pair[i * rows : (i + 1) * rows].astype(BF), r)
    u2_second, h2_first, h1_core = hop_second(*u2), hop_first(h2_keep, h2_core), to_core(h1_send)
    h3_keep, h3_send = back(r3, [u13_second, t])
    t, u2_second, h2_first, h1_core = now(smalls[r3], u2_second, h2_first, h1_core)
    h2 = h2_keep, h2_core, h2_first
    units_of[r2] = to_plane(total(*u2, u2_second).astype(BF), r2)
    h2_second, h1_first, h3_core = hop_second(*h2), hop_first(h1_keep, h1_core), to_core(h3_send)
    grad_tokens, keep, send = call(
        partial(last_kernel, *spec, planes),
        "last",
        22,
        58,
        [(info, SMEM)]
        + [(v, VMEM if v is ls[0] else HBM) for v in (branch, n1, qs[0], ws[0], os[0], ls[0])]
        + [(tokens, HBM), (row(gain_attn), VMEM), (grad_mixed, HBM), (sm1, VMEM)]
        + [(smalls[r], VMEM) for r in far]
        + [(ds[r], HBM) for r in far]
        + [(ws[r], HBM) for r in far],
        [(SDS((T, D), F32), HBM)] + [(SDS((half, n + TAIL, 4 * e), BF), HBM)] * 2,
        [VMEM((T, D), BF), VMEM((T, D), BF), VMEM((3 * e, T), BF), VMEM((4 * e, D), BF), VMEM((e, T), BF)]
        + [VMEM((D, 4 * e), BF), VMEM((3 * e, T), BF), VMEM((T, D), BF), VMEM((T, D), F32)]
        + [VMEM((planes - 1, 3 * e, T), BF), VMEM((planes - 1, 3 * e, D), BF), VMEM((T, D), F32)]
        + [VMEM((TAIL, D), F32), VMEM((TAIL, D), BF), sems(48)]
        + back_sc,
        after=[h2_first, t],
    )

    keep, h2_second, h1_first, h3_core, *came = now(keep, h2_second, h1_first, h3_core, *(units_of[r] for r in far))
    units_of.update(zip(far, came))
    h1 = h1_keep, h1_core, h1_first
    h0_core, h3_first, h1_second = to_core(send), hop_first(h3_keep, h3_core), hop_second(*h1)
    heads_of = {r2: to_plane(total(*h2, h2_second).astype(BF), r2)}
    h0_core, h3_first, h1_second = now(h0_core, h3_first, h1_second)
    h3 = h3_keep, h3_core, h3_first
    h0_first, h3_second = hop_first(keep, h0_core), hop_second(*h3)
    heads_of[r1] = to_plane(total(*h1, h1_second).astype(BF), r1)
    h0_first, h3_second = now(h0_first, h3_second)
    h0 = keep, h0_core, h0_first
    h0_second = hop_second(*h0)
    heads_of[r3] = to_plane(total(*h3, h3_second).astype(BF), r3)
    heads_of[0], tail = total(*h0, h0_second, riders=True)
    tail_low = tail.astype(BF)
    tails = {0: tail, **{r: f32(to_plane(tail_low, r)) for r in far}}

    m = D // places
    units = units_of[0] + sum(f32(units_of[r]) for r in far)
    hd = heads_of[0] + sum(f32(heads_of[r]) for r in far)
    grad_w_up, grad_w_down = units[:m], units[m:].T
    grad_w_qkv = hd[:, : 3 * e].reshape(m, 3, e).transpose(1, 0, 2)
    grad_w_out = hd[:, 3 * e :].T

    seat = {r: i for i, r in enumerate([0] + far)}
    g_ga, g_sa, g_bo, g_gm, g_sm, g_bd = [sum(v[j] for v in tails.values()) for j in (0, 1, 6, 7, 8, 9)]
    bu = sum(tails[r][10 + seat[r]] for r in range(planes))
    qv = sum(tails[r][2 + seat[r]] for r in range(planes))
    slice_of = lambda v, at, size: lax.dynamic_slice_in_dim(v, at, size, v.ndim - 1)
    size = D // (places * planes)
    vecs = [slice_of(v, (d * planes + z) * size, size) for v in (g_ga, g_sa, g_bo, g_gm, g_sm, g_bd)]
    grad_bias_up = slice_of(bu, d * (H // places), H // places)
    qv = jnp.stack([qv[:e], qv[256 : 256 + e]])
    grad_bias_qv = slice_of(qv, d * (e // places), e // places)
    return (
        result,
        grad_tokens,
        vecs[0],
        vecs[1],
        grad_w_qkv,
        grad_bias_qv,
        grad_w_out,
        vecs[2],
        vecs[3],
        vecs[4],
        grad_w_up,
        grad_bias_up,
        grad_w_down,
        vecs[5],
    )


def solution(mesh):
    return jax.shard_map(
        partial(on_device, mesh.shape["dp"], mesh.shape["mp"]),
        mesh=mesh,
        in_specs=(
            P(("dp", "mp"), None),
            P("dp", None),
            P(),
            P(),
            P(None, None, "mp"),
            P(None, "mp"),
            P("mp", None),
            P(),
            P(),
            P(),
            P(None, "mp"),
            P("mp"),
            P("mp", None),
            P(),
            P(("dp", "mp"), None),
        ),
        out_specs=(
            P(("dp", "mp"), None),
            P(("dp", "mp"), None),
            P(("dp", "mp")),
            P(("dp", "mp")),
            P(None, "dp", "mp"),
            P(None, ("mp", "dp")),
            P("mp", "dp"),
            P(("dp", "mp")),
            P(("dp", "mp")),
            P(("dp", "mp")),
            P("dp", "mp"),
            P(("mp", "dp")),
            P("mp", "dp"),
            P(("dp", "mp")),
        ),
        check_vma=False,
    )
```

```python
from functools import partial

import jax
import jax.numpy as jnp
import numpy as np
from jax import lax
from jax.experimental import pallas as pl
from jax.experimental.pallas import tpu as pltpu
from jax.sharding import PartitionSpec as P

F32, BF = jnp.float32, jnp.bfloat16
HEAD_DIM = 64
MOST = 256
EPSILON = 1e-06
MASKED = -1e30
LOG2E = 1.4426950408889634
ROOT_HALF = 0.7071067811865476
RSQRT_2PI = 0.3989422804014327
PARTS = 8
KEY_BLOCK = 128
TAIL = 16
GATHERED, EXCHANGED, PLACE = 8, 16, 24
VMEM, SMEM, HBM = pltpu.VMEM, pltpu.SMEM, pltpu.HBM
LANES = 128
SDS = jax.ShapeDtypeStruct


def _dot(a, b, i, j):
    return lax.dot_general(a, b, (((i,), (j,)), ((), ())), preferred_element_type=F32)


def nn(a, b):
    return _dot(a, b, 1, 0)


def nt(a, b):
    return _dot(a, b, 1, 1)


def tn(a, b):
    return _dot(a, b, 0, 0)


def tt(a, b):
    return _dot(a, b, 0, 1)


def call(body, name, us, megabytes, ins, outs, scratch, after=()):
    count, skip = len(ins), len(ins) + len(after)

    def kernel(*refs):
        body(*refs[:count], *refs[skip:])

    return pl.pallas_call(
        kernel,
        out_shape=tuple(o[0] for o in outs),
        in_specs=[pl.BlockSpec(memory_space=m) for _, m in ins] + [pl.BlockSpec(memory_space=HBM)] * len(after),
        out_specs=tuple(pl.BlockSpec(memory_space=m) for _, m in outs),
        scratch_shapes=scratch,
        compiler_params=pltpu.CompilerParams(vmem_limit_bytes=megabytes << 20),
        cost_estimate=pl.CostEstimate(flops=int(us * 1.0e9), bytes_accessed=1 << 20, transcendentals=0),
        name=name,
    )(*(a for a, _ in ins), *after)


class Mover:
    def __init__(self, sems):
        self.sems, self.used = sems, 0

    def __call__(self, src, dst):
        c = pltpu.make_async_copy(src, dst, self.sems.at[self.used])
        self.used += 1
        c.start()
        return c


def wait(*copies):
    for c in copies:
        c.wait()


def windows(slots, width=256):
    out = []
    for q0 in range(0, slots, width):
        qn = min(width, slots - q0)
        lo = max(0, (q0 - MOST + 1) // 128 * 128)
        hi = min(slots, -(-(q0 + qn + MOST - 1) // 128) * 128)
        out.append((q0, qn, lo, hi - lo))
    return out


def segments(info, clips, shape, axis):
    place = lax.broadcasted_iota(jnp.int32, shape, axis)
    seg = jnp.zeros(shape, jnp.int32)
    for c in range(clips):
        seg = seg + jnp.where(place >= info[c], 1, 0)
    return jnp.where(seg == clips - 1, place + clips, seg)


def fill_mask(bias_sc, segc, segr, q0, qn, k0, w):
    for b in range(0, w, KEY_BLOCK):
        same = segc[k0 + b : k0 + b + KEY_BLOCK, :] == segr[:, q0 : q0 + qn]
        bias_sc[b : b + KEY_BLOCK, :qn] = jnp.where(same, 0.0, MASKED)


def fold(x, f):
    return f(x.reshape(x.shape[0] // 8, 8, x.shape[1]), axis=0)


def attend(tl, heads, scale, qkvT, kn, segc, segr, oT, lse, bias_sc, s_sc, p_sc):
    e, hd = heads * HEAD_DIM, HEAD_DIM
    for q0, qn, k0, w in tl:
        fill_mask(bias_sc, segc, segr, q0, qn, k0, w)
        for h in range(heads):
            q = qkvT[h * hd : (h + 1) * hd, q0 : q0 + qn]
            m = None
            for b in range(0, w, KEY_BLOCK):
                s = nn(kn[h, k0 + b : k0 + b + KEY_BLOCK, :], q) * scale + bias_sc[b : b + KEY_BLOCK, :qn]
                s_sc[b : b + KEY_BLOCK, :qn] = s
                mb = fold(s, jnp.max)
                m = mb if m is None else jnp.maximum(m, mb)
            m = jnp.max(m, axis=0, keepdims=True)
            total = None
            for b in range(0, w, KEY_BLOCK):
                p = jnp.exp2(s_sc[b : b + KEY_BLOCK, :qn] - m)
                p_sc[b : b + KEY_BLOCK, :qn] = p.astype(BF)
                lb = fold(p, jnp.sum)
                total = lb if total is None else total + lb
            total = jnp.sum(total, axis=0, keepdims=True)
            o = nn(qkvT[2 * e + h * hd : 2 * e + (h + 1) * hd, k0 : k0 + w], p_sc[:w, :qn])
            oT[h * hd : (h + 1) * hd, q0 : q0 + qn] = (o * (1.0 / total)).astype(BF)
            lse[h : h + 1, q0 : q0 + qn] = m + jnp.log2(total)


def unit(x):
    y = x - jnp.mean(x, axis=1, keepdims=True)
    inverse = lax.rsqrt(jnp.mean(y * y, axis=1, keepdims=True) + EPSILON)
    return y * inverse, inverse


def unit_back(up, n, inverse, gain):
    g = up * gain
    return inverse * (g - jnp.mean(g, axis=1, keepdims=True) - n * jnp.mean(g * n, axis=1, keepdims=True))


def normal(u):
    bell = jnp.exp2(u * u * (-0.5 * LOG2E))
    d = jnp.abs(u) * (0.3275911 * ROOT_HALF) + 1.0
    t = pl.reciprocal(d, approx=True)
    t = t * (2.0 - d * t)
    q = 0.5 * 1.061405429
    for c in (-1.453152027, 1.421413741, -0.284496736, 0.254829592):
        q = q * t + 0.5 * c
    q = q * t * bell
    return jnp.where(u >= 0.0, 1.0 - q, q), bell * RSQRT_2PI


def gather_rows(move, info, at, blocks, target, n):
    return [
        move(ref.at[pl.ds(row, n)], target.at[pl.ds(pl.multiple_of(info[at + i] * n, n), n)])
        for i, (ref, row) in enumerate(blocks)
    ]


def blocks_out(move, info, source, place, keep, send):
    n, half = source.shape[0] // PARTS, PARTS // 2
    return [
        move(
            source.at[pl.ds(pl.multiple_of(info[EXCHANGED + j] * n, n), n)],
            (keep if j < half else send).at[j % half, pl.ds(place, n)],
        )
        for j in range(PARTS)
    ]


def cut_kernel(info, w_heads, w_out, w_up, w_down, bias_qv, bias_up, w0, piece, units, up, down, tail_s, sems):
    e, H = w_out.shape[0], bias_up.shape[1]
    n = units.shape[0] // 2
    move = Mover(sems)
    row = pl.ds(pl.multiple_of(info[PLACE] * n, n), n)
    tail = piece.at[pl.ds(n, TAIL)]
    tail_s[...] = jnp.zeros_like(tail_s)
    tail_s[0:1, :H] = bias_up[...].astype(F32)
    for i in range(2):
        tail_s[1:2, 256 * i : 256 * i + e] = bias_qv[i : i + 1, :].astype(F32)
    tail[...] = tail_s[...].astype(BF)
    done = [move(w_up.at[row], units.at[pl.ds(0, n)]), move(w_down.at[row], units.at[pl.ds(n, n)])]
    done += [move(w_heads, w0.at[pl.ds(0, 3 * e)]), move(w_out, w0.at[pl.ds(3 * e, e)])]
    wait(*done)
    piece[pl.ds(0, n), :] = w0[row, :]
    up[...] = units[:n, :]
    down[...] = units[n:, :]


def project(heads, n1, w, piece, qkvT):
    e = heads * HEAD_DIM
    n = piece.shape[0] - TAIL
    biases = piece[n : n + TAIL, :512].astype(F32)[1:2, :]
    for c in range(3):
        t = nt(w[c * e : (c + 1) * e, :], n1[...])
        if c != 1:
            at = 128 * c
            t = t + jnp.broadcast_to(biases[:, at : at + 256], (LANES, 256)).T[:e, :1]
        qkvT[c * e : (c + 1) * e, :] = t.astype(BF)


def attend_kernel(clips, tl, heads, scale, info, qkvT, oT, lse, kn, bias_sc, s_sc, p_sc):
    slots = qkvT.shape[1]
    segc = segments(info, clips, (slots, 1), 0)
    segr = segments(info, clips, (1, slots), 1)
    e = heads * HEAD_DIM
    for h in range(heads):
        kn[h] = qkvT[e + h * HEAD_DIM : e + (h + 1) * HEAD_DIM, :].T
    attend(tl, heads, scale, qkvT, kn, segc, segr, oT, lse, bias_sc, s_sc, p_sc)


def first_kernel(heads, x, gain, shift, w, piece, n1, qkvT):
    for i in range(0, x.shape[0], LANES):
        n, _ = unit(x[i : i + LANES, :].astype(F32))
        n1[i : i + LANES, :] = (n * gain[...].astype(F32) + shift[...].astype(F32)).astype(BF)
    project(heads, n1, w, piece, qkvT)


def attn_kernel(clips, tl, heads, scale, info, n1, piece, p4, r4, w, qkvT, oT, lse, *scratch):
    n = w.shape[0] // PARTS
    for i in range(PARTS):
        ref = (p4, r4)[i // 4]
        w[pl.ds(pl.multiple_of(info[GATHERED + i] * n, n), n), :] = ref[i % 4 * n : (i % 4 + 1) * n, :]
    project(heads, n1, w, piece, qkvT)
    attend_kernel(clips, tl, heads, scale, info, qkvT, oT, lse, *scratch)


def chunk_front(n2, cot, wup, wdn, piece, hid, gp, gb):
    n = piece.shape[0] - TAIL
    u = nn(n2[...], wup[...]) + piece[n : n + TAIL, :].astype(F32)[0:1, : wup.shape[1]]
    ga = nt(cot[...], wdn[...])
    dist, dens = normal(u)
    hid[...] = (u * dist).astype(BF)
    g = (ga * (dist + u * dens)).astype(BF)
    gp[...] = g
    gb[...] = jnp.sum(g.astype(F32), axis=0, keepdims=True)


def chunk_sums(hid, gp, wup, wdn, out_acc, g_acc, fresh):
    o = nn(hid[...], wdn[...])
    out_acc[...] = o if fresh else out_acc[...] + o
    g = nt(gp[...], wup[...])
    g_acc[...] = g if fresh else g_acc[...] + g


def chunk_grads(move, info, n2, cot, hid, gp, up_sc, dn_sc, k, keep, send):
    n = n2.shape[1] // PARTS
    dn_sc[...] = tn(cot[...], hid[...]).astype(BF)
    copies = blocks_out(move, info, dn_sc, (2 * k + 1) * n, keep, send)
    up_sc[...] = tn(n2[...], gp[...]).astype(BF)
    return copies + blocks_out(move, info, up_sc, 2 * k * n, keep, send)


def mid_kernel(x, bias_out, gain, shift, *refs):
    count = (len(refs) - 6) // 2
    o, w, refs = refs[:count], refs[count : 2 * count], refs[2 * count :]
    mixed, n2, o_s, wo_s, mixed_s, sems = refs
    e = o[0].shape[0]
    move = Mover(sems)
    for r in range(count):
        o_s[r * e : (r + 1) * e, :] = o[r][...]
        wo_s[r * e : (r + 1) * e, :] = w[r][3 * e : 4 * e, :]
    mixed_s[...] = tn(o_s[...], wo_s[...])
    done = []
    for i in range(0, x.shape[0], LANES):
        k = slice(i, i + LANES)
        m = mixed_s[k, :] + x[k, :].astype(F32) + bias_out[...].astype(F32)
        mixed_s[k, :] = m
        done.append(move(mixed_s.at[pl.ds(i, LANES)], mixed.at[pl.ds(i, LANES)]))
        n, _ = unit(m)
        n2[k, :] = (n * gain[...].astype(F32) + shift[...].astype(F32)).astype(BF)
    wait(*done)


def own_kernel(info, n2, cot, piece, wup, wdn, out, g, keep, send, gb, out_s, g_s, hid, gp, up_sc, dn_sc, sems):
    move = Mover(sems)
    chunk_front(n2, cot, wup, wdn, piece, hid, gp, gb)
    chunk_sums(hid, gp, wup, wdn, out_s, g_s, True)
    done = [move(out_s, out), move(g_s, g)]
    wait(*chunk_grads(move, info, n2, cot, hid, gp, up_sc, dn_sc, 0, keep, send), *done)


def mlp_kernel(count, info, n2, cot, out_in, g_in, p4, r4, *refs):
    small, refs = refs[:count], refs[count:]
    out, g, keep, send, gb = refs[:5]
    n2_s, cot_s, out_s, g_s, hid, gp, up_sc, dn_sc, sems = refs[5:14]
    wup_s, wdn_s = refs[14 : 14 + count], refs[14 + count :]
    move = Mover(sems)
    n = n2_s.shape[1] // PARTS
    front = [move(n2, n2_s), move(cot, cot_s)]
    ready = [units_here(move, info, p4, r4, wup_s[k], wdn_s[k], n, k, count) for k in range(count)]
    sums = [move(out_in, out_s), move(g_in, g_s)]
    wait(*front)
    done = []
    for k in range(count):
        wait(*ready[k])
        chunk_front(n2_s, cot_s, wup_s[k], wdn_s[k], small[k], hid, gp, gb.at[pl.ds(k, 1)])
        if k == 0:
            wait(*sums)
        chunk_sums(hid, gp, wup_s[k], wdn_s[k], out_s, g_s, False)
        wait(*done)
        done = []
        if k == count - 1:
            done = [move(out_s, out), move(g_s, g)]
        done += chunk_grads(move, info, n2_s, cot_s, hid, gp, up_sc, dn_sc, k, keep, send)
    wait(*done)


def units_here(move, info, p4, r4, wup, wdn, n, k, count):
    blocks = [(ref, (i * count + k) * 2 * n) for ref in (p4, r4) for i in range(PARTS // 2)]
    return gather_rows(move, info, GATHERED, blocks, wup, n) + gather_rows(
        move, info, GATHERED, [(ref, row + n) for ref, row in blocks], wdn, n
    )


def mlp_last_kernel(info, n2, cot, out_in, g_in, p4, r4, small, mixed, bias_down, gain, *refs):
    gbs, refs = refs[: len(refs) - 19], refs[len(refs) - 19 :]
    result, grad_mixed, branch, keep, send, sm = refs[:6]
    n2_s, cot_s, out_s, g_s, hid, gp, up_sc, dn_sc, wup_s, wdn_s, mixed_s, result_s, sems = refs[6:]
    move = Mover(sems)
    n = n2_s.shape[1] // PARTS
    front = [move(n2, n2_s), move(cot, cot_s)] + units_here(move, info, p4, r4, wup_s, wdn_s, n, 0, 1)
    sums = [move(out_in, out_s), move(g_in, g_s), move(mixed, mixed_s)]
    wait(*front)
    chunk_front(n2_s, cot_s, wup_s, wdn_s, small, hid, gp, sm.at[pl.ds(7, 1)])
    wait(*sums)
    chunk_sums(hid, gp, wup_s, wdn_s, out_s, g_s, False)
    vecs = [0.0] * 4
    for i in range(0, n2.shape[0], LANES):
        k = slice(i, i + LANES)
        up, mid, c = g_s[k, :], mixed_s[k, :], cot_s[k, :].astype(F32)
        result_s[k, :] = (mid + out_s[k, :] + bias_down[...].astype(F32)).astype(BF)
        m, inverse = unit(mid)
        gm = c + unit_back(up, m, inverse, gain[...].astype(F32))
        mixed_s[k, :] = gm
        branch[k, :] = gm.astype(BF)
        for j, v in enumerate((gm, up * m, up, c)):
            vecs[j] = vecs[j] + fold(v, jnp.sum)
    done = [move(mixed_s, grad_mixed), move(result_s, result)]
    for j in range(4):
        sm[j : j + 1, :] = jnp.sum(vecs[j], axis=0, keepdims=True)
    at = 4
    for ref in gbs:
        sm[at : at + ref.shape[0], :] = ref[...]
        at += ref.shape[0]
    done += chunk_grads(move, info, n2_s, cot_s, hid, gp, up_sc, dn_sc, 0, keep, send)
    wait(*done)


def back_heads(clips, tl, heads, scale, part, info, gb, w, q_s, oT, lse, d_s, scratch):
    kn, vn, ga, bias_sc, pb_sc, ds_sc, dk, dv = scratch
    e, hd = heads * HEAD_DIM, HEAD_DIM
    slots = gb.shape[0]
    segc = segments(info, clips, (slots, 1), 0)
    segr = segments(info, clips, (1, slots), 1)
    ga[...] = nt(w[3 * e : 4 * e, :], gb[...]).astype(BF)
    for h in range(heads):
        kn[h] = q_s[e + h * hd : e + (h + 1) * hd, :].T
        vn[h] = q_s[2 * e + h * hd : 2 * e + (h + 1) * hd, :].T
    dk[...] = jnp.zeros_like(dk)
    dv[...] = jnp.zeros_like(dv)
    for q0, qn, k0, wide in tl:
        fill_mask(bias_sc, segc, segr, q0, qn, k0, wide)
        for h in range(heads):
            hs = slice(h * hd, (h + 1) * hd)
            q, go = q_s[hs, q0 : q0 + qn], ga[hs, q0 : q0 + qn]
            total = lse[h : h + 1, q0 : q0 + qn]
            centre = jnp.sum(go.astype(F32) * oT[hs, q0 : q0 + qn].astype(F32), axis=0, keepdims=True)
            for b in range(0, wide, KEY_BLOCK):
                k, v = slice(b, b + KEY_BLOCK), slice(k0 + b, k0 + b + KEY_BLOCK)
                p = jnp.exp2(nn(kn[h, v, :], q) * scale + bias_sc[k, :qn] - total)
                pb_sc[k, :qn] = p.astype(BF)
                ds_sc[k, :qn] = (p * (nn(vn[h, v, :], go) - centre)).astype(BF)
            ds = ds_sc[:wide, :qn]
            d_s[hs, q0 : q0 + qn] = (nn(q_s[e + h * hd : e + (h + 1) * hd, k0 : k0 + wide], ds) * part).astype(BF)
            dk[hs, k0 : k0 + wide] += nt(q, ds)
            dv[hs, k0 : k0 + wide] += nt(go, pb_sc[:wide, :qn])
    d_s[e : 2 * e, :] = (dk[...] * part).astype(BF)
    d_s[2 * e : 3 * e, :] = dv[...].astype(BF)


def bias_rows(d_s, small, at, e):
    rows = nt(jnp.ones((8, d_s.shape[1]), BF), d_s[...])
    small[at : at + 1, 0:e] = rows[0:1, 0:e]
    small[at : at + 1, 256 : 256 + e] = rows[0:1, 2 * e : 3 * e]


def head_grads(move, info, gb, n1, oT, d_s, acc, keep, send):
    k = d_s.shape[0]
    acc[:, :k] = tt(n1[...], d_s[...]).astype(BF)
    acc[:, k:] = tt(gb[...], oT[...]).astype(BF)
    return blocks_out(move, info, acc, 0, keep, send)


def back_kernel(clips, tl, heads, scale, part, info, gb, n1, q, w, oT, lse, d, keep, send, small, acc, sems, *scratch):
    small[...] = jnp.zeros_like(small)
    back_heads(clips, tl, heads, scale, part, info, gb, w, q, oT, lse, d, scratch)
    bias_rows(d, small, 0, heads * HEAD_DIM)
    wait(*head_grads(Mover(sems), info, gb, n1, oT, d, acc, keep, send))


def last_kernel(planes, x, gain, grad_mixed, sm1, *refs):
    d, w, smalls = refs[:planes], refs[planes : 2 * planes], refs[2 * planes : 3 * planes]
    grad_tokens, sm, g_sc, gm_s, sems = refs[3 * planes :]
    rows = d[0].shape[0]
    move = Mover(sems)
    for r in range(planes):
        g = tn(d[r][...], w[r][:rows, :])
        g_sc[...] = g if r == 0 else g_sc[...] + g
    vecs, done = [0.0] * 2, []
    for i in range(0, x.shape[0], LANES):
        k = slice(i, i + LANES)
        up = g_sc[k, :]
        m, inverse = unit(x[k, :].astype(F32))
        gm_s[k, :] = grad_mixed[k, :] + unit_back(up, m, inverse, gain[...].astype(F32))
        done.append(move(gm_s.at[pl.ds(i, LANES)], grad_tokens.at[pl.ds(i, LANES)]))
        for j, v in enumerate((up * m, up)):
            vecs[j] = vecs[j] + fold(v, jnp.sum)
    sm[...] = jnp.zeros_like(sm)
    for j in range(2):
        sm[j : j + 1, :] = jnp.sum(vecs[j], axis=0, keepdims=True)
    for r in range(planes):
        sm[2 + r : 3 + r, :512] = smalls[r][...]
    sm[6:14, :] = sm1[...]
    wait(*done)


def on_device(
    places,
    planes,
    tokens,
    clip_lengths,
    gain_attn,
    shift_attn,
    w_qkv,
    bias_qv,
    w_out,
    bias_out,
    gain_mlp,
    shift_mlp,
    w_up,
    bias_up,
    w_down,
    bias_down,
    cotangent,
):
    T, D = tokens.shape
    clips = clip_lengths.shape[1]
    e = w_out.shape[0]
    heads = e // HEAD_DIM
    H = w_up.shape[1]
    n = D // PARTS
    rest = places // PARTS
    d, z = lax.axis_index("dp"), lax.axis_index("mp")
    hi = d // rest
    f32 = lambda v: v.astype(F32)
    row = lambda v: v.reshape(1, -1)

    core = hi % 2
    first, second = jnp.where(core == 0, 2, 4), jnp.where(core == 0, 4, 2)
    both = lambda a, f, s: [a, a ^ f, a ^ s, a ^ 6]
    order = lambda a, f, s: [a, a ^ s, a ^ f, a ^ 6]
    gathered = both(hi, first, second) + both(hi ^ 1, second, first)
    exchanged = order(hi, first, second) + order(hi ^ 1, second, first)
    ends = jnp.cumsum(lax.dynamic_index_in_dim(clip_lengths, z, 0, keepdims=False))
    ends = jnp.concatenate([ends, jnp.zeros((GATHERED - clips,), jnp.int32)])
    info = jnp.concatenate([ends, jnp.stack(gathered + exchanged + [hi]).astype(jnp.int32)])

    def over_plane(v, flip):
        to = lambda a: ((a // rest) ^ flip((a // rest) % 2)) * rest + a % rest
        return lax.ppermute(v, "dp", [(a, to(a)) for a in range(places)])

    to_core = lambda v: over_plane(v, lambda c: 1)
    to_first = lambda v: over_plane(v, lambda c: 4 if c else 2)
    to_second = lambda v: over_plane(v, lambda c: 2 if c else 4)
    to_both = lambda v: over_plane(v, lambda c: 6)
    shift = lambda v, r: lax.ppermute(v, "mp", [(a, (a + r) % planes) for a in range(planes)])
    from_plane = lambda v, r: shift(v, -r)
    to_plane = shift

    def now(*arrays):
        return lax.optimization_barrier(arrays)

    near, last_far = [1, 3], 2
    far = near + [last_far]

    sems = lambda k: pltpu.SemaphoreType.DMA((k,))
    w_heads = w_qkv.transpose(0, 2, 1).reshape(3 * e, D)
    w0, piece, unit_piece, *unit_halves = call(
        cut_kernel,
        "cut",
        3,
        60,
        [(info, SMEM), (w_heads, HBM), (w_out, HBM), (w_up, HBM), (w_down, HBM), (bias_qv, VMEM), (row(bias_up), VMEM)],
        [(SDS((4 * e, D), BF), VMEM), (SDS((n + TAIL, D), BF), VMEM), (SDS((2 * n, D), BF), VMEM)]
        + [(SDS((n, D), BF), VMEM)] * 2,
        [VMEM((TAIL, D), F32), sems(4)],
    )
    pieces = {0: piece, **{r: from_plane(piece, r) for r in far}}

    tl = windows(T)
    wm, qm = max(t[3] for t in tl), max(t[1] for t in tl)
    scale = HEAD_DIM**-0.5 * LOG2E
    attn_out = [(SDS((3 * e, T), BF), VMEM), (SDS((e, T), BF), VMEM), (SDS((8, T), F32), VMEM)]
    attn_sc = [VMEM((heads, T, HEAD_DIM), BF), VMEM((wm, qm), F32), VMEM((wm, qm), F32), VMEM((wm, qm), BF)]
    n1, q0 = call(
        partial(first_kernel, heads),
        "first",
        4,
        20,
        [(tokens, VMEM), (row(gain_attn), VMEM), (row(shift_attn), VMEM), (w0, VMEM), (piece, VMEM)],
        [(SDS((T, D), BF), VMEM), attn_out[0]],
        [],
    )
    ws, qs, os, ls = {0: w0}, {0: q0}, {}, {}

    def join(*v):
        return jnp.concatenate(v)

    def attn(r, c4, r4, after, us=7):
        ws[r], qs[r], os[r], ls[r] = call(
            partial(attn_kernel, clips, tl, heads, scale),
            f"attn{r}",
            us,
            24,
            [(info, SMEM), (n1, VMEM), (pieces[r], VMEM), (c4, VMEM), (r4, VMEM)],
            [(SDS((4 * e, D), BF), VMEM)] + attn_out,
            attn_sc,
            after=after,
        )
        return ls[r]

    a1, a3, a2 = far
    q0, p1, p3 = now(q0, pieces[a1], pieces[a3])
    got1 = [p1, to_first(p1), to_second(p1), to_both(p1)]
    f3 = to_first(p3)
    os[0], ls[0] = call(
        partial(attend_kernel, clips, tl, heads, scale),
        "attend0",
        4,
        20,
        [(info, SMEM), (q0, VMEM)],
        attn_out[1:],
        attn_sc,
    )
    _, p3, f3, p2, *got1 = now(ls[0], p3, f3, pieces[a2], *got1)
    c1, c3 = join(*(v[:n] for v in got1)), join(p3[:n], f3[:n])
    core1, s3, f2 = to_core(c1), to_second(c3), to_first(p2)
    near_piece = now(unit_piece, c1)[0]
    near_z = [from_plane(near_piece, r) for r in near]
    t = attn(a1, c1, core1, [])
    _, s3, f2, *near_z = now(t, s3, f2, *near_z)
    c3, c2, near_b = join(c3, s3), join(p2[:n], f2[:n]), join(*near_z)
    core3, s2, near_f = to_core(c3), to_second(c2), to_first(near_b)
    far_up = from_plane(now(unit_halves[0], near_b)[0], last_far)
    t = attn(a3, c3, core3, [c2, near_b])
    _, s2, near_f, far_up = now(t, s2, near_f, far_up)
    far_down = from_plane(now(unit_halves[1], far_up)[0], last_far)
    c2, near_b = join(c2, s2), join(near_b, near_f)
    core2, near_s = to_core(c2), to_second(near_b)
    t = attn(a2, c2, core2, [near_b])
    far_b = join(far_up, now(t, far_down)[1])
    far_f = to_first(far_b)

    def block(i, keep, core, first):
        return f32(keep[i]) + f32(core[i]) + f32(first[i])

    def hop_first(keep, core):
        half = PARTS // 4
        return to_first((f32(keep[half:]) + f32(core[half:])).astype(BF))

    def hop_second(*had):
        return to_second(block(1, *had).astype(BF))

    def total(keep, core, first, second):
        k = block(0, keep, core, first) + f32(second)
        if rest > 1:
            groups = [[a * rest + b for b in range(rest)] for a in range(PARTS)]
            k = k.reshape(-1, n, k.shape[-1])
            k = lax.psum_scatter(k, "dp", scatter_dimension=1, axis_index_groups=groups, tiled=True)
            k = k.reshape(-1, k.shape[-1])
        return k

    half = PARTS // 2
    acts = [VMEM((T, D), BF)] * 2 + [VMEM((T, D), F32)] * 2 + [VMEM((T, H), BF)] * 2 + [VMEM((D, H), BF)] * 2
    grads = lambda k: [(SDS((half, k * 2 * n, H), BF), HBM)] * 2
    sums = [(SDS((T, D), F32), HBM)] * 2
    mixed, n2 = call(
        mid_kernel,
        "mid",
        6,
        24,
        [(tokens, VMEM), (row(bias_out), VMEM), (row(gain_mlp), VMEM), (row(shift_mlp), VMEM)]
        + [(os[r], VMEM) for r in range(planes)]
        + [(ws[r], VMEM) for r in range(planes)],
        [(SDS((T, D), F32), HBM), (SDS((T, D), BF), VMEM)],
        [VMEM((planes * e, T), BF), VMEM((planes * e, D), BF), VMEM((T, D), F32), sems(8)],
        after=[far_b],
    )
    n2, near_s, far_f = now(n2, near_s, far_f)
    near_b, far_b = join(near_b, near_s), join(far_b, far_f)
    near_r, far_s = to_core(near_b), to_second(far_b)
    out_acc, g_acc, u0_keep, u0_send, gb0 = call(
        own_kernel,
        "own",
        12,
        40,
        [(info, SMEM), (n2, VMEM), (cotangent, VMEM), (piece, VMEM), (w_up, VMEM), (w_down, VMEM)],
        sums + grads(1) + [(SDS((1, H), F32), VMEM)],
        acts[2:] + [sems(24)],
        after=[near_b, far_b],
    )
    gb0, near_r, far_s = now(gb0, near_r, far_s)
    far_b = join(far_b, far_s)
    far_r, u0_core = to_core(far_b), to_core(u0_send)
    k = len(near)
    out_acc, g_acc, u13_keep, u13_send, gb13 = call(
        partial(mlp_kernel, k),
        "mlp",
        22,
        58,
        [(info, SMEM), (n2, HBM), (cotangent, HBM), (out_acc, HBM), (g_acc, HBM), (near_b, HBM), (near_r, HBM)]
        + [(pieces[r], VMEM) for r in near],
        sums + grads(k) + [(SDS((k, H), F32), VMEM)],
        acts + [sems(80)] + [VMEM((D, H), BF)] * k + [VMEM((H, D), BF)] * k,
        after=[far_b],
    )
    gb13, far_r, u0_core = now(gb13, far_r, u0_core)
    u0_first, u13_core = hop_first(u0_keep, u0_core), to_core(u13_send)
    result, grad_mixed, branch, u2_keep, u2_send, sm1 = call(
        mlp_last_kernel,
        "mlplast",
        15,
        58,
        [(info, SMEM), (n2, HBM), (cotangent, HBM), (out_acc, HBM), (g_acc, HBM), (far_b, HBM), (far_r, HBM)]
        + [(pieces[last_far], VMEM), (mixed, HBM), (row(bias_down), VMEM), (row(gain_mlp), VMEM), (gb0, VMEM), (gb13, VMEM)],
        [(SDS((T, D), BF), HBM), (SDS((T, D), F32), HBM), (SDS((T, D), BF), VMEM)]
        + grads(1)
        + [(SDS((8, H), F32), VMEM)],
        acts + [VMEM((D, H), BF), VMEM((H, D), BF), VMEM((T, D), F32), VMEM((T, D), BF), sems(56)],
    )

    back_sc = (
        [VMEM((heads, T, HEAD_DIM), BF)] * 2
        + [VMEM((e, T), BF)]
        + [VMEM((wm, qm), F32)]
        + [VMEM((wm, qm), BF)] * 2
        + [VMEM((e, T), F32)] * 2
    )
    spec = (clips, tl, heads, scale, HEAD_DIM**-0.5)
    ins = lambda r: [(v, VMEM) for v in (branch, n1, qs[r], ws[r], os[r], ls[r])]
    ds, smalls = {}, {}

    def back(r, after):
        ds[r], keep, send, smalls[r] = call(
            partial(back_kernel, *spec),
            f"back{r}",
            11,
            30,
            [(info, SMEM)] + ins(r),
            [(SDS((3 * e, T), BF), VMEM)] + [(SDS((half, n, 4 * e), BF), HBM)] * 2 + [(SDS((1, 512), F32), VMEM)],
            [VMEM((D, 4 * e), BF), sems(8)] + back_sc,
            after=after,
        )
        return keep, send

    r2, r1, r3 = last_far, *near
    sm1, u0_first, u13_core = now(sm1, u0_first, u13_core)
    u0 = u0_keep, u0_core, u0_first
    u0_second, u13_first, u2_core = hop_second(*u0), hop_first(u13_keep, u13_core), to_core(u2_send)
    h2_keep, h2_send = back(r2, [sm1])
    t, u0_second, u13_first, u2_core = now(smalls[r2], u0_second, u13_first, u2_core)
    u13 = u13_keep, u13_core, u13_first
    u13_second, u2_first, h2_core = hop_second(*u13), hop_first(u2_keep, u2_core), to_core(h2_send)
    h1_keep, h1_send = back(r1, [u0_second, t])
    t, u13_second, u2_first, h2_core = now(smalls[r1], u13_second, u2_first, h2_core)
    u2 = u2_keep, u2_core, u2_first
    units_of = {0: total(*u0, u0_second)}
    pair = total(*u13, u13_second)
    rows = pair.shape[0] // len(near)
    for i, r in enumerate(near):
        units_of[r] = to_plane(pair[i * rows : (i + 1) * rows].astype(BF), r)
    u2_second, h2_first, h1_core = hop_second(*u2), hop_first(h2_keep, h2_core), to_core(h1_send)
    h3_keep, h3_send = back(r3, [u13_second, t])
    t, u2_second, h2_first, h1_core, *came = now(smalls[r3], u2_second, h2_first, h1_core, *(units_of[r] for r in near))
    units_of.update(zip(near, came))
    h2 = h2_keep, h2_core, h2_first
    units_of[r2] = to_plane(total(*u2, u2_second).astype(BF), r2)
    h2_second, h1_first, h3_core = hop_second(*h2), hop_first(h1_keep, h1_core), to_core(h3_send)
    h0_keep, h0_send = back(0, [h2_first, t])
    t, h2_second, h1_first, h3_core, units_of[r2] = now(smalls[0], h2_second, h1_first, h3_core, units_of[r2])
    h1 = h1_keep, h1_core, h1_first
    heads_of = {r2: to_plane(total(*h2, h2_second).astype(BF), r2)}
    h1_second, h3_first, h0_core = hop_second(*h1), hop_first(h3_keep, h3_core), to_core(h0_send)
    grad_tokens, small = call(
        partial(last_kernel, planes),
        "last",
        8,
        20,
        [(tokens, VMEM), (row(gain_attn), VMEM), (grad_mixed, VMEM), (sm1, VMEM)]
        + [(ds[r], VMEM) for r in range(planes)]
        + [(ws[r], VMEM) for r in range(planes)]
        + [(smalls[r], VMEM) for r in [0] + far],
        [(SDS((T, D), F32), HBM), (SDS((TAIL, D), F32), VMEM)],
        [VMEM((T, D), F32), VMEM((T, D), F32), sems(8)],
        after=[h2_second, h1_first],
    )

    steps = [1 << i for i in range(places.bit_length() - 1)]
    hop_small = lambda v, step: v + lax.ppermute(v, "dp", [(a, a ^ step) for a in range(places)])
    small, h1_second, h3_first, h0_core, heads_of[r2] = now(small, h1_second, h3_first, h0_core, heads_of[r2])
    h3, small = (h3_keep, h3_core, h3_first), hop_small(small, steps[0])
    h0_first, h3_second = hop_first(h0_keep, h0_core), hop_second(*h3)
    heads_of[r1] = to_plane(total(*h1, h1_second).astype(BF), r1)
    small, h0_first, h3_second, heads_of[r1] = now(small, h0_first, h3_second, heads_of[r1])
    h0, small = (h0_keep, h0_core, h0_first), hop_small(small, steps[1])
    h0_second = hop_second(*h0)
    heads_of[r3] = to_plane(total(*h3, h3_second).astype(BF), r3)
    for step in steps[2:]:
        small = hop_small(small, step)
    tails = {0: small, **{r: to_plane(small, r) for r in far}}
    heads_of[0] = total(*h0, h0_second)

    m = D // places
    units = units_of[0] + sum(f32(units_of[r]) for r in far)
    hd = heads_of[0] + sum(f32(heads_of[r]) for r in far)
    grad_w_up, grad_w_down = units[:m], units[m:].T
    grad_w_qkv = hd[:, : 3 * e].reshape(m, 3, e).transpose(1, 0, 2)
    grad_w_out = hd[:, 3 * e :].T

    seat = {r: i for i, r in enumerate([0] + far)}
    g_ga, g_sa, g_bo, g_gm, g_sm, g_bd = [sum(v[j] for v in tails.values()) for j in (0, 1, 6, 7, 8, 9)]
    bu = sum(tails[r][10 + seat[r]] for r in range(planes))
    qv = sum(tails[r][2 + seat[r]] for r in range(planes))
    slice_of = lambda v, at, size: lax.dynamic_slice_in_dim(v, at, size, v.ndim - 1)
    size = D // (places * planes)
    vecs = [slice_of(v, (d * planes + z) * size, size) for v in (g_ga, g_sa, g_bo, g_gm, g_sm, g_bd)]
    grad_bias_up = slice_of(bu, d * (H // places), H // places)
    qv = jnp.stack([qv[:e], qv[256 : 256 + e]])
    grad_bias_qv = slice_of(qv, d * (e // places), e // places)
    return (
        result,
        grad_tokens,
        vecs[0],
        vecs[1],
        grad_w_qkv,
        grad_bias_qv,
        grad_w_out,
        vecs[2],
        vecs[3],
        vecs[4],
        grad_w_up,
        grad_bias_up,
        grad_w_down,
        vecs[5],
    )


def solution(mesh):
    return jax.shard_map(
        partial(on_device, mesh.shape["dp"], mesh.shape["mp"]),
        mesh=mesh,
        in_specs=(
            P(("dp", "mp"), None),
            P("dp", None),
            P(),
            P(),
            P(None, None, "mp"),
            P(None, "mp"),
            P("mp", None),
            P(),
            P(),
            P(),
            P(None, "mp"),
            P("mp"),
            P("mp", None),
            P(),
            P(("dp", "mp"), None),
        ),
        out_specs=(
            P(("dp", "mp"), None),
            P(("dp", "mp"), None),
            P(("dp", "mp")),
            P(("dp", "mp")),
            P(None, "dp", "mp"),
            P(None, ("mp", "dp")),
            P("mp", "dp"),
            P(("dp", "mp")),
            P(("dp", "mp")),
            P(("dp", "mp")),
            P("dp", "mp"),
            P(("mp", "dp")),
            P("mp", "dp"),
            P(("dp", "mp")),
        ),
        check_vma=False,
    )
```

```python
from functools import partial

import jax
import jax.numpy as jnp
import numpy as np
from jax import lax
from jax.experimental import pallas as pl
from jax.experimental.pallas import tpu as pltpu
from jax.sharding import PartitionSpec as P

F32, BF = jnp.float32, jnp.bfloat16
HEAD_DIM = 64
MOST = 256
EPSILON = 1e-06
MASKED = -1e30
LOG2E = 1.4426950408889634
ROOT_HALF = 0.7071067811865476
RSQRT_2PI = 0.3989422804014327
PARTS = 8
KEY_BLOCK = 128
TAIL = 16
GATHERED, EXCHANGED, PLACE = 8, 16, 24
VMEM, SMEM, HBM = pltpu.VMEM, pltpu.SMEM, pltpu.HBM
LANES = 128
SDS = jax.ShapeDtypeStruct


def _dot(a, b, i, j):
    return lax.dot_general(a, b, (((i,), (j,)), ((), ())), preferred_element_type=F32)


def nn(a, b):
    return _dot(a, b, 1, 0)


def nt(a, b):
    return _dot(a, b, 1, 1)


def tn(a, b):
    return _dot(a, b, 0, 0)


def tt(a, b):
    return _dot(a, b, 0, 1)


def call(body, name, us, megabytes, ins, outs, scratch, after=()):
    count, skip = len(ins), len(ins) + len(after)

    def kernel(*refs):
        body(*refs[:count], *refs[skip:])

    pinned = lambda o, m: HBM(o.shape, o.dtype) if m is HBM else o
    there = lambda a, m: pltpu.with_memory_space_constraint(a, HBM) if m is HBM else a
    return pl.pallas_call(
        kernel,
        out_shape=tuple(pinned(*o) for o in outs),
        in_specs=[pl.BlockSpec(memory_space=m) for _, m in ins] + [pl.BlockSpec(memory_space=pl.ANY)] * len(after),
        out_specs=tuple(pl.BlockSpec(memory_space=m) for _, m in outs),
        scratch_shapes=scratch,
        compiler_params=pltpu.CompilerParams(vmem_limit_bytes=megabytes << 20),
        cost_estimate=pl.CostEstimate(flops=int(us * 1.0e9), bytes_accessed=1 << 20, transcendentals=0),
        name=name,
    )(*(there(*a) for a in ins), *after)


class Mover:
    def __init__(self, sems):
        self.sems, self.used = sems, 0

    def __call__(self, src, dst):
        c = pltpu.make_async_copy(src, dst, self.sems.at[self.used])
        self.used += 1
        c.start()
        return c


def wait(*copies):
    for c in copies:
        c.wait()


def windows(slots, width=256):
    out = []
    for q0 in range(0, slots, width):
        qn = min(width, slots - q0)
        lo = max(0, (q0 - MOST + 1) // 128 * 128)
        hi = min(slots, -(-(q0 + qn + MOST - 1) // 128) * 128)
        out.append((q0, qn, lo, hi - lo))
    return out


def segments(info, clips, shape, axis):
    place = lax.broadcasted_iota(jnp.int32, shape, axis)
    seg = jnp.zeros(shape, jnp.int32)
    for c in range(clips):
        seg = seg + jnp.where(place >= info[c], 1, 0)
    return jnp.where(seg == clips - 1, place + clips, seg)


def fill_mask(bias_sc, segc, segr, q0, qn, k0, w):
    for b in range(0, w, KEY_BLOCK):
        same = segc[k0 + b : k0 + b + KEY_BLOCK, :] == segr[:, q0 : q0 + qn]
        bias_sc[b : b + KEY_BLOCK, :qn] = jnp.where(same, 0.0, MASKED)


def fold(x, f):
    return f(x.reshape(x.shape[0] // 8, 8, x.shape[1]), axis=0)


def attend(tl, heads, scale, qkvT, kn, segc, segr, oT, lse, bias_sc, s_sc, p_sc):
    e, hd = heads * HEAD_DIM, HEAD_DIM
    for q0, qn, k0, w in tl:
        fill_mask(bias_sc, segc, segr, q0, qn, k0, w)
        for h in range(heads):
            q = qkvT[h * hd : (h + 1) * hd, q0 : q0 + qn]
            m = None
            for b in range(0, w, KEY_BLOCK):
                s = nn(kn[h, k0 + b : k0 + b + KEY_BLOCK, :], q) * scale + bias_sc[b : b + KEY_BLOCK, :qn]
                s_sc[b : b + KEY_BLOCK, :qn] = s
                mb = fold(s, jnp.max)
                m = mb if m is None else jnp.maximum(m, mb)
            m = jnp.max(m, axis=0, keepdims=True)
            total = None
            for b in range(0, w, KEY_BLOCK):
                p = jnp.exp2(s_sc[b : b + KEY_BLOCK, :qn] - m)
                p_sc[b : b + KEY_BLOCK, :qn] = p.astype(BF)
                lb = fold(p, jnp.sum)
                total = lb if total is None else total + lb
            total = jnp.sum(total, axis=0, keepdims=True)
            o = nn(qkvT[2 * e + h * hd : 2 * e + (h + 1) * hd, k0 : k0 + w], p_sc[:w, :qn])
            oT[h * hd : (h + 1) * hd, q0 : q0 + qn] = (o * (1.0 / total)).astype(BF)
            lse[h : h + 1, q0 : q0 + qn] = m + jnp.log2(total)


def unit(x):
    y = x - jnp.mean(x, axis=1, keepdims=True)
    inverse = lax.rsqrt(jnp.mean(y * y, axis=1, keepdims=True) + EPSILON)
    return y * inverse, inverse


def unit_back(up, n, inverse, gain):
    g = up * gain
    return inverse * (g - jnp.mean(g, axis=1, keepdims=True) - n * jnp.mean(g * n, axis=1, keepdims=True))


def normal(u):
    bell = jnp.exp2(u * u * (-0.5 * LOG2E))
    d = jnp.abs(u) * (0.3275911 * ROOT_HALF) + 1.0
    t = pl.reciprocal(d, approx=True)
    t = t * (2.0 - d * t)
    q = 0.5 * 1.061405429
    for c in (-1.453152027, 1.421413741, -0.284496736, 0.254829592):
        q = q * t + 0.5 * c
    q = q * t * bell
    return jnp.where(u >= 0.0, 1.0 - q, q), bell * RSQRT_2PI


def blocks_out(move, info, source, place, keep, send):
    n, half = source.shape[0] // PARTS, PARTS // 2
    copies = []
    for j in range(PARTS):
        row = pl.ds(pl.multiple_of(info[EXCHANGED + j] * n, n), n)
        out = keep if j < half else send
        if move is None:
            out[j % half, place : place + n, :] = source[row, :]
        else:
            copies.append(move(source.at[row], out.at[j % half, pl.ds(place, n)]))
    return copies


def cut_kernel(info, w_heads, w_out, w_up, w_down, bias_qv, bias_up, piece, units, up, down, tail_s, sems):
    e, H = w_out.shape[0], bias_up.shape[1]
    n = units.shape[0] // 2
    move = Mover(sems)
    at = info[PLACE]
    row = pl.ds(pl.multiple_of(at * n, n), n)
    edge = w_heads.shape[0] // n
    loads = [move(w_up.at[row], units.at[pl.ds(0, n)]), move(w_down.at[row], units.at[pl.ds(n, n)])]
    loads += [move(w_up.at[row], up), move(w_down.at[row], down)]
    tail_s[...] = jnp.zeros_like(tail_s)
    tail_s[0:1, :H] = bias_up[...].astype(F32)
    for i in range(2):
        tail_s[1:2, 256 * i : 256 * i + e] = bias_qv[i : i + 1, :].astype(F32)
    piece[pl.ds(n, TAIL), :] = tail_s[...].astype(BF)

    @pl.when(at < edge)
    def _():
        src = w_heads.at[pl.ds(pl.multiple_of(jnp.minimum(at, edge - 1) * n, n), n)]
        wait(move(src, piece.at[pl.ds(0, n)]))

    @pl.when(at >= edge)
    def _():
        src = w_out.at[pl.ds(pl.multiple_of(jnp.maximum(at - edge, 0) * n, n), n)]
        wait(move(src, piece.at[pl.ds(0, n)]))

    wait(*loads)


def project(heads, n1, w, piece, qkvT):
    e = heads * HEAD_DIM
    n = piece.shape[0] - TAIL
    biases = piece[n : n + TAIL, :512].astype(F32)[1:2, :]
    for c in range(3):
        t = nt(w[c * e : (c + 1) * e, :], n1[...])
        if c != 1:
            at = 128 * c
            t = t + jnp.broadcast_to(biases[:, at : at + 256], (LANES, 256)).T[:e, :1]
        qkvT[c * e : (c + 1) * e, :] = t.astype(BF)


def attend_kernel(clips, tl, heads, scale, info, qkvT, oT, lse, kn, bias_sc, s_sc, p_sc):
    slots = qkvT.shape[1]
    segc = segments(info, clips, (slots, 1), 0)
    segr = segments(info, clips, (1, slots), 1)
    e = heads * HEAD_DIM
    for h in range(heads):
        kn[h] = qkvT[e + h * HEAD_DIM : e + (h + 1) * HEAD_DIM, :].T
    attend(tl, heads, scale, qkvT, kn, segc, segr, oT, lse, bias_sc, s_sc, p_sc)


def first_kernel(heads, x, gain, shift, w, piece, n1, qkvT):
    for i in range(0, x.shape[0], LANES):
        n, _ = unit(x[i : i + LANES, :].astype(F32))
        n1[i : i + LANES, :] = (n * gain[...].astype(F32) + shift[...].astype(F32)).astype(BF)
    project(heads, n1, w, piece, qkvT)


def attn_kernel(clips, tl, heads, scale, info, n1, piece, p4, r4, w, qkvT, oT, lse, *scratch):
    n = w.shape[0] // PARTS
    for i in range(PARTS):
        ref = (p4, r4)[i // 4]
        w[pl.ds(pl.multiple_of(info[GATHERED + i] * n, n), n), :] = ref[i % 4 * n : (i % 4 + 1) * n, :]
    project(heads, n1, w, piece, qkvT)
    attend_kernel(clips, tl, heads, scale, info, qkvT, oT, lse, *scratch)


def chunk_front(n2, cot, wup, wdn, piece, hid, gp, gb):
    n = piece.shape[0] - TAIL
    u = nn(n2[...], wup[...]) + piece[n : n + TAIL, :].astype(F32)[0:1, : wup.shape[1]]
    ga = nt(cot[...], wdn[...])
    dist, dens = normal(u)
    hid[...] = (u * dist).astype(BF)
    g = (ga * (dist + u * dens)).astype(BF)
    gp[...] = g
    gb[...] = jnp.sum(g.astype(F32), axis=0, keepdims=True)


def chunk_sums(hid, gp, wup, wdn, out_acc, g_acc, fresh):
    o = nn(hid[...], wdn[...])
    out_acc[...] = o if fresh else out_acc[...] + o
    g = nt(gp[...], wup[...])
    g_acc[...] = g if fresh else g_acc[...] + g


def chunk_grads(move, info, n2, cot, hid, gp, up_sc, dn_sc, k, keep, send):
    n = n2.shape[1] // PARTS
    dn_sc[...] = tn(cot[...], hid[...]).astype(BF)
    copies = blocks_out(move, info, dn_sc, (2 * k + 1) * n, keep, send)
    up_sc[...] = tn(n2[...], gp[...]).astype(BF)
    return copies + blocks_out(move, info, up_sc, 2 * k * n, keep, send)


def mid_kernel(x, bias_out, gain, shift, *refs):
    count = (len(refs) - 6) // 2
    o, w, refs = refs[:count], refs[count : 2 * count], refs[2 * count :]
    mixed, n2, o_s, wo_s, mixed_s, sems = refs
    e = o[0].shape[0]
    move = Mover(sems)
    for r in range(count):
        o_s[r * e : (r + 1) * e, :] = o[r][...]
        wo_s[r * e : (r + 1) * e, :] = w[r][w[r].shape[0] - e :, :]
    mixed_s[...] = tn(o_s[...], wo_s[...])
    done = []
    for i in range(0, x.shape[0], LANES):
        k = slice(i, i + LANES)
        m = mixed_s[k, :] + x[k, :].astype(F32) + bias_out[...].astype(F32)
        mixed_s[k, :] = m
        done.append(move(mixed_s.at[pl.ds(i, LANES)], mixed.at[pl.ds(i, LANES)]))
        n, _ = unit(m)
        n2[k, :] = (n * gain[...].astype(F32) + shift[...].astype(F32)).astype(BF)
    wait(*done)


def own_kernel(info, n2, cot, piece, wup, wdn, out, g, keep, send, gb, out_s, g_s, hid, gp, up_sc, dn_sc, sems):
    move = Mover(sems)
    chunk_front(n2, cot, wup, wdn, piece, hid, gp, gb)
    chunk_sums(hid, gp, wup, wdn, out_s, g_s, True)
    done = [move(out_s, out), move(g_s, g)]
    wait(*chunk_grads(move, info, n2, cot, hid, gp, up_sc, dn_sc, 0, keep, send), *done)


def units_here(info, p4, r4, wup, wdn, k, count):
    n = wup.shape[0] // PARTS
    for i in range(PARTS):
        ref, at = (p4, r4)[i // 4], (i % 4 * count + k) * 2 * n
        row = pl.ds(pl.multiple_of(info[GATHERED + i] * n, n), n)
        wup[row, :] = ref[at : at + n, :]
        wdn[row, :] = ref[at + n : at + 2 * n, :]


def mlp_kernel(count, info, n2, cot, out_in, g_in, p4, r4, *refs):
    piece, refs = refs[:count], refs[count:]
    out, g, keep, send, gb, out_s, g_s, hid, gp, up_sc, dn_sc, wup, wdn, sems = refs
    move = Mover(sems)
    sums = [move(out_in, out_s), move(g_in, g_s)]
    done = []
    for k in range(count):
        units_here(info, p4, r4, wup, wdn, k, count)
        chunk_front(n2, cot, wup, wdn, piece[k], hid, gp, gb.at[pl.ds(k, 1)])
        if k == 0:
            wait(*sums)
        chunk_sums(hid, gp, wup, wdn, out_s, g_s, False)
        wait(*done)
        done = []
        if k == count - 1:
            done = [move(out_s, out), move(g_s, g)]
        done += chunk_grads(move, info, n2, cot, hid, gp, up_sc, dn_sc, k, keep, send)
    wait(*done)


def mlp_last_kernel(info, n2, cot, out_in, g_in, p4, r4, piece, mixed, bias_down, gain, *refs):
    gbs, refs = refs[: len(refs) - 17], refs[len(refs) - 17 :]
    result, grad_mixed, branch, keep, send, sm = refs[:6]
    out_s, g_s, hid, gp, up_sc, dn_sc, wup, wdn, mixed_s, result_s, sems = refs[6:]
    move = Mover(sems)
    sums = [move(out_in, out_s), move(g_in, g_s), move(mixed, mixed_s)]
    units_here(info, p4, r4, wup, wdn, 0, 1)
    chunk_front(n2, cot, wup, wdn, piece, hid, gp, sm.at[pl.ds(7, 1)])
    wait(*sums)
    chunk_sums(hid, gp, wup, wdn, out_s, g_s, False)
    vecs = [0.0] * 4
    for i in range(0, n2.shape[0], LANES):
        k = slice(i, i + LANES)
        up, mid, c = g_s[k, :], mixed_s[k, :], cot[k, :].astype(F32)
        result_s[k, :] = (mid + out_s[k, :] + bias_down[...].astype(F32)).astype(BF)
        m, inverse = unit(mid)
        gm = c + unit_back(up, m, inverse, gain[...].astype(F32))
        mixed_s[k, :] = gm
        branch[k, :] = gm.astype(BF)
        for j, v in enumerate((gm, up * m, up, c)):
            vecs[j] = vecs[j] + fold(v, jnp.sum)
    done = [move(mixed_s, grad_mixed), move(result_s, result)]
    for j in range(4):
        sm[j : j + 1, :] = jnp.sum(vecs[j], axis=0, keepdims=True)
    at = 4
    for ref in gbs:
        sm[at : at + ref.shape[0], :] = ref[...]
        at += ref.shape[0]
    done += chunk_grads(move, info, n2, cot, hid, gp, up_sc, dn_sc, 0, keep, send)
    wait(*done)


def back_heads(clips, tl, heads, scale, part, info, gb, w, q_s, oT, lse, d_s, scratch):
    kn, vn, ga, bias_sc, pb_sc, ds_sc, dk, dv = scratch
    e, hd = heads * HEAD_DIM, HEAD_DIM
    slots = gb.shape[0]
    segc = segments(info, clips, (slots, 1), 0)
    segr = segments(info, clips, (1, slots), 1)
    ga[...] = nt(w[w.shape[0] - e :, :], gb[...]).astype(BF)
    for h in range(heads):
        kn[h] = q_s[e + h * hd : e + (h + 1) * hd, :].T
        vn[h] = q_s[2 * e + h * hd : 2 * e + (h + 1) * hd, :].T
    dk[...] = jnp.zeros_like(dk)
    dv[...] = jnp.zeros_like(dv)
    for q0, qn, k0, wide in tl:
        fill_mask(bias_sc, segc, segr, q0, qn, k0, wide)
        for h in range(heads):
            hs = slice(h * hd, (h + 1) * hd)
            q, go = q_s[hs, q0 : q0 + qn], ga[hs, q0 : q0 + qn]
            total = lse[h : h + 1, q0 : q0 + qn]
            centre = jnp.sum(go.astype(F32) * oT[hs, q0 : q0 + qn].astype(F32), axis=0, keepdims=True)
            for b in range(0, wide, KEY_BLOCK):
                k, v = slice(b, b + KEY_BLOCK), slice(k0 + b, k0 + b + KEY_BLOCK)
                p = jnp.exp2(nn(kn[h, v, :], q) * scale + bias_sc[k, :qn] - total)
                pb_sc[k, :qn] = p.astype(BF)
                ds_sc[k, :qn] = (p * (nn(vn[h, v, :], go) - centre)).astype(BF)
            ds = ds_sc[:wide, :qn]
            d_s[hs, q0 : q0 + qn] = (nn(q_s[e + h * hd : e + (h + 1) * hd, k0 : k0 + wide], ds) * part).astype(BF)
            dk[hs, k0 : k0 + wide] += nt(q, ds)
            dv[hs, k0 : k0 + wide] += nt(go, pb_sc[:wide, :qn])
    d_s[e : 2 * e, :] = (dk[...] * part).astype(BF)
    d_s[2 * e : 3 * e, :] = dv[...].astype(BF)


def bias_rows(d_s, small, at, e):
    rows = nt(jnp.ones((8, d_s.shape[1]), BF), d_s[...])
    small[at : at + 1, 0:e] = rows[0:1, 0:e]
    small[at : at + 1, 256 : 256 + e] = rows[0:1, 2 * e : 3 * e]


def head_grads(move, info, gb, n1, oT, d_s, acc, keep, send):
    k = d_s.shape[0]
    acc[:, :k] = tt(n1[...], d_s[...]).astype(BF)
    acc[:, k:] = tt(gb[...], oT[...]).astype(BF)
    return blocks_out(move, info, acc, 0, keep, send)


def back_kernel(clips, tl, heads, scale, part, info, gb, n1, q, w, oT, lse, d, keep, send, small, acc, *scratch):
    small[...] = jnp.zeros_like(small)
    back_heads(clips, tl, heads, scale, part, info, gb, w, q, oT, lse, d, scratch)
    bias_rows(d, small, 0, heads * HEAD_DIM)
    head_grads(None, info, gb, n1, oT, d, acc, keep, send)


def last_kernel(planes, x, gain, grad_mixed, sm1, *refs):
    d, w, smalls = refs[:planes], refs[planes : 2 * planes], refs[2 * planes : 3 * planes]
    grad_tokens, sm, g_sc, gm_s, sems = refs[3 * planes :]
    rows = d[0].shape[0]
    move = Mover(sems)
    for r in range(planes):
        g = tn(d[r][...], w[r][:rows, :])
        g_sc[...] = g if r == 0 else g_sc[...] + g
    vecs, done = [0.0] * 2, []
    for i in range(0, x.shape[0], LANES):
        k = slice(i, i + LANES)
        up = g_sc[k, :]
        m, inverse = unit(x[k, :].astype(F32))
        gm_s[k, :] = grad_mixed[k, :] + unit_back(up, m, inverse, gain[...].astype(F32))
        done.append(move(gm_s.at[pl.ds(i, LANES)], grad_tokens.at[pl.ds(i, LANES)]))
        for j, v in enumerate((up * m, up)):
            vecs[j] = vecs[j] + fold(v, jnp.sum)
    sm[...] = jnp.zeros_like(sm)
    for j in range(2):
        sm[j : j + 1, :] = jnp.sum(vecs[j], axis=0, keepdims=True)
    for r in range(planes):
        sm[2 + r : 3 + r, :512] = smalls[r][...]
    sm[6:14, :] = sm1[...]
    wait(*done)


def on_device(
    places,
    planes,
    tokens,
    clip_lengths,
    gain_attn,
    shift_attn,
    w_qkv,
    bias_qv,
    w_out,
    bias_out,
    gain_mlp,
    shift_mlp,
    w_up,
    bias_up,
    w_down,
    bias_down,
    cotangent,
):
    T, D = tokens.shape
    clips = clip_lengths.shape[1]
    e = w_out.shape[0]
    heads = e // HEAD_DIM
    H = w_up.shape[1]
    n = D // PARTS
    rest = places // PARTS
    d, z = lax.axis_index("dp"), lax.axis_index("mp")
    hi = d // rest
    f32 = lambda v: v.astype(F32)
    row = lambda v: v.reshape(1, -1)

    core = hi % 2
    first, second = jnp.where(core == 0, 2, 4), jnp.where(core == 0, 4, 2)
    both = lambda a, f, s: [a, a ^ f, a ^ s, a ^ 6]
    order = lambda a, f, s: [a, a ^ s, a ^ f, a ^ 6]
    gathered = both(hi, first, second) + both(hi ^ 1, second, first)
    exchanged = order(hi, first, second) + order(hi ^ 1, second, first)
    ends = jnp.cumsum(lax.dynamic_index_in_dim(clip_lengths, z, 0, keepdims=False))
    ends = jnp.concatenate([ends, jnp.zeros((GATHERED - clips,), jnp.int32)])
    info = jnp.concatenate([ends, jnp.stack(gathered + exchanged + [hi]).astype(jnp.int32)])

    def over_plane(v, flip):
        to = lambda a: ((a // rest) ^ flip((a // rest) % 2)) * rest + a % rest
        return lax.ppermute(v, "dp", [(a, to(a)) for a in range(places)])

    to_core = lambda v: over_plane(v, lambda c: 1)
    to_first = lambda v: over_plane(v, lambda c: 4 if c else 2)
    to_second = lambda v: over_plane(v, lambda c: 2 if c else 4)
    to_both = lambda v: over_plane(v, lambda c: 6)
    shift = lambda v, r: lax.ppermute(v, "mp", [(a, (a + r) % planes) for a in range(planes)])
    from_plane = lambda v, r: shift(v, -r)
    to_plane = shift

    def now(*arrays):
        return lax.optimization_barrier(arrays)

    near, last_far = [1, 3], 2
    far = near + [last_far]

    sems = lambda k: pltpu.SemaphoreType.DMA((k,))
    w_heads = w_qkv.transpose(0, 2, 1).reshape(3 * e, D)
    piece, unit_piece, *unit_halves = call(
        cut_kernel,
        "cut",
        2,
        16,
        [(info, SMEM), (w_heads, HBM), (w_out, HBM), (w_up, HBM), (w_down, HBM), (bias_qv, VMEM), (row(bias_up), VMEM)],
        [(SDS((n + TAIL, D), BF), VMEM), (SDS((2 * n, D), BF), VMEM)]
        + [(SDS((n, D), BF), VMEM)] * 2,
        [VMEM((TAIL, D), F32), sems(8)],
    )
    pieces = {0: piece, **{r: from_plane(piece, r) for r in far}}

    tl = windows(T)
    wm, qm = max(t[3] for t in tl), max(t[1] for t in tl)
    scale = HEAD_DIM**-0.5 * LOG2E
    attn_out = [(SDS((3 * e, T), BF), VMEM), (SDS((e, T), BF), VMEM), (SDS((8, T), F32), VMEM)]
    attn_sc = [VMEM((heads, T, HEAD_DIM), BF), VMEM((wm, qm), F32), VMEM((wm, qm), F32), VMEM((wm, qm), BF)]
    n1, q0 = call(
        partial(first_kernel, heads),
        "first",
        4,
        20,
        [(tokens, VMEM), (row(gain_attn), VMEM), (row(shift_attn), VMEM), (w_heads, VMEM), (piece, VMEM)],
        [(SDS((T, D), BF), VMEM), attn_out[0]],
        [],
    )
    ws, qs, os, ls = {0: w_out}, {0: q0}, {}, {}

    def join(*v):
        return jnp.concatenate(v)

    def attn(r, c4, r4, after, us=7):
        ws[r], qs[r], os[r], ls[r] = call(
            partial(attn_kernel, clips, tl, heads, scale),
            f"attn{r}",
            us,
            24,
            [(info, SMEM), (n1, VMEM), (pieces[r], VMEM), (c4, VMEM), (r4, VMEM)],
            [(SDS((4 * e, D), BF), VMEM)] + attn_out,
            attn_sc,
            after=after,
        )
        return ls[r]

    a1, a3, a2 = far
    q0, p1, p3 = now(q0, pieces[a1], pieces[a3])
    got1 = [p1, to_first(p1), to_second(p1), to_both(p1)]
    f3 = to_first(p3)
    os[0], ls[0] = call(
        partial(attend_kernel, clips, tl, heads, scale),
        "attend0",
        4,
        20,
        [(info, SMEM), (q0, VMEM)],
        attn_out[1:],
        attn_sc,
    )
    _, p3, f3, p2, *got1 = now(ls[0], p3, f3, pieces[a2], *got1)
    c1, c3 = join(*(v[:n] for v in got1)), join(p3[:n], f3[:n])
    core1, s3, f2 = to_core(c1), to_second(c3), to_first(p2)
    near_piece = now(unit_piece, c1)[0]
    near_z = [from_plane(near_piece, r) for r in near]
    t = attn(a1, c1, core1, [])
    _, s3, f2, *near_z = now(t, s3, f2, *near_z)
    c3, c2, near_b = join(c3, s3), join(p2[:n], f2[:n]), join(*near_z)
    core3, s2, near_f = to_core(c3), to_second(c2), to_first(near_b)
    far_up = from_plane(now(unit_halves[0], near_b)[0], last_far)
    t = attn(a3, c3, core3, [c2, near_b])
    _, s2, near_f, far_up = now(t, s2, near_f, far_up)
    far_down = from_plane(now(unit_halves[1], far_up)[0], last_far)
    c2, near_b = join(c2, s2), join(near_b, near_f)
    core2, near_s = to_core(c2), to_second(near_b)
    t = attn(a2, c2, core2, [near_b])
    far_b = join(far_up, now(t, far_down)[1])
    far_f = to_first(far_b)

    def block(i, keep, core, first):
        return f32(keep[i]) + f32(core[i]) + f32(first[i])

    def hop_first(*had):
        half = PARTS // 4
        return apart(to_first, [(f32(keep[half:]) + f32(core[half:])).astype(BF) for keep, core in had], 1)

    def hop_second(*had):
        return apart(to_second, [block(1, *v).astype(BF) for v in had], 0)

    def apart(hop, v, axis):
        if len(v) == 1:
            return [hop(v[0])]
        return jnp.split(hop(jnp.concatenate(v, axis)), np.cumsum([a.shape[axis] for a in v])[:-1], axis)

    def total(keep, core, first, second):
        k = block(0, keep, core, first) + f32(second)
        if rest > 1:
            groups = [[a * rest + b for b in range(rest)] for a in range(PARTS)]
            k = k.reshape(-1, n, k.shape[-1])
            k = lax.psum_scatter(k, "dp", scatter_dimension=1, axis_index_groups=groups, tiled=True)
            k = k.reshape(-1, k.shape[-1])
        return k

    half = PARTS // 2
    acts = [VMEM((T, D), F32)] * 2 + [VMEM((T, H), BF)] * 2 + [VMEM((D, H), BF)] * 2
    weights = [VMEM((D, H), BF), VMEM((H, D), BF)]
    grads = lambda k: [(SDS((half, k * 2 * n, H), BF), HBM)] * 2
    sums = [(SDS((T, D), F32), HBM)] * 2
    mixed, n2 = call(
        mid_kernel,
        "mid",
        6,
        24,
        [(tokens, VMEM), (row(bias_out), VMEM), (row(gain_mlp), VMEM), (row(shift_mlp), VMEM)]
        + [(os[r], VMEM) for r in range(planes)]
        + [(ws[r], VMEM) for r in range(planes)],
        [(SDS((T, D), F32), HBM), (SDS((T, D), BF), VMEM)],
        [VMEM((planes * e, T), BF), VMEM((planes * e, D), BF), VMEM((T, D), F32), sems(8)],
        after=[far_b],
    )
    n2, near_s, far_f = now(n2, near_s, far_f)
    near_b, far_b = join(near_b, near_s), join(far_b, far_f)
    near_r, far_s = to_core(near_b), to_second(far_b)
    out_acc, g_acc, u0_keep, u0_send, gb0 = call(
        own_kernel,
        "own",
        12,
        40,
        [(info, SMEM), (n2, VMEM), (cotangent, VMEM), (piece, VMEM), (w_up, VMEM), (w_down, VMEM)],
        sums + grads(1) + [(SDS((1, H), F32), VMEM)],
        acts + [sems(24)],
        after=[near_b, far_b],
    )
    gb0, near_r, far_s = now(gb0, near_r, far_s)
    far_b = join(far_b, far_s)
    far_r, u0_core = to_core(far_b), to_core(u0_send)
    k = len(near)
    out_acc, g_acc, u13_keep, u13_send, gb13 = call(
        partial(mlp_kernel, k),
        "mlp",
        22,
        40,
        [(info, SMEM), (n2, VMEM), (cotangent, VMEM), (out_acc, HBM), (g_acc, HBM), (near_b, VMEM), (near_r, VMEM)]
        + [(pieces[r], VMEM) for r in near],
        sums + grads(k) + [(SDS((k, H), F32), VMEM)],
        acts + weights + [sems(40)],
        after=[far_b],
    )
    gb13, far_r, u0_core = now(gb13, far_r, u0_core)
    (u0_first,), u13_core = hop_first((u0_keep, u0_core)), to_core(u13_send)
    result, grad_mixed, branch, u2_keep, u2_send, sm1 = call(
        mlp_last_kernel,
        "mlplast",
        15,
        42,
        [(info, SMEM), (n2, VMEM), (cotangent, VMEM), (out_acc, HBM), (g_acc, HBM), (far_b, VMEM), (far_r, VMEM)]
        + [(pieces[last_far], VMEM), (mixed, HBM), (row(bias_down), VMEM), (row(gain_mlp), VMEM), (gb0, VMEM), (gb13, VMEM)],
        [(SDS((T, D), BF), HBM), (SDS((T, D), F32), HBM), (SDS((T, D), BF), VMEM)]
        + grads(1)
        + [(SDS((8, H), F32), VMEM)],
        acts + weights + [VMEM((T, D), F32), VMEM((T, D), BF), sems(32)],
    )

    back_sc = (
        [VMEM((heads, T, HEAD_DIM), BF)] * 2
        + [VMEM((e, T), BF)]
        + [VMEM((wm, qm), F32)]
        + [VMEM((wm, qm), BF)] * 2
        + [VMEM((e, T), F32)] * 2
    )
    spec = (clips, tl, heads, scale, HEAD_DIM**-0.5)
    ins = lambda r: [(v, VMEM) for v in (branch, n1, qs[r], ws[r], os[r], ls[r])]
    ds, smalls = {}, {}

    def back(r, after):
        ds[r], keep, send, smalls[r] = call(
            partial(back_kernel, *spec),
            f"back{r}",
            11,
            30,
            [(info, SMEM)] + ins(r),
            [(SDS((3 * e, T), BF), VMEM)] + [(SDS((half, n, 4 * e), BF), VMEM)] * 2 + [(SDS((1, 512), F32), VMEM)],
            [VMEM((D, 4 * e), BF)] + back_sc,
            after=after,
        )
        return keep, send

    r2, r1, r3 = last_far, *near
    sm1, u0_first, u13_core = now(sm1, u0_first, u13_core)
    u0 = u0_keep, u0_core, u0_first
    (u0_second,), (u13_first,), u2_core = hop_second(u0), hop_first((u13_keep, u13_core)), to_core(u2_send)
    h2_keep, h2_send = back(r2, [sm1])
    t, u0_second, u2_core = now(smalls[r2], u0_second, u2_core)
    (u2_first,), h2_core = hop_first((u2_keep, u2_core)), to_core(h2_send)
    h1_keep, h1_send = back(r1, [t])
    t, u13_first, u2_first, h2_core = now(smalls[r1], u13_first, u2_first, h2_core)
    u13, u2 = (u13_keep, u13_core, u13_first), (u2_keep, u2_core, u2_first)
    seconds, h1_core = hop_second(u13, u2), to_core(h1_send)
    units_of = {0: total(*u0, u0_second)}
    h3_keep, h3_send = back(r3, [t])
    t, h1_core, *seconds = now(smalls[r3], h1_core, *seconds)
    pair = total(*u13, seconds[0])
    rows = pair.shape[0] // len(near)
    for i, r in enumerate(near):
        units_of[r] = to_plane(pair[i * rows : (i + 1) * rows].astype(BF), r)
    units_of[r2] = to_plane(total(*u2, seconds[1]).astype(BF), r2)
    (h2_first, h1_first), h3_core = hop_first((h2_keep, h2_core), (h1_keep, h1_core)), to_core(h3_send)
    h0_keep, h0_send = back(0, [t])
    t, h2_first, h1_first, h3_core = now(smalls[0], h2_first, h1_first, h3_core)
    h2, h1 = (h2_keep, h2_core, h2_first), (h1_keep, h1_core, h1_first)
    seconds = hop_second(h2, h1)
    (h3_first,), h0_core = hop_first((h3_keep, h3_core)), to_core(h0_send)
    grad_tokens, small = call(
        partial(last_kernel, planes),
        "last",
        8,
        20,
        [(tokens, VMEM), (row(gain_attn), VMEM), (grad_mixed, VMEM), (sm1, VMEM)]
        + [(ds[r], VMEM) for r in range(planes)]
        + [(ws[r] if r else w_heads, VMEM) for r in range(planes)]
        + [(smalls[r], VMEM) for r in [0] + far],
        [(SDS((T, D), F32), HBM), (SDS((TAIL, D), F32), VMEM)],
        [VMEM((T, D), F32), VMEM((T, D), F32), sems(8)],
        after=[h2_first],
    )

    steps = [1 << i for i in range(places.bit_length() - 1)]
    hop_small = lambda v, step: v + lax.ppermute(v, "dp", [(a, a ^ step) for a in range(places)])
    small, h3_first, h0_core, *seconds = now(small, h3_first, h0_core, *seconds)
    h3, small = (h3_keep, h3_core, h3_first), hop_small(small, steps[0])
    (h0_first,), (h3_second,) = hop_first((h0_keep, h0_core)), hop_second(h3)
    heads_of = {r: to_plane(total(*h, v).astype(BF), r) for r, h, v in zip((r2, r1), (h2, h1), seconds)}
    small, h0_first, h3_second, *came = now(small, h0_first, h3_second, *(units_of[r] for r in far))
    units_of.update(zip(far, came))
    h0, small = (h0_keep, h0_core, h0_first), hop_small(small, steps[1])
    (h0_second,) = hop_second(h0)
    heads_of[r3] = to_plane(total(*h3, h3_second).astype(BF), r3)
    for step in steps[2:]:
        small = hop_small(small, step)
    tails = {0: small, **{r: to_plane(small, r) for r in far}}
    heads_of[0] = total(*h0, h0_second)

    m = D // places
    units = units_of[0] + sum(f32(units_of[r]) for r in far)
    hd = heads_of[0] + sum(f32(heads_of[r]) for r in far)
    grad_w_up, grad_w_down = units[:m], units[m:].T
    grad_w_qkv = hd[:, : 3 * e].reshape(m, 3, e).transpose(1, 0, 2)
    grad_w_out = hd[:, 3 * e :].T

    seat = {r: i for i, r in enumerate([0] + far)}
    g_ga, g_sa, g_bo, g_gm, g_sm, g_bd = [sum(v[j] for v in tails.values()) for j in (0, 1, 6, 7, 8, 9)]
    bu = sum(tails[r][10 + seat[r]] for r in range(planes))
    qv = sum(tails[r][2 + seat[r]] for r in range(planes))
    slice_of = lambda v, at, size: lax.dynamic_slice_in_dim(v, at, size, v.ndim - 1)
    size = D // (places * planes)
    vecs = [slice_of(v, (d * planes + z) * size, size) for v in (g_ga, g_sa, g_bo, g_gm, g_sm, g_bd)]
    grad_bias_up = slice_of(bu, d * (H // places), H // places)
    qv = jnp.stack([qv[:e], qv[256 : 256 + e]])
    grad_bias_qv = slice_of(qv, d * (e // places), e // places)
    return (
        result,
        grad_tokens,
        vecs[0],
        vecs[1],
        grad_w_qkv,
        grad_bias_qv,
        grad_w_out,
        vecs[2],
        vecs[3],
        vecs[4],
        grad_w_up,
        grad_bias_up,
        grad_w_down,
        vecs[5],
    )


def solution(mesh):
    return jax.shard_map(
        partial(on_device, mesh.shape["dp"], mesh.shape["mp"]),
        mesh=mesh,
        in_specs=(
            P(("dp", "mp"), None),
            P("dp", None),
            P(),
            P(),
            P(None, None, "mp"),
            P(None, "mp"),
            P("mp", None),
            P(),
            P(),
            P(),
            P(None, "mp"),
            P("mp"),
            P("mp", None),
            P(),
            P(("dp", "mp"), None),
        ),
        out_specs=(
            P(("dp", "mp"), None),
            P(("dp", "mp"), None),
            P(("dp", "mp")),
            P(("dp", "mp")),
            P(None, "dp", "mp"),
            P(None, ("mp", "dp")),
            P("mp", "dp"),
            P(("dp", "mp")),
            P(("dp", "mp")),
            P(("dp", "mp")),
            P("dp", "mp"),
            P(("mp", "dp")),
            P("mp", "dp"),
            P(("dp", "mp")),
        ),
        check_vma=False,
    )
```

```python
from functools import partial

import jax
import jax.numpy as jnp
import numpy as np
from jax import lax
from jax.experimental import pallas as pl
from jax.experimental.pallas import tpu as pltpu
from jax.sharding import PartitionSpec as P

F32, BF = jnp.float32, jnp.bfloat16
HEAD_DIM = 64
MOST = 256
EPSILON = 1e-06
MASKED = -1e30
LOG2E = 1.4426950408889634
ROOT_HALF = 0.7071067811865476
RSQRT_2PI = 0.3989422804014327
PARTS = 8
KEY_BLOCK = 128
TAIL = 16
GATHERED, EXCHANGED, PLACE = 8, 16, 24
VMEM, SMEM, HBM = pltpu.VMEM, pltpu.SMEM, pltpu.HBM
LANES = 128
SDS = jax.ShapeDtypeStruct


def _dot(a, b, i, j):
    return lax.dot_general(a, b, (((i,), (j,)), ((), ())), preferred_element_type=F32)


def nn(a, b):
    return _dot(a, b, 1, 0)


def nt(a, b):
    return _dot(a, b, 1, 1)


def tn(a, b):
    return _dot(a, b, 0, 0)


def tt(a, b):
    return _dot(a, b, 0, 1)


def call(body, name, us, megabytes, ins, outs, scratch, after=()):
    count, skip = len(ins), len(ins) + len(after)

    def kernel(*refs):
        body(*refs[:count], *refs[skip:])

    pinned = lambda o, m: HBM(o.shape, o.dtype) if m is HBM else o
    there = lambda a, m: pltpu.with_memory_space_constraint(a, HBM) if m is HBM else a
    return pl.pallas_call(
        kernel,
        out_shape=tuple(pinned(*o) for o in outs),
        in_specs=[pl.BlockSpec(memory_space=m) for _, m in ins] + [pl.BlockSpec(memory_space=pl.ANY)] * len(after),
        out_specs=tuple(pl.BlockSpec(memory_space=m) for _, m in outs),
        scratch_shapes=scratch,
        compiler_params=pltpu.CompilerParams(vmem_limit_bytes=megabytes << 20),
        cost_estimate=pl.CostEstimate(flops=int(us * 1.0e9), bytes_accessed=1 << 20, transcendentals=0),
        name=name,
    )(*(there(*a) for a in ins), *after)


class Mover:
    def __init__(self, sems):
        self.sems, self.used = sems, 0

    def __call__(self, src, dst):
        c = pltpu.make_async_copy(src, dst, self.sems.at[self.used])
        self.used += 1
        c.start()
        return c


def wait(*copies):
    for c in copies:
        c.wait()


def windows(slots, width=256):
    out = []
    for q0 in range(0, slots, width):
        qn = min(width, slots - q0)
        lo = max(0, (q0 - MOST + 1) // 128 * 128)
        hi = min(slots, -(-(q0 + qn + MOST - 1) // 128) * 128)
        out.append((q0, qn, lo, hi - lo))
    return out


def segments(info, clips, shape, axis):
    place = lax.broadcasted_iota(jnp.int32, shape, axis)
    seg = jnp.zeros(shape, jnp.int32)
    for c in range(clips):
        seg = seg + jnp.where(place >= info[c], 1, 0)
    return jnp.where(seg == clips - 1, place + clips, seg)


def fill_mask(bias_sc, segc, segr, q0, qn, k0, w):
    for b in range(0, w, KEY_BLOCK):
        same = segc[k0 + b : k0 + b + KEY_BLOCK, :] == segr[:, q0 : q0 + qn]
        bias_sc[b : b + KEY_BLOCK, :qn] = jnp.where(same, 0.0, MASKED)


def fold(x, f):
    return f(x.reshape(x.shape[0] // 8, 8, x.shape[1]), axis=0)


def attend(tl, heads, scale, qkvT, kn, segc, segr, oT, lse, bias_sc, s_sc, p_sc):
    e, hd = heads * HEAD_DIM, HEAD_DIM

    def scores(tile, h):
        q0, qn, k0, w = tl[tile]
        if h == 0:
            fill_mask(bias_sc.at[tile % 2], segc, segr, q0, qn, k0, w)
        q = qkvT[h * hd : (h + 1) * hd, q0 : q0 + qn]
        m = None
        for b in range(0, w, KEY_BLOCK):
            k = slice(b, b + KEY_BLOCK)
            s = nn(kn[h, k0 + b : k0 + b + KEY_BLOCK, :], q) * scale + bias_sc[tile % 2, k, :qn]
            s_sc[h, k, :qn] = s
            mb = fold(s, jnp.max)
            m = mb if m is None else jnp.maximum(m, mb)
        return jnp.max(m, axis=0, keepdims=True)

    def finish(tile, h, m):
        q0, qn, k0, w = tl[tile]
        total = None
        for b in range(0, w, KEY_BLOCK):
            p = jnp.exp2(s_sc[h, b : b + KEY_BLOCK, :qn] - m)
            p_sc[h, b : b + KEY_BLOCK, :qn] = p.astype(BF)
            lb = fold(p, jnp.sum)
            total = lb if total is None else total + lb
        total = jnp.sum(total, axis=0, keepdims=True)
        o = nn(qkvT[2 * e + h * hd : 2 * e + (h + 1) * hd, k0 : k0 + w], p_sc[h, :w, :qn])
        oT[h * hd : (h + 1) * hd, q0 : q0 + qn] = (o * (1.0 / total)).astype(BF)
        lse[h : h + 1, q0 : q0 + qn] = m + jnp.log2(total)

    steps = [(tile, h) for tile in range(len(tl)) for h in range(heads)]
    ahead = scores(*steps[0])
    for at, step in enumerate(steps):
        m = ahead
        if at + 1 < len(steps):
            ahead = scores(*steps[at + 1])
        finish(*step, m)


def unit(x):
    y = x - jnp.mean(x, axis=1, keepdims=True)
    inverse = lax.rsqrt(jnp.mean(y * y, axis=1, keepdims=True) + EPSILON)
    return y * inverse, inverse


def unit_back(up, n, inverse, gain):
    g = up * gain
    return inverse * (g - jnp.mean(g, axis=1, keepdims=True) - n * jnp.mean(g * n, axis=1, keepdims=True))


def normal(u):
    bell = jnp.exp2(u * u * (-0.5 * LOG2E))
    d = jnp.abs(u) * (0.3275911 * ROOT_HALF) + 1.0
    t = pl.reciprocal(d, approx=True)
    t = t * (2.0 - d * t)
    q = 0.5 * 1.061405429
    for c in (-1.453152027, 1.421413741, -0.284496736, 0.254829592):
        q = q * t + 0.5 * c
    q = q * t * bell
    return jnp.where(u >= 0.0, 1.0 - q, q), bell * RSQRT_2PI


def blocks_out(move, info, source, place, keep, send):
    n, half = source.shape[0] // PARTS, PARTS // 2
    copies = []
    for j in range(PARTS):
        row = pl.ds(pl.multiple_of(info[EXCHANGED + j] * n, n), n)
        out = keep if j < half else send
        if move is None:
            out[j % half, place : place + n, :] = source[row, :]
        else:
            copies.append(move(source.at[row], out.at[j % half, pl.ds(place, n)]))
    return copies


def cut_kernel(info, w_heads, w_out, w_up, w_down, bias_qv, bias_up, piece, units, tail_s, sems):
    e, H = w_out.shape[0], bias_up.shape[1]
    n = units.shape[0] // 2
    move = Mover(sems)
    at = info[PLACE]
    row = pl.ds(pl.multiple_of(at * n, n), n)
    edge = w_heads.shape[0] // n
    loads = [move(w_up.at[row], units.at[pl.ds(0, n)]), move(w_down.at[row], units.at[pl.ds(n, n)])]
    tail_s[...] = jnp.zeros_like(tail_s)
    tail_s[0:1, :H] = bias_up[...].astype(F32)
    for i in range(2):
        tail_s[1:2, 256 * i : 256 * i + e] = bias_qv[i : i + 1, :].astype(F32)
    piece[pl.ds(n, TAIL), :] = tail_s[...].astype(BF)

    @pl.when(at < edge)
    def _():
        src = w_heads.at[pl.ds(pl.multiple_of(jnp.minimum(at, edge - 1) * n, n), n)]
        wait(move(src, piece.at[pl.ds(0, n)]))

    @pl.when(at >= edge)
    def _():
        src = w_out.at[pl.ds(pl.multiple_of(jnp.maximum(at - edge, 0) * n, n), n)]
        wait(move(src, piece.at[pl.ds(0, n)]))

    wait(*loads)


def project(heads, n1, w, piece, qkvT):
    e = heads * HEAD_DIM
    n = piece.shape[0] - TAIL
    biases = piece[n : n + TAIL, :512].astype(F32)[1:2, :]
    for c in range(3):
        t = nt(w[c * e : (c + 1) * e, :], n1[...])
        if c != 1:
            at = 128 * c
            t = t + jnp.broadcast_to(biases[:, at : at + 256], (LANES, 256)).T[:e, :1]
        qkvT[c * e : (c + 1) * e, :] = t.astype(BF)


def attend_kernel(clips, tl, heads, scale, info, qkvT, oT, lse, kn, bias_sc, s_sc, p_sc):
    slots = qkvT.shape[1]
    segc = segments(info, clips, (slots, 1), 0)
    segr = segments(info, clips, (1, slots), 1)
    e = heads * HEAD_DIM
    for h in range(heads):
        kn[h] = qkvT[e + h * HEAD_DIM : e + (h + 1) * HEAD_DIM, :].T
    attend(tl, heads, scale, qkvT, kn, segc, segr, oT, lse, bias_sc, s_sc, p_sc)


def first_kernel(heads, x, gain, shift, w, piece, n1, qkvT):
    for i in range(0, x.shape[0], LANES):
        n, _ = unit(x[i : i + LANES, :].astype(F32))
        n1[i : i + LANES, :] = (n * gain[...].astype(F32) + shift[...].astype(F32)).astype(BF)
    project(heads, n1, w, piece, qkvT)


def attn_kernel(clips, tl, heads, scale, info, n1, piece, p4, r4, w, qkvT, oT, lse, *scratch):
    n = w.shape[0] // PARTS
    for i in range(PARTS):
        ref = (p4, r4)[i // 4]
        w[pl.ds(pl.multiple_of(info[GATHERED + i] * n, n), n), :] = ref[i % 4 * n : (i % 4 + 1) * n, :]
    project(heads, n1, w, piece, qkvT)
    attend_kernel(clips, tl, heads, scale, info, qkvT, oT, lse, *scratch)


def chunk_front(n2, cot, wup, wdn, piece, hid, gp, gb):
    n = piece.shape[0] - TAIL
    u = nn(n2[...], wup[...]) + piece[n : n + TAIL, :].astype(F32)[0:1, : wup.shape[1]]
    ga = nt(cot[...], wdn[...])
    dist, dens = normal(u)
    hid[...] = (u * dist).astype(BF)
    g = (ga * (dist + u * dens)).astype(BF)
    gp[...] = g
    gb[...] = jnp.sum(g.astype(F32), axis=0, keepdims=True)


def chunk_sums(hid, gp, wup, wdn, out_acc, g_acc, fresh):
    o = nn(hid[...], wdn[...])
    out_acc[...] = o if fresh else out_acc[...] + o
    g = nt(gp[...], wup[...])
    g_acc[...] = g if fresh else g_acc[...] + g


def chunk_grads(move, info, n2, cot, hid, gp, up_sc, dn_sc, k, keep, send):
    n = n2.shape[1] // PARTS
    dn_sc[...] = tn(cot[...], hid[...]).astype(BF)
    copies = blocks_out(move, info, dn_sc, (2 * k + 1) * n, keep, send)
    up_sc[...] = tn(n2[...], gp[...]).astype(BF)
    return copies + blocks_out(move, info, up_sc, 2 * k * n, keep, send)


def mid_kernel(x, bias_out, gain, shift, *refs):
    count = (len(refs) - 6) // 2
    o, w, refs = refs[:count], refs[count : 2 * count], refs[2 * count :]
    mixed, n2, o_s, wo_s, mixed_s, sems = refs
    e = o[0].shape[0]
    move = Mover(sems)
    for r in range(count):
        o_s[r * e : (r + 1) * e, :] = o[r][...]
        wo_s[r * e : (r + 1) * e, :] = w[r][w[r].shape[0] - e :, :]
    mixed_s[...] = tn(o_s[...], wo_s[...])
    done = []
    for i in range(0, x.shape[0], LANES):
        k = slice(i, i + LANES)
        m = mixed_s[k, :] + x[k, :].astype(F32) + bias_out[...].astype(F32)
        mixed_s[k, :] = m
        done.append(move(mixed_s.at[pl.ds(i, LANES)], mixed.at[pl.ds(i, LANES)]))
        n, _ = unit(m)
        n2[k, :] = (n * gain[...].astype(F32) + shift[...].astype(F32)).astype(BF)
    wait(*done)


def own_kernel(info, n2, cot, piece, wup, wdn, out, g, keep, send, gb, out_s, g_s, hid, gp, up_sc, dn_sc, sems):
    move = Mover(sems)
    chunk_front(n2, cot, wup, wdn, piece, hid, gp, gb)
    chunk_sums(hid, gp, wup, wdn, out_s, g_s, True)
    done = [move(out_s, out), move(g_s, g)]
    wait(*chunk_grads(move, info, n2, cot, hid, gp, up_sc, dn_sc, 0, keep, send), *done)


def units_here(info, p4, r4, wup, wdn, k, count):
    n = wup.shape[0] // PARTS
    for i in range(PARTS):
        ref, at = (p4, r4)[i // 4], (i % 4 * count + k) * 2 * n
        row = pl.ds(pl.multiple_of(info[GATHERED + i] * n, n), n)
        wup[row, :] = ref[at : at + n, :]
        wdn[row, :] = ref[at + n : at + 2 * n, :]


def mlp_kernel(count, info, n2, cot, out_in, g_in, p4, r4, *refs):
    piece, refs = refs[:count], refs[count:]
    out, g, keep, send, gb, out_s, g_s, hid, gp, up_sc, dn_sc, wup, wdn, sems = refs
    move = Mover(sems)
    sums = [move(out_in, out_s), move(g_in, g_s)]
    done = []
    for k in range(count):
        units_here(info, p4, r4, wup, wdn, k, count)
        chunk_front(n2, cot, wup, wdn, piece[k], hid, gp, gb.at[pl.ds(k, 1)])
        if k == 0:
            wait(*sums)
        chunk_sums(hid, gp, wup, wdn, out_s, g_s, False)
        wait(*done)
        done = []
        if k == count - 1:
            done = [move(out_s, out), move(g_s, g)]
        done += chunk_grads(move, info, n2, cot, hid, gp, up_sc, dn_sc, k, keep, send)
    wait(*done)


def mlp_last_kernel(info, n2, cot, out_in, g_in, p4, r4, piece, mixed, bias_down, gain, *refs):
    gbs, refs = refs[: len(refs) - 17], refs[len(refs) - 17 :]
    result, grad_mixed, branch, keep, send, sm = refs[:6]
    out_s, g_s, hid, gp, up_sc, dn_sc, wup, wdn, mixed_s, result_s, sems = refs[6:]
    move = Mover(sems)
    sums = [move(out_in, out_s), move(g_in, g_s), move(mixed, mixed_s)]
    units_here(info, p4, r4, wup, wdn, 0, 1)
    chunk_front(n2, cot, wup, wdn, piece, hid, gp, sm.at[pl.ds(7, 1)])
    wait(*sums)
    chunk_sums(hid, gp, wup, wdn, out_s, g_s, False)
    vecs = [0.0] * 4
    for i in range(0, n2.shape[0], LANES):
        k = slice(i, i + LANES)
        up, mid, c = g_s[k, :], mixed_s[k, :], cot[k, :].astype(F32)
        result_s[k, :] = (mid + out_s[k, :] + bias_down[...].astype(F32)).astype(BF)
        m, inverse = unit(mid)
        gm = c + unit_back(up, m, inverse, gain[...].astype(F32))
        mixed_s[k, :] = gm
        branch[k, :] = gm.astype(BF)
        for j, v in enumerate((gm, up * m, up, c)):
            vecs[j] = vecs[j] + fold(v, jnp.sum)
    done = [move(mixed_s, grad_mixed), move(result_s, result)]
    for j in range(4):
        sm[j : j + 1, :] = jnp.sum(vecs[j], axis=0, keepdims=True)
    at = 4
    for ref in gbs:
        sm[at : at + ref.shape[0], :] = ref[...]
        at += ref.shape[0]
    done += chunk_grads(move, info, n2, cot, hid, gp, up_sc, dn_sc, 0, keep, send)
    wait(*done)


def back_heads(clips, tl, heads, scale, part, info, gb, w, q_s, oT, lse, d_s, scratch):
    kn, vn, ga, bias_sc, pb_sc, ds_sc, dk, dv = scratch
    e, hd = heads * HEAD_DIM, HEAD_DIM
    slots = gb.shape[0]
    segc = segments(info, clips, (slots, 1), 0)
    segr = segments(info, clips, (1, slots), 1)
    ga[...] = nt(w[w.shape[0] - e :, :], gb[...]).astype(BF)
    for h in range(heads):
        kn[h] = q_s[e + h * hd : e + (h + 1) * hd, :].T
        vn[h] = q_s[2 * e + h * hd : 2 * e + (h + 1) * hd, :].T
    dk[...] = jnp.zeros_like(dk)
    dv[...] = jnp.zeros_like(dv)

    def scores(tile, h):
        q0, qn, k0, wide = tl[tile]
        if h == 0:
            fill_mask(bias_sc.at[tile % 2], segc, segr, q0, qn, k0, wide)
        hs = slice(h * hd, (h + 1) * hd)
        q, go = q_s[hs, q0 : q0 + qn], ga[hs, q0 : q0 + qn]
        total = lse[h : h + 1, q0 : q0 + qn]
        centre = jnp.sum(go.astype(F32) * oT[hs, q0 : q0 + qn].astype(F32), axis=0, keepdims=True)
        for b in range(0, wide, KEY_BLOCK):
            k, v = slice(b, b + KEY_BLOCK), slice(k0 + b, k0 + b + KEY_BLOCK)
            p = jnp.exp2(nn(kn[h, v, :], q) * scale + bias_sc[tile % 2, k, :qn] - total)
            pb_sc[h, k, :qn] = p.astype(BF)
            ds_sc[h, k, :qn] = (p * (nn(vn[h, v, :], go) - centre)).astype(BF)

    def finish(tile, h):
        q0, qn, k0, wide = tl[tile]
        hs = slice(h * hd, (h + 1) * hd)
        q, go = q_s[hs, q0 : q0 + qn], ga[hs, q0 : q0 + qn]
        ds = ds_sc[h, :wide, :qn]
        d_s[hs, q0 : q0 + qn] = (nn(q_s[e + h * hd : e + (h + 1) * hd, k0 : k0 + wide], ds) * part).astype(BF)
        dk[hs, k0 : k0 + wide] += nt(q, ds)
        dv[hs, k0 : k0 + wide] += nt(go, pb_sc[h, :wide, :qn])

    steps = [(tile, h) for tile in range(len(tl)) for h in range(heads)]
    scores(*steps[0])
    for at, step in enumerate(steps):
        if at + 1 < len(steps):
            scores(*steps[at + 1])
        finish(*step)
    d_s[e : 2 * e, :] = (dk[...] * part).astype(BF)
    d_s[2 * e : 3 * e, :] = dv[...].astype(BF)


def bias_rows(d_s, small, at, e):
    rows = nt(jnp.ones((8, d_s.shape[1]), BF), d_s[...])
    small[at : at + 1, 0:e] = rows[0:1, 0:e]
    small[at : at + 1, 256 : 256 + e] = rows[0:1, 2 * e : 3 * e]


def head_grads(move, info, gb, n1, oT, d_s, acc, keep, send):
    k = d_s.shape[0]
    acc[:, :k] = tt(n1[...], d_s[...]).astype(BF)
    acc[:, k:] = tt(gb[...], oT[...]).astype(BF)
    return blocks_out(move, info, acc, 0, keep, send)


def back_kernel(clips, tl, heads, scale, part, info, gb, n1, q, w, oT, lse, d, keep, send, small, acc, *scratch):
    small[...] = jnp.zeros_like(small)
    back_heads(clips, tl, heads, scale, part, info, gb, w, q, oT, lse, d, scratch)
    bias_rows(d, small, 0, heads * HEAD_DIM)
    head_grads(None, info, gb, n1, oT, d, acc, keep, send)


def last_kernel(planes, x, gain, grad_mixed, sm1, *refs):
    d, w, smalls = refs[:planes], refs[planes : 2 * planes], refs[2 * planes : 3 * planes]
    grad_tokens, sm, g_sc, gm_s, sems = refs[3 * planes :]
    rows = d[0].shape[0]
    move = Mover(sems)
    for r in range(planes):
        g = tn(d[r][...], w[r][:rows, :])
        g_sc[...] = g if r == 0 else g_sc[...] + g
    vecs, done = [0.0] * 2, []
    for i in range(0, x.shape[0], LANES):
        k = slice(i, i + LANES)
        up = g_sc[k, :]
        m, inverse = unit(x[k, :].astype(F32))
        gm_s[k, :] = grad_mixed[k, :] + unit_back(up, m, inverse, gain[...].astype(F32))
        done.append(move(gm_s.at[pl.ds(i, LANES)], grad_tokens.at[pl.ds(i, LANES)]))
        for j, v in enumerate((up * m, up)):
            vecs[j] = vecs[j] + fold(v, jnp.sum)
    sm[...] = jnp.zeros_like(sm)
    for j in range(2):
        sm[j : j + 1, :] = jnp.sum(vecs[j], axis=0, keepdims=True)
    for r in range(planes):
        sm[2 + r : 3 + r, :512] = smalls[r][...]
    sm[6:14, :] = sm1[...]
    wait(*done)


def cut_sums_kernel(seats, at, *refs):
    count = len(seats)
    tails, (g_ga, g_sa, g_bo, g_gm, g_sm, g_bd, g_bu, g_qv) = refs[:count], refs[count:]
    width = tails[0].shape[1]
    total = tails[0][...]
    for t in tails[1:]:
        total = total + t[...]
    bu = tails[0][10 + seats[0] : 11 + seats[0], :]
    qv = tails[0][2 + seats[0] : 3 + seats[0], :]
    for t, seat in zip(tails[1:], seats[1:]):
        bu = bu + t[10 + seat : 11 + seat, :]
        qv = qv + t[2 + seat : 3 + seat, :]
    shifted = lambda v, i: pltpu.roll(v, jnp.where(at[i] == 0, 0, width - at[i]), 1)
    vecs = shifted(total, 0)
    for j, ref in zip((0, 1, 6, 7, 8, 9), (g_ga, g_sa, g_bo, g_gm, g_sm, g_bd)):
        ref[...] = vecs[j, : ref.shape[0]]
    g_bu[...] = shifted(jnp.broadcast_to(bu, (8, width)), 1)[0, : g_bu.shape[0]]
    qv = shifted(jnp.broadcast_to(qv, (8, width)), 2)
    for i in range(2):
        g_qv[i : i + 1, :] = qv[0:1, 256 * i : 256 * i + g_qv.shape[1]]


def on_device(
    places,
    planes,
    tokens,
    clip_lengths,
    gain_attn,
    shift_attn,
    w_qkv,
    bias_qv,
    w_out,
    bias_out,
    gain_mlp,
    shift_mlp,
    w_up,
    bias_up,
    w_down,
    bias_down,
    cotangent,
):
    T, D = tokens.shape
    clips = clip_lengths.shape[1]
    e = w_out.shape[0]
    heads = e // HEAD_DIM
    H = w_up.shape[1]
    n = D // PARTS
    rest = places // PARTS
    d, z = lax.axis_index("dp"), lax.axis_index("mp")
    hi = d // rest
    f32 = lambda v: v.astype(F32)
    row = lambda v: v.reshape(1, -1)

    core = hi % 2
    first, second = jnp.where(core == 0, 2, 4), jnp.where(core == 0, 4, 2)
    both = lambda a, f, s: [a, a ^ f, a ^ s, a ^ 6]
    order = lambda a, f, s: [a, a ^ s, a ^ f, a ^ 6]
    gathered = both(hi, first, second) + both(hi ^ 1, second, first)
    exchanged = order(hi, first, second) + order(hi ^ 1, second, first)
    ends = jnp.cumsum(lax.dynamic_index_in_dim(clip_lengths, z, 0, keepdims=False))
    ends = jnp.concatenate([ends, jnp.zeros((GATHERED - clips,), jnp.int32)])
    info = jnp.concatenate([ends, jnp.stack(gathered + exchanged + [hi]).astype(jnp.int32)])

    def over_plane(v, flip):
        to = lambda a: ((a // rest) ^ flip((a // rest) % 2)) * rest + a % rest
        return lax.ppermute(v, "dp", [(a, to(a)) for a in range(places)])

    to_core = lambda v: over_plane(v, lambda c: 1)
    to_first = lambda v: over_plane(v, lambda c: 4 if c else 2)
    to_second = lambda v: over_plane(v, lambda c: 2 if c else 4)
    to_both = lambda v: over_plane(v, lambda c: 6)
    shift = lambda v, r: lax.ppermute(v, "mp", [(a, (a + r) % planes) for a in range(planes)])
    from_plane = lambda v, r: shift(v, -r)
    to_plane = shift

    def now(*arrays):
        return lax.optimization_barrier(arrays)

    near, last_far = [1, 3], 2
    far = near + [last_far]

    sems = lambda k: pltpu.SemaphoreType.DMA((k,))
    w_heads = w_qkv.transpose(0, 2, 1).reshape(3 * e, D)
    piece, unit_piece = call(
        cut_kernel,
        "cut",
        2,
        16,
        [(info, SMEM), (w_heads, HBM), (w_out, HBM), (w_up, HBM), (w_down, HBM), (bias_qv, VMEM), (row(bias_up), VMEM)],
        [(SDS((n + TAIL, D), BF), VMEM), (SDS((2 * n, D), BF), VMEM)],
        [VMEM((TAIL, D), F32), sems(8)],
    )
    pieces = {0: piece, **{r: from_plane(piece, r) for r in far}}

    tl = windows(T)
    wm, qm = max(t[3] for t in tl), max(t[1] for t in tl)
    scale = HEAD_DIM**-0.5 * LOG2E
    attn_out = [(SDS((3 * e, T), BF), VMEM), (SDS((e, T), BF), VMEM), (SDS((8, T), F32), VMEM)]
    attn_sc = [VMEM((heads, T, HEAD_DIM), BF), VMEM((2, wm, qm), F32), VMEM((heads, wm, qm), F32), VMEM((heads, wm, qm), BF)]
    n1, q0 = call(
        partial(first_kernel, heads),
        "first",
        4,
        20,
        [(tokens, VMEM), (row(gain_attn), VMEM), (row(shift_attn), VMEM), (w_heads, VMEM), (piece, VMEM)],
        [(SDS((T, D), BF), VMEM), attn_out[0]],
        [],
    )
    ws, qs, os, ls = {0: w_out}, {0: q0}, {}, {}

    def join(*v):
        return jnp.concatenate(v)

    def attn(r, c4, r4, after, us=7):
        ws[r], qs[r], os[r], ls[r] = call(
            partial(attn_kernel, clips, tl, heads, scale),
            f"attn{r}",
            us,
            24,
            [(info, SMEM), (n1, VMEM), (pieces[r], VMEM), (c4, VMEM), (r4, VMEM)],
            [(SDS((4 * e, D), BF), VMEM)] + attn_out,
            attn_sc,
            after=after,
        )
        return ls[r]

    a1, a3, a2 = far
    q0, p1, p3 = now(q0, pieces[a1], pieces[a3])
    got1 = [p1, to_first(p1), to_second(p1), to_both(p1)]
    f3 = to_first(p3)
    os[0], ls[0] = call(
        partial(attend_kernel, clips, tl, heads, scale),
        "attend0",
        4,
        20,
        [(info, SMEM), (q0, VMEM)],
        attn_out[1:],
        attn_sc,
    )
    _, p3, f3, p2, *got1 = now(ls[0], p3, f3, pieces[a2], *got1)
    c1, c3 = join(*(v[:n] for v in got1)), join(p3[:n], f3[:n])
    core1, s3, f2 = to_core(c1), to_second(c3), to_first(p2)
    near_piece = now(unit_piece, c1)[0]
    near_z = [from_plane(near_piece, r) for r in near]
    t = attn(a1, c1, core1, [])
    _, s3, f2, *near_z = now(t, s3, f2, *near_z)
    c3, c2, near_b = join(c3, s3), join(p2[:n], f2[:n]), join(*near_z)
    core3, s2, near_f = to_core(c3), to_second(c2), to_first(near_b)
    far_b = from_plane(near_z[0], 1)
    t = attn(a3, c3, core3, [c2, near_b])
    _, s2, near_f, far_b = now(t, s2, near_f, far_b)
    c2, near_b = join(c2, s2), join(near_b, near_f)
    core2, near_s, far_f = to_core(c2), to_second(near_b), to_first(far_b)
    attn(a2, c2, core2, [near_b])

    def block(i, keep, core, first):
        return f32(keep[i]) + f32(core[i]) + f32(first[i])

    def hop_first(*had):
        half = PARTS // 4
        return apart(to_first, [(f32(keep[half:]) + f32(core[half:])).astype(BF) for keep, core in had], 1)

    def hop_second(*had):
        return apart(to_second, [block(1, *v).astype(BF) for v in had], 0)

    def apart(hop, v, axis):
        if len(v) == 1:
            return [hop(v[0])]
        return jnp.split(hop(jnp.concatenate(v, axis)), np.cumsum([a.shape[axis] for a in v])[:-1], axis)

    def total(keep, core, first, second):
        k = block(0, keep, core, first) + f32(second)
        if rest > 1:
            groups = [[a * rest + b for b in range(rest)] for a in range(PARTS)]
            k = k.reshape(-1, n, k.shape[-1])
            k = lax.psum_scatter(k, "dp", scatter_dimension=1, axis_index_groups=groups, tiled=True)
            k = k.reshape(-1, k.shape[-1])
        return k

    half = PARTS // 2
    acts = [VMEM((T, D), F32)] * 2 + [VMEM((T, H), BF)] * 2 + [VMEM((D, H), BF)] * 2
    weights = [VMEM((D, H), BF), VMEM((H, D), BF)]
    grads = lambda k: [(SDS((half, k * 2 * n, H), BF), HBM)] * 2
    sums = [(SDS((T, D), F32), HBM)] * 2
    mixed, n2 = call(
        mid_kernel,
        "mid",
        6,
        24,
        [(tokens, VMEM), (row(bias_out), VMEM), (row(gain_mlp), VMEM), (row(shift_mlp), VMEM)]
        + [(os[r], VMEM) for r in range(planes)]
        + [(ws[r], VMEM) for r in range(planes)],
        [(SDS((T, D), F32), HBM), (SDS((T, D), BF), VMEM)],
        [VMEM((planes * e, T), BF), VMEM((planes * e, D), BF), VMEM((T, D), F32), sems(8)],
        after=[far_b],
    )
    n2, near_s, far_f = now(n2, near_s, far_f)
    near_b, far_b = join(near_b, near_s), join(far_b, far_f)
    near_r, far_s = to_core(near_b), to_second(far_b)
    out_acc, g_acc, u0_keep, u0_send, gb0 = call(
        own_kernel,
        "own",
        12,
        40,
        [(info, SMEM), (n2, VMEM), (cotangent, VMEM), (piece, VMEM), (w_up, VMEM), (w_down, VMEM)],
        sums + grads(1) + [(SDS((1, H), F32), VMEM)],
        acts + [sems(24)],
        after=[near_b, far_b],
    )
    gb0, near_r, far_s = now(gb0, near_r, far_s)
    far_b = join(far_b, far_s)
    far_r, u0_core = to_core(far_b), to_core(u0_send)
    k = len(near)
    out_acc, g_acc, u13_keep, u13_send, gb13 = call(
        partial(mlp_kernel, k),
        "mlp",
        22,
        40,
        [(info, SMEM), (n2, VMEM), (cotangent, VMEM), (out_acc, HBM), (g_acc, HBM), (near_b, VMEM), (near_r, VMEM)]
        + [(pieces[r], VMEM) for r in near],
        sums + grads(k) + [(SDS((k, H), F32), VMEM)],
        acts + weights + [sems(40)],
        after=[far_b],
    )
    gb13, far_r, u0_core = now(gb13, far_r, u0_core)
    (u0_first,), u13_core = hop_first((u0_keep, u0_core)), to_core(u13_send)
    result, grad_mixed, branch, u2_keep, u2_send, sm1 = call(
        mlp_last_kernel,
        "mlplast",
        15,
        42,
        [(info, SMEM), (n2, VMEM), (cotangent, VMEM), (out_acc, HBM), (g_acc, HBM), (far_b, VMEM), (far_r, VMEM)]
        + [(pieces[last_far], VMEM), (mixed, HBM), (row(bias_down), VMEM), (row(gain_mlp), VMEM), (gb0, VMEM), (gb13, VMEM)],
        [(SDS((T, D), BF), HBM), (SDS((T, D), F32), HBM), (SDS((T, D), BF), VMEM)]
        + grads(1)
        + [(SDS((8, H), F32), VMEM)],
        acts + weights + [VMEM((T, D), F32), VMEM((T, D), BF), sems(32)],
    )

    back_sc = (
        [VMEM((heads, T, HEAD_DIM), BF)] * 2
        + [VMEM((e, T), BF)]
        + [VMEM((2, wm, qm), F32)]
        + [VMEM((heads, wm, qm), BF)] * 2
        + [VMEM((e, T), F32)] * 2
    )
    spec = (clips, tl, heads, scale, HEAD_DIM**-0.5)
    ins = lambda r: [(v, VMEM) for v in (branch, n1, qs[r], ws[r], os[r], ls[r])]
    ds, smalls = {}, {}

    def back(r, after):
        ds[r], keep, send, smalls[r] = call(
            partial(back_kernel, *spec),
            f"back{r}",
            11,
            30,
            [(info, SMEM)] + ins(r),
            [(SDS((3 * e, T), BF), VMEM)] + [(SDS((half, n, 4 * e), BF), VMEM)] * 2 + [(SDS((1, 512), F32), VMEM)],
            [VMEM((D, 4 * e), BF)] + back_sc,
            after=after,
        )
        return keep, send

    r2, r1, r3 = last_far, *near
    sm1, u0_first, u13_core = now(sm1, u0_first, u13_core)
    u0 = u0_keep, u0_core, u0_first
    (u0_second,), (u13_first,), u2_core = hop_second(u0), hop_first((u13_keep, u13_core)), to_core(u2_send)
    h2_keep, h2_send = back(r2, [sm1])
    t, u0_second, u2_core = now(smalls[r2], u0_second, u2_core)
    (u2_first,), h2_core = hop_first((u2_keep, u2_core)), to_core(h2_send)
    h1_keep, h1_send = back(r1, [t])
    t, u13_first, u2_first, h2_core = now(smalls[r1], u13_first, u2_first, h2_core)
    u13, u2 = (u13_keep, u13_core, u13_first), (u2_keep, u2_core, u2_first)
    seconds, h1_core = hop_second(u13, u2), to_core(h1_send)
    units_of = {0: total(*u0, u0_second)}
    h3_keep, h3_send = back(r3, [t])
    t, h1_core, *seconds = now(smalls[r3], h1_core, *seconds)
    pair = total(*u13, seconds[0])
    rows = pair.shape[0] // len(near)
    for i, r in enumerate(near):
        units_of[r] = to_plane(pair[i * rows : (i + 1) * rows].astype(BF), r)
    units_of[r2] = to_plane(total(*u2, seconds[1]).astype(BF), r2)
    (h2_first, h1_first), h3_core = hop_first((h2_keep, h2_core), (h1_keep, h1_core)), to_core(h3_send)
    h0_keep, h0_send = back(0, [t])
    t, h2_first, h1_first, h3_core = now(smalls[0], h2_first, h1_first, h3_core)
    h2, h1 = (h2_keep, h2_core, h2_first), (h1_keep, h1_core, h1_first)
    seconds = hop_second(h2, h1)
    (h3_first,), h0_core = hop_first((h3_keep, h3_core)), to_core(h0_send)
    grad_tokens, small = call(
        partial(last_kernel, planes),
        "last",
        8,
        20,
        [(tokens, VMEM), (row(gain_attn), VMEM), (grad_mixed, VMEM), (sm1, VMEM)]
        + [(ds[r], VMEM) for r in range(planes)]
        + [(ws[r] if r else w_heads, VMEM) for r in range(planes)]
        + [(smalls[r], VMEM) for r in [0] + far],
        [(SDS((T, D), F32), HBM), (SDS((TAIL, D), F32), VMEM)],
        [VMEM((T, D), F32), VMEM((T, D), F32), sems(8)],
        after=[h2_first],
    )

    steps = [1 << i for i in range(places.bit_length() - 1)]
    hop_small = lambda v, step: v + lax.ppermute(v, "dp", [(a, a ^ step) for a in range(places)])
    small, h3_first, h0_core, *seconds = now(small, h3_first, h0_core, *seconds)
    h3, small = (h3_keep, h3_core, h3_first), hop_small(small, steps[0])
    (h0_first,), (h3_second,) = hop_first((h0_keep, h0_core)), hop_second(h3)
    heads_of = {r: to_plane(total(*h, v).astype(BF), r) for r, h, v in zip((r2, r1), (h2, h1), seconds)}
    small, h0_first, h3_second, *came = now(small, h0_first, h3_second, *(units_of[r] for r in far))
    units_of.update(zip(far, came))
    h0, small = (h0_keep, h0_core, h0_first), hop_small(small, steps[1])
    (h0_second,) = hop_second(h0)
    heads_of[r3] = to_plane(total(*h3, h3_second).astype(BF), r3)
    for step in steps[2:]:
        small = hop_small(small, step)
    tails = {0: small, **{r: to_plane(small, r) for r in far}}
    heads_of[0] = total(*h0, h0_second)

    m = D // places
    units = units_of[0] + sum(f32(units_of[r]) for r in far)
    hd = heads_of[0] + sum(f32(heads_of[r]) for r in far)
    grad_w_up, grad_w_down = units[:m], units[m:].T
    grad_w_qkv = hd[:, : 3 * e].reshape(m, 3, e).transpose(1, 0, 2)
    grad_w_out = hd[:, 3 * e :].T

    seat = {r: i for i, r in enumerate([0] + far)}
    size = D // (places * planes)
    spots = jnp.stack([(d * planes + z) * size, d * (H // places), d * (e // places)]).astype(jnp.int32)
    *vecs, grad_bias_up, grad_bias_qv = call(
        partial(cut_sums_kernel, [seat[r] for r in range(planes)]),
        "cutsums",
        1,
        16,
        [(spots, SMEM)] + [(tails[r], VMEM) for r in range(planes)],
        [(SDS((size,), F32), VMEM)] * 6 + [(SDS((H // places,), F32), VMEM), (SDS((2, e // places), F32), VMEM)],
        [],
    )
    return (
        result,
        grad_tokens,
        vecs[0],
        vecs[1],
        grad_w_qkv,
        grad_bias_qv,
        grad_w_out,
        vecs[2],
        vecs[3],
        vecs[4],
        grad_w_up,
        grad_bias_up,
        grad_w_down,
        vecs[5],
    )


def solution(mesh):
    return jax.shard_map(
        partial(on_device, mesh.shape["dp"], mesh.shape["mp"]),
        mesh=mesh,
        in_specs=(
            P(("dp", "mp"), None),
            P("dp", None),
            P(),
            P(),
            P(None, None, "mp"),
            P(None, "mp"),
            P("mp", None),
            P(),
            P(),
            P(),
            P(None, "mp"),
            P("mp"),
            P("mp", None),
            P(),
            P(("dp", "mp"), None),
        ),
        out_specs=(
            P(("dp", "mp"), None),
            P(("dp", "mp"), None),
            P(("dp", "mp")),
            P(("dp", "mp")),
            P(None, "dp", "mp"),
            P(None, ("mp", "dp")),
            P("mp", "dp"),
            P(("dp", "mp")),
            P(("dp", "mp")),
            P(("dp", "mp")),
            P("dp", "mp"),
            P(("mp", "dp")),
            P("mp", "dp"),
            P(("dp", "mp")),
        ),
        check_vma=False,
    )
```

```python
from functools import partial

import jax
import jax.numpy as jnp
import numpy as np
from jax import lax
from jax.experimental import pallas as pl
from jax.experimental.pallas import tpu as pltpu
from jax.sharding import PartitionSpec as P

F32, BF = jnp.float32, jnp.bfloat16
HEAD_DIM = 64
MOST = 256
EPSILON = 1e-06
MASKED = -1e30
LOG2E = 1.4426950408889634
ROOT_HALF = 0.7071067811865476
RSQRT_2PI = 0.3989422804014327
PARTS = 8
KEY_BLOCK = 128
TAIL = 16
GATHERED, EXCHANGED, PLACE = 8, 16, 24
VMEM, SMEM, HBM = pltpu.VMEM, pltpu.SMEM, pltpu.HBM
LANES = 128
SDS = jax.ShapeDtypeStruct


def _dot(a, b, i, j):
    return lax.dot_general(a, b, (((i,), (j,)), ((), ())), preferred_element_type=F32)


def nn(a, b):
    return _dot(a, b, 1, 0)


def nt(a, b):
    return _dot(a, b, 1, 1)


def tn(a, b):
    return _dot(a, b, 0, 0)


def tt(a, b):
    return _dot(a, b, 0, 1)


def call(body, name, us, megabytes, ins, outs, scratch, after=()):
    count, skip = len(ins), len(ins) + len(after)

    def kernel(*refs):
        body(*refs[:count], *refs[skip:])

    pinned = lambda o, m: HBM(o.shape, o.dtype) if m is HBM else o
    there = lambda a, m: pltpu.with_memory_space_constraint(a, HBM) if m is HBM else a
    return pl.pallas_call(
        kernel,
        out_shape=tuple(pinned(*o) for o in outs),
        in_specs=[pl.BlockSpec(memory_space=m) for _, m in ins] + [pl.BlockSpec(memory_space=pl.ANY)] * len(after),
        out_specs=tuple(pl.BlockSpec(memory_space=m) for _, m in outs),
        scratch_shapes=scratch,
        compiler_params=pltpu.CompilerParams(vmem_limit_bytes=megabytes << 20),
        cost_estimate=pl.CostEstimate(flops=int(us * 1.0e9), bytes_accessed=1 << 20, transcendentals=0),
        name=name,
    )(*(there(*a) for a in ins), *after)


class Mover:
    def __init__(self, sems):
        self.sems, self.used = sems, 0

    def __call__(self, src, dst):
        c = pltpu.make_async_copy(src, dst, self.sems.at[self.used])
        self.used += 1
        c.start()
        return c


def wait(*copies):
    for c in copies:
        c.wait()


def windows(slots, width=256):
    out = []
    for q0 in range(0, slots, width):
        qn = min(width, slots - q0)
        lo = max(0, (q0 - MOST + 1) // 128 * 128)
        hi = min(slots, -(-(q0 + qn + MOST - 1) // 128) * 128)
        out.append((q0, qn, lo, hi - lo))
    return out


def segments(info, clips, shape, axis):
    place = lax.broadcasted_iota(jnp.int32, shape, axis)
    seg = jnp.zeros(shape, jnp.int32)
    for c in range(clips):
        seg = seg + jnp.where(place >= info[c], 1, 0)
    return jnp.where(seg == clips - 1, place + clips, seg)


def fill_mask(bias_sc, segc, segr, q0, qn, k0, w):
    for b in range(0, w, KEY_BLOCK):
        same = segc[k0 + b : k0 + b + KEY_BLOCK, :] == segr[:, q0 : q0 + qn]
        bias_sc[b : b + KEY_BLOCK, :qn] = jnp.where(same, 0.0, MASKED)


def fold(x, f):
    return f(x.reshape(x.shape[0] // 8, 8, x.shape[1]), axis=0)


def attend(tl, heads, scale, qkvT, kn, segc, segr, oT, lse, bias_sc, s_sc, p_sc):
    e, hd = heads * HEAD_DIM, HEAD_DIM

    def scores(tile, h):
        q0, qn, k0, w = tl[tile]
        if h == 0:
            fill_mask(bias_sc.at[tile % 2], segc, segr, q0, qn, k0, w)
        q = qkvT[h * hd : (h + 1) * hd, q0 : q0 + qn]
        m = None
        for b in range(0, w, KEY_BLOCK):
            k = slice(b, b + KEY_BLOCK)
            s = nn(kn[h, k0 + b : k0 + b + KEY_BLOCK, :], q) * scale + bias_sc[tile % 2, k, :qn]
            s_sc[h, k, :qn] = s
            mb = fold(s, jnp.max)
            m = mb if m is None else jnp.maximum(m, mb)
        return jnp.max(m, axis=0, keepdims=True)

    def finish(tile, h, m):
        q0, qn, k0, w = tl[tile]
        total = None
        for b in range(0, w, KEY_BLOCK):
            p = jnp.exp2(s_sc[h, b : b + KEY_BLOCK, :qn] - m)
            p_sc[h, b : b + KEY_BLOCK, :qn] = p.astype(BF)
            lb = fold(p, jnp.sum)
            total = lb if total is None else total + lb
        total = jnp.sum(total, axis=0, keepdims=True)
        o = nn(qkvT[2 * e + h * hd : 2 * e + (h + 1) * hd, k0 : k0 + w], p_sc[h, :w, :qn])
        oT[h * hd : (h + 1) * hd, q0 : q0 + qn] = (o * (1.0 / total)).astype(BF)
        lse[h : h + 1, q0 : q0 + qn] = m + jnp.log2(total)

    steps = [(tile, h) for tile in range(len(tl)) for h in range(heads)]
    ahead = scores(*steps[0])
    for at, step in enumerate(steps):
        m = ahead
        if at + 1 < len(steps):
            ahead = scores(*steps[at + 1])
        finish(*step, m)


def unit(x):
    y = x - jnp.mean(x, axis=1, keepdims=True)
    inverse = lax.rsqrt(jnp.mean(y * y, axis=1, keepdims=True) + EPSILON)
    return y * inverse, inverse


def unit_back(up, n, inverse, gain):
    g = up * gain
    return inverse * (g - jnp.mean(g, axis=1, keepdims=True) - n * jnp.mean(g * n, axis=1, keepdims=True))


def normal(u):
    bell = jnp.exp2(u * u * (-0.5 * LOG2E))
    d = jnp.abs(u) * (0.3275911 * ROOT_HALF) + 1.0
    t = pl.reciprocal(d, approx=True)
    t = t * (2.0 - d * t)
    q = 0.5 * 1.061405429
    for c in (-1.453152027, 1.421413741, -0.284496736, 0.254829592):
        q = q * t + 0.5 * c
    q = q * t * bell
    return jnp.where(u >= 0.0, 1.0 - q, q), bell * RSQRT_2PI


def blocks_out(move, info, source, place, keep, send):
    n, half = source.shape[0] // PARTS, PARTS // 2
    copies = []
    for j in range(PARTS):
        row = pl.ds(pl.multiple_of(info[EXCHANGED + j] * n, n), n)
        out = keep if j < half else send
        if move is None:
            out[j % half, place : place + n, :] = source[row, :]
        else:
            copies.append(move(source.at[row], out.at[j % half, pl.ds(place, n)]))
    return copies


def cut_kernel(info, w_heads, w_out, w_up, w_down, bias_qv, bias_up, piece, units, tail_s, sems):
    e, H = w_out.shape[0], bias_up.shape[1]
    n = units.shape[0] // 2
    move = Mover(sems)
    at = info[PLACE]
    row = pl.ds(pl.multiple_of(at * n, n), n)
    edge = w_heads.shape[0] // n
    loads = [move(w_up.at[row], units.at[pl.ds(0, n)]), move(w_down.at[row], units.at[pl.ds(n, n)])]
    tail_s[...] = jnp.zeros_like(tail_s)
    tail_s[0:1, :H] = bias_up[...].astype(F32)
    for i in range(2):
        tail_s[1:2, 256 * i : 256 * i + e] = bias_qv[i : i + 1, :].astype(F32)
    piece[pl.ds(n, TAIL), :] = tail_s[...].astype(BF)

    @pl.when(at < edge)
    def _():
        src = w_heads.at[pl.ds(pl.multiple_of(jnp.minimum(at, edge - 1) * n, n), n)]
        wait(move(src, piece.at[pl.ds(0, n)]))

    @pl.when(at >= edge)
    def _():
        src = w_out.at[pl.ds(pl.multiple_of(jnp.maximum(at - edge, 0) * n, n), n)]
        wait(move(src, piece.at[pl.ds(0, n)]))

    wait(*loads)


def project(heads, n1, w, piece, qkvT):
    e = heads * HEAD_DIM
    n = piece.shape[0] - TAIL
    biases = piece[n : n + TAIL, :512].astype(F32)[1:2, :]
    for c in range(3):
        t = nt(w[c * e : (c + 1) * e, :], n1[...])
        if c != 1:
            at = 128 * c
            t = t + jnp.broadcast_to(biases[:, at : at + 256], (LANES, 256)).T[:e, :1]
        qkvT[c * e : (c + 1) * e, :] = t.astype(BF)


def attend_kernel(clips, tl, heads, scale, info, qkvT, oT, lse, kn, bias_sc, s_sc, p_sc):
    slots = qkvT.shape[1]
    segc = segments(info, clips, (slots, 1), 0)
    segr = segments(info, clips, (1, slots), 1)
    e = heads * HEAD_DIM
    for h in range(heads):
        kn[h] = qkvT[e + h * HEAD_DIM : e + (h + 1) * HEAD_DIM, :].T
    attend(tl, heads, scale, qkvT, kn, segc, segr, oT, lse, bias_sc, s_sc, p_sc)


def first_kernel(heads, x, gain, shift, w, piece, n1, qkvT):
    for i in range(0, x.shape[0], LANES):
        n, _ = unit(x[i : i + LANES, :].astype(F32))
        n1[i : i + LANES, :] = (n * gain[...].astype(F32) + shift[...].astype(F32)).astype(BF)
    project(heads, n1, w, piece, qkvT)


def attn_kernel(clips, tl, heads, scale, info, n1, piece, p4, r4, w, qkvT, oT, lse, *scratch):
    n = w.shape[0] // PARTS
    for i in range(PARTS):
        ref = (p4, r4)[i // 4]
        w[pl.ds(pl.multiple_of(info[GATHERED + i] * n, n), n), :] = ref[i % 4 * n : (i % 4 + 1) * n, :]
    project(heads, n1, w, piece, qkvT)
    attend_kernel(clips, tl, heads, scale, info, qkvT, oT, lse, *scratch)


def chunk_front(n2, cot, wup, wdn, piece, hid, gp, gb):
    n = piece.shape[0] - TAIL
    u = nn(n2[...], wup[...]) + piece[n : n + TAIL, :].astype(F32)[0:1, : wup.shape[1]]
    ga = nt(cot[...], wdn[...])
    dist, dens = normal(u)
    hid[...] = (u * dist).astype(BF)
    g = (ga * (dist + u * dens)).astype(BF)
    gp[...] = g
    gb[...] = jnp.sum(g.astype(F32), axis=0, keepdims=True)


def chunk_sums(hid, gp, wup, wdn, out_acc, g_acc, fresh):
    o = nn(hid[...], wdn[...])
    out_acc[...] = o if fresh else out_acc[...] + o
    g = nt(gp[...], wup[...])
    g_acc[...] = g if fresh else g_acc[...] + g


def chunk_grads(move, info, n2, cot, hid, gp, up_sc, dn_sc, k, keep, send):
    n = n2.shape[1] // PARTS
    dn_sc[...] = tn(cot[...], hid[...]).astype(BF)
    copies = blocks_out(move, info, dn_sc, (2 * k + 1) * n, keep, send)
    up_sc[...] = tn(n2[...], gp[...]).astype(BF)
    return copies + blocks_out(move, info, up_sc, 2 * k * n, keep, send)


def mid_kernel(x, bias_out, gain, shift, *refs):
    count = (len(refs) - 6) // 2
    o, w, refs = refs[:count], refs[count : 2 * count], refs[2 * count :]
    mixed, n2, o_s, wo_s, mixed_s, sems = refs
    e = o[0].shape[0]
    move = Mover(sems)
    for r in range(count):
        o_s[r * e : (r + 1) * e, :] = o[r][...]
        wo_s[r * e : (r + 1) * e, :] = w[r][w[r].shape[0] - e :, :]
    mixed_s[...] = tn(o_s[...], wo_s[...])
    done = []
    for i in range(0, x.shape[0], LANES):
        k = slice(i, i + LANES)
        m = mixed_s[k, :] + x[k, :].astype(F32) + bias_out[...].astype(F32)
        mixed_s[k, :] = m
        done.append(move(mixed_s.at[pl.ds(i, LANES)], mixed.at[pl.ds(i, LANES)]))
        n, _ = unit(m)
        n2[k, :] = (n * gain[...].astype(F32) + shift[...].astype(F32)).astype(BF)
    wait(*done)


def own_kernel(info, n2, cot, piece, wup, wdn, out, g, keep, send, gb, out_s, g_s, hid, gp, up_sc, dn_sc, sems):
    move = Mover(sems)
    chunk_front(n2, cot, wup, wdn, piece, hid, gp, gb)
    chunk_sums(hid, gp, wup, wdn, out_s, g_s, True)
    done = [move(out_s, out), move(g_s, g)]
    wait(*chunk_grads(move, info, n2, cot, hid, gp, up_sc, dn_sc, 0, keep, send), *done)


def units_here(info, refs, wup, wdn, k, count):
    n = wup.shape[0] // PARTS
    for i in range(PARTS):
        ref, at = refs[i // 2], (i % 2 * count + k) * 2 * n
        row = pl.ds(pl.multiple_of(info[GATHERED + i] * n, n), n)
        wup[row, :] = ref[at : at + n, :]
        wdn[row, :] = ref[at + n : at + 2 * n, :]


def mlp_kernel(count, info, n2, cot, out_in, g_in, own, own2, core, core2, *refs):
    piece, refs = refs[:count], refs[count:]
    out, g, keep, send, gb, out_s, g_s, hid, gp, up_sc, dn_sc, wup, wdn, sems = refs
    move = Mover(sems)
    sums = [move(out_in, out_s), move(g_in, g_s)]
    done = []
    for k in range(count):
        units_here(info, (own, own2, core, core2), wup, wdn, k, count)
        chunk_front(n2, cot, wup, wdn, piece[k], hid, gp, gb.at[pl.ds(k, 1)])
        if k == 0:
            wait(*sums)
        chunk_sums(hid, gp, wup, wdn, out_s, g_s, False)
        wait(*done)
        done = []
        if k == count - 1:
            done = [move(out_s, out), move(g_s, g)]
        done += chunk_grads(move, info, n2, cot, hid, gp, up_sc, dn_sc, k, keep, send)
    wait(*done)


def mlp_last_kernel(info, n2, cot, out_in, g_in, own, own2, core, core2, piece, mixed, bias_down, gain, *refs):
    gbs, refs = refs[: len(refs) - 17], refs[len(refs) - 17 :]
    result, grad_mixed, branch, keep, send, sm = refs[:6]
    out_s, g_s, hid, gp, up_sc, dn_sc, wup, wdn, mixed_s, result_s, sems = refs[6:]
    move = Mover(sems)
    sums = [move(out_in, out_s), move(g_in, g_s), move(mixed, mixed_s)]
    units_here(info, (own, own2, core, core2), wup, wdn, 0, 1)
    chunk_front(n2, cot, wup, wdn, piece, hid, gp, sm.at[pl.ds(7, 1)])
    wait(*sums)
    chunk_sums(hid, gp, wup, wdn, out_s, g_s, False)
    vecs = [0.0] * 4
    for i in range(0, n2.shape[0], LANES):
        k = slice(i, i + LANES)
        up, mid, c = g_s[k, :], mixed_s[k, :], cot[k, :].astype(F32)
        result_s[k, :] = (mid + out_s[k, :] + bias_down[...].astype(F32)).astype(BF)
        m, inverse = unit(mid)
        gm = c + unit_back(up, m, inverse, gain[...].astype(F32))
        mixed_s[k, :] = gm
        branch[k, :] = gm.astype(BF)
        for j, v in enumerate((gm, up * m, up, c)):
            vecs[j] = vecs[j] + fold(v, jnp.sum)
    done = [move(mixed_s, grad_mixed), move(result_s, result)]
    for j in range(4):
        sm[j : j + 1, :] = jnp.sum(vecs[j], axis=0, keepdims=True)
    at = 4
    for ref in gbs:
        sm[at : at + ref.shape[0], :] = ref[...]
        at += ref.shape[0]
    done += chunk_grads(move, info, n2, cot, hid, gp, up_sc, dn_sc, 0, keep, send)
    wait(*done)


def back_heads(clips, tl, heads, scale, part, info, gb, w, q_s, oT, lse, d_s, scratch):
    kn, vn, ga, bias_sc, pb_sc, ds_sc, dk, dv = scratch
    e, hd = heads * HEAD_DIM, HEAD_DIM
    slots = gb.shape[0]
    segc = segments(info, clips, (slots, 1), 0)
    segr = segments(info, clips, (1, slots), 1)
    ga[...] = nt(w[w.shape[0] - e :, :], gb[...]).astype(BF)
    for h in range(heads):
        kn[h] = q_s[e + h * hd : e + (h + 1) * hd, :].T
        vn[h] = q_s[2 * e + h * hd : 2 * e + (h + 1) * hd, :].T
    dk[...] = jnp.zeros_like(dk)
    dv[...] = jnp.zeros_like(dv)

    def scores(tile, h):
        q0, qn, k0, wide = tl[tile]
        if h == 0:
            fill_mask(bias_sc.at[tile % 2], segc, segr, q0, qn, k0, wide)
        hs = slice(h * hd, (h + 1) * hd)
        q, go = q_s[hs, q0 : q0 + qn], ga[hs, q0 : q0 + qn]
        total = lse[h : h + 1, q0 : q0 + qn]
        centre = jnp.sum(go.astype(F32) * oT[hs, q0 : q0 + qn].astype(F32), axis=0, keepdims=True)
        for b in range(0, wide, KEY_BLOCK):
            k, v = slice(b, b + KEY_BLOCK), slice(k0 + b, k0 + b + KEY_BLOCK)
            p = jnp.exp2(nn(kn[h, v, :], q) * scale + bias_sc[tile % 2, k, :qn] - total)
            pb_sc[h, k, :qn] = p.astype(BF)
            ds_sc[h, k, :qn] = (p * (nn(vn[h, v, :], go) - centre)).astype(BF)

    def finish(tile, h):
        q0, qn, k0, wide = tl[tile]
        hs = slice(h * hd, (h + 1) * hd)
        q, go = q_s[hs, q0 : q0 + qn], ga[hs, q0 : q0 + qn]
        ds = ds_sc[h, :wide, :qn]
        d_s[hs, q0 : q0 + qn] = (nn(q_s[e + h * hd : e + (h + 1) * hd, k0 : k0 + wide], ds) * part).astype(BF)
        dk[hs, k0 : k0 + wide] += nt(q, ds)
        dv[hs, k0 : k0 + wide] += nt(go, pb_sc[h, :wide, :qn])

    steps = [(tile, h) for tile in range(len(tl)) for h in range(heads)]
    scores(*steps[0])
    for at, step in enumerate(steps):
        if at + 1 < len(steps):
            scores(*steps[at + 1])
        finish(*step)
    d_s[e : 2 * e, :] = (dk[...] * part).astype(BF)
    d_s[2 * e : 3 * e, :] = dv[...].astype(BF)


def bias_rows(d_s, small, at, e):
    rows = nt(jnp.ones((8, d_s.shape[1]), BF), d_s[...])
    small[at : at + 1, 0:e] = rows[0:1, 0:e]
    small[at : at + 1, 256 : 256 + e] = rows[0:1, 2 * e : 3 * e]


def head_grads(move, info, gb, n1, oT, d_s, acc, keep, send):
    k = d_s.shape[0]
    acc[:, :k] = tt(n1[...], d_s[...]).astype(BF)
    acc[:, k:] = tt(gb[...], oT[...]).astype(BF)
    return blocks_out(move, info, acc, 0, keep, send)


def back_kernel(clips, tl, heads, scale, part, info, gb, n1, q, w, oT, lse, d, keep, send, small, acc, *scratch):
    small[...] = jnp.zeros_like(small)
    back_heads(clips, tl, heads, scale, part, info, gb, w, q, oT, lse, d, scratch)
    bias_rows(d, small, 0, heads * HEAD_DIM)
    head_grads(None, info, gb, n1, oT, d, acc, keep, send)


def last_kernel(planes, x, gain, grad_mixed, sm1, *refs):
    d, w, smalls = refs[:planes], refs[planes : 2 * planes], refs[2 * planes : 3 * planes]
    grad_tokens, sm, g_sc, gm_s, sems = refs[3 * planes :]
    rows = d[0].shape[0]
    move = Mover(sems)
    for r in range(planes):
        g = tn(d[r][...], w[r][:rows, :])
        g_sc[...] = g if r == 0 else g_sc[...] + g
    vecs, done = [0.0] * 2, []
    for i in range(0, x.shape[0], LANES):
        k = slice(i, i + LANES)
        up = g_sc[k, :]
        m, inverse = unit(x[k, :].astype(F32))
        gm_s[k, :] = grad_mixed[k, :] + unit_back(up, m, inverse, gain[...].astype(F32))
        done.append(move(gm_s.at[pl.ds(i, LANES)], grad_tokens.at[pl.ds(i, LANES)]))
        for j, v in enumerate((up * m, up)):
            vecs[j] = vecs[j] + fold(v, jnp.sum)
    sm[...] = jnp.zeros_like(sm)
    for j in range(2):
        sm[j : j + 1, :] = jnp.sum(vecs[j], axis=0, keepdims=True)
    for r in range(planes):
        sm[2 + r : 3 + r, :512] = smalls[r][...]
    sm[6:14, :] = sm1[...]
    wait(*done)


def cut_sums_kernel(seats, at, *refs):
    count = len(seats)
    tails, (g_ga, g_sa, g_bo, g_gm, g_sm, g_bd, g_bu, g_qv) = refs[:count], refs[count:]
    width = tails[0].shape[1]
    total = tails[0][...]
    for t in tails[1:]:
        total = total + t[...]
    bu = tails[0][10 + seats[0] : 11 + seats[0], :]
    qv = tails[0][2 + seats[0] : 3 + seats[0], :]
    for t, seat in zip(tails[1:], seats[1:]):
        bu = bu + t[10 + seat : 11 + seat, :]
        qv = qv + t[2 + seat : 3 + seat, :]
    shifted = lambda v, i: pltpu.roll(v, jnp.where(at[i] == 0, 0, width - at[i]), 1)
    vecs = shifted(total, 0)
    for j, ref in zip((0, 1, 6, 7, 8, 9), (g_ga, g_sa, g_bo, g_gm, g_sm, g_bd)):
        ref[...] = vecs[j, : ref.shape[0]]
    g_bu[...] = shifted(jnp.broadcast_to(bu, (8, width)), 1)[0, : g_bu.shape[0]]
    qv = shifted(jnp.broadcast_to(qv, (8, width)), 2)
    for i in range(2):
        g_qv[i : i + 1, :] = qv[0:1, 256 * i : 256 * i + g_qv.shape[1]]


def on_device(
    places,
    planes,
    tokens,
    clip_lengths,
    gain_attn,
    shift_attn,
    w_qkv,
    bias_qv,
    w_out,
    bias_out,
    gain_mlp,
    shift_mlp,
    w_up,
    bias_up,
    w_down,
    bias_down,
    cotangent,
):
    T, D = tokens.shape
    clips = clip_lengths.shape[1]
    e = w_out.shape[0]
    heads = e // HEAD_DIM
    H = w_up.shape[1]
    n = D // PARTS
    rest = places // PARTS
    d, z = lax.axis_index("dp"), lax.axis_index("mp")
    hi = d // rest
    f32 = lambda v: v.astype(F32)
    row = lambda v: v.reshape(1, -1)

    core = hi % 2
    first, second = jnp.where(core == 0, 2, 4), jnp.where(core == 0, 4, 2)
    both = lambda a, f, s: [a, a ^ f, a ^ s, a ^ 6]
    order = lambda a, f, s: [a, a ^ s, a ^ f, a ^ 6]
    gathered = both(hi, first, second) + both(hi ^ 1, second, first)
    exchanged = order(hi, first, second) + order(hi ^ 1, second, first)
    ends = jnp.cumsum(lax.dynamic_index_in_dim(clip_lengths, z, 0, keepdims=False))
    ends = jnp.concatenate([ends, jnp.zeros((GATHERED - clips,), jnp.int32)])
    info = jnp.concatenate([ends, jnp.stack(gathered + exchanged + [hi]).astype(jnp.int32)])

    def over_plane(v, flip):
        to = lambda a: ((a // rest) ^ flip((a // rest) % 2)) * rest + a % rest
        return lax.ppermute(v, "dp", [(a, to(a)) for a in range(places)])

    to_core = lambda v: over_plane(v, lambda c: 1)
    to_first = lambda v: over_plane(v, lambda c: 4 if c else 2)
    to_second = lambda v: over_plane(v, lambda c: 2 if c else 4)
    to_both = lambda v: over_plane(v, lambda c: 6)
    shift = lambda v, r: lax.ppermute(v, "mp", [(a, (a + r) % planes) for a in range(planes)])
    from_plane = lambda v, r: shift(v, -r)
    to_plane = shift

    def now(*arrays):
        return lax.optimization_barrier(arrays)

    near, last_far = [1, 3], 2
    far = near + [last_far]

    sems = lambda k: pltpu.SemaphoreType.DMA((k,))
    w_heads = w_qkv.transpose(0, 2, 1).reshape(3 * e, D)
    piece, unit_piece = call(
        cut_kernel,
        "cut",
        2,
        16,
        [(info, SMEM), (w_heads, HBM), (w_out, HBM), (w_up, HBM), (w_down, HBM), (bias_qv, VMEM), (row(bias_up), VMEM)],
        [(SDS((n + TAIL, D), BF), VMEM), (SDS((2 * n, D), BF), VMEM)],
        [VMEM((TAIL, D), F32), sems(8)],
    )
    pieces = {0: piece, **{r: from_plane(piece, r) for r in far}}

    tl = windows(T)
    wm, qm = max(t[3] for t in tl), max(t[1] for t in tl)
    scale = HEAD_DIM**-0.5 * LOG2E
    attn_out = [(SDS((3 * e, T), BF), VMEM), (SDS((e, T), BF), VMEM), (SDS((8, T), F32), VMEM)]
    attn_sc = [VMEM((heads, T, HEAD_DIM), BF), VMEM((2, wm, qm), F32), VMEM((heads, wm, qm), F32), VMEM((heads, wm, qm), BF)]
    n1, q0 = call(
        partial(first_kernel, heads),
        "first",
        4,
        20,
        [(tokens, VMEM), (row(gain_attn), VMEM), (row(shift_attn), VMEM), (w_heads, VMEM), (piece, VMEM)],
        [(SDS((T, D), BF), VMEM), attn_out[0]],
        [],
    )
    ws, qs, os, ls = {0: w_out}, {0: q0}, {}, {}

    def join(*v):
        return jnp.concatenate(v)

    def attn(r, c4, r4, after, us=7):
        ws[r], qs[r], os[r], ls[r] = call(
            partial(attn_kernel, clips, tl, heads, scale),
            f"attn{r}",
            us,
            24,
            [(info, SMEM), (n1, VMEM), (pieces[r], VMEM), (c4, VMEM), (r4, VMEM)],
            [(SDS((4 * e, D), BF), VMEM)] + attn_out,
            attn_sc,
            after=after,
        )
        return ls[r]

    a1, a3, a2 = far
    q0, p1, p3 = now(q0, pieces[a1], pieces[a3])
    got1 = [p1, to_first(p1), to_second(p1), to_both(p1)]
    f3 = to_first(p3)
    os[0], ls[0] = call(
        partial(attend_kernel, clips, tl, heads, scale),
        "attend0",
        4,
        20,
        [(info, SMEM), (q0, VMEM)],
        attn_out[1:],
        attn_sc,
    )
    _, p3, f3, p2, *got1 = now(ls[0], p3, f3, pieces[a2], *got1)
    c1, c3 = join(*(v[:n] for v in got1)), join(p3[:n], f3[:n])
    core1, s3, f2 = to_core(c1), to_second(c3), to_first(p2)
    near_piece = now(unit_piece, c1)[0]
    near_z = [from_plane(near_piece, r) for r in near]
    t = attn(a1, c1, core1, [])
    _, s3, f2, *near_z = now(t, s3, f2, *near_z)
    c3, c2, near_b = join(c3, s3), join(p2[:n], f2[:n]), join(*near_z)
    core3, s2, near_f = to_core(c3), to_second(c2), to_first(near_b)
    far_b = from_plane(near_z[0], 1)
    t = attn(a3, c3, core3, [c2, near_b])
    _, s2, near_f, far_b = now(t, s2, near_f, far_b)
    c2, near_b = join(c2, s2), join(near_b, near_f)
    core2, near_s, far_f = to_core(c2), to_second(near_b), to_first(far_b)
    attn(a2, c2, core2, [near_b])

    def block(i, keep, core, first):
        return f32(keep[i]) + f32(core[i]) + f32(first[i])

    def hop_first(*had):
        half = PARTS // 4
        return apart(to_first, [(f32(keep[half:]) + f32(core[half:])).astype(BF) for keep, core in had], 1)

    def hop_second(*had):
        return apart(to_second, [block(1, *v).astype(BF) for v in had], 0)

    def apart(hop, v, axis):
        if len(v) == 1:
            return [hop(v[0])]
        return jnp.split(hop(jnp.concatenate(v, axis)), np.cumsum([a.shape[axis] for a in v])[:-1], axis)

    def total(keep, core, first, second):
        k = block(0, keep, core, first) + f32(second)
        if rest > 1:
            groups = [[a * rest + b for b in range(rest)] for a in range(PARTS)]
            k = k.reshape(-1, n, k.shape[-1])
            k = lax.psum_scatter(k, "dp", scatter_dimension=1, axis_index_groups=groups, tiled=True)
            k = k.reshape(-1, k.shape[-1])
        return k

    half = PARTS // 2
    acts = [VMEM((T, D), F32)] * 2 + [VMEM((T, H), BF)] * 2 + [VMEM((D, H), BF)] * 2
    weights = [VMEM((D, H), BF), VMEM((H, D), BF)]
    grads = lambda k: [(SDS((half, k * 2 * n, H), BF), HBM)] * 2
    sums = [(SDS((T, D), F32), HBM)] * 2
    mixed, n2 = call(
        mid_kernel,
        "mid",
        6,
        24,
        [(tokens, VMEM), (row(bias_out), VMEM), (row(gain_mlp), VMEM), (row(shift_mlp), VMEM)]
        + [(os[r], VMEM) for r in range(planes)]
        + [(ws[r], VMEM) for r in range(planes)],
        [(SDS((T, D), F32), HBM), (SDS((T, D), BF), VMEM)],
        [VMEM((planes * e, T), BF), VMEM((planes * e, D), BF), VMEM((T, D), F32), sems(8)],
    )
    near_r = to_core(now(near_b, n2)[0])
    out_acc, g_acc, u0_keep, u0_send, gb0 = call(
        own_kernel,
        "own",
        2,
        40,
        [(info, SMEM), (n2, VMEM), (cotangent, VMEM), (piece, VMEM), (w_up, VMEM), (w_down, VMEM)],
        sums + grads(1) + [(SDS((1, H), F32), VMEM)],
        acts + [sems(24)],
    )
    gb0, near_r, near_s, far_f = now(gb0, near_r, near_s, far_f)
    far_b = join(far_b, far_f)
    near_r2, far_s, far_r, u0_core = to_core(near_s), to_second(far_b), to_core(far_b), to_core(u0_send)
    k = len(near)
    out_acc, g_acc, u13_keep, u13_send, gb13 = call(
        partial(mlp_kernel, k),
        "mlp",
        22,
        40,
        [(info, SMEM), (n2, VMEM), (cotangent, VMEM), (out_acc, HBM), (g_acc, HBM)]
        + [(v, VMEM) for v in (near_b, near_s, near_r, near_r2)]
        + [(pieces[r], VMEM) for r in near],
        sums + grads(k) + [(SDS((k, H), F32), VMEM)],
        acts + weights + [sems(40)],
        after=[far_b],
    )
    gb13, far_s, far_r, u0_core = now(gb13, far_s, far_r, u0_core)
    far_r2 = to_core(far_s)
    (u0_first,), u13_core = hop_first((u0_keep, u0_core)), to_core(u13_send)
    result, grad_mixed, branch, u2_keep, u2_send, sm1 = call(
        mlp_last_kernel,
        "mlplast",
        15,
        42,
        [(info, SMEM), (n2, VMEM), (cotangent, VMEM), (out_acc, HBM), (g_acc, HBM)]
        + [(v, VMEM) for v in (far_b, far_s, far_r, far_r2)]
        + [(pieces[last_far], VMEM), (mixed, HBM), (row(bias_down), VMEM), (row(gain_mlp), VMEM), (gb0, VMEM), (gb13, VMEM)],
        [(SDS((T, D), BF), HBM), (SDS((T, D), F32), HBM), (SDS((T, D), BF), VMEM)]
        + grads(1)
        + [(SDS((8, H), F32), VMEM)],
        acts + weights + [VMEM((T, D), F32), VMEM((T, D), BF), sems(32)],
    )

    back_sc = (
        [VMEM((heads, T, HEAD_DIM), BF)] * 2
        + [VMEM((e, T), BF)]
        + [VMEM((2, wm, qm), F32)]
        + [VMEM((heads, wm, qm), BF)] * 2
        + [VMEM((e, T), F32)] * 2
    )
    spec = (clips, tl, heads, scale, HEAD_DIM**-0.5)
    ins = lambda r: [(v, VMEM) for v in (branch, n1, qs[r], ws[r], os[r], ls[r])]
    ds, smalls = {}, {}

    def back(r, after):
        ds[r], keep, send, smalls[r] = call(
            partial(back_kernel, *spec),
            f"back{r}",
            11,
            30,
            [(info, SMEM)] + ins(r),
            [(SDS((3 * e, T), BF), VMEM)] + [(SDS((half, n, 4 * e), BF), VMEM)] * 2 + [(SDS((1, 512), F32), VMEM)],
            [VMEM((D, 4 * e), BF)] + back_sc,
            after=after,
        )
        return keep, send

    r2, r1, r3 = last_far, *near
    sm1, u0_first, u13_core = now(sm1, u0_first, u13_core)
    u0 = u0_keep, u0_core, u0_first
    (u0_second,), (u13_first,), u2_core = hop_second(u0), hop_first((u13_keep, u13_core)), to_core(u2_send)
    h2_keep, h2_send = back(r2, [sm1])
    t, u0_second, u2_core = now(smalls[r2], u0_second, u2_core)
    (u2_first,), h2_core = hop_first((u2_keep, u2_core)), to_core(h2_send)
    h1_keep, h1_send = back(r1, [t])
    t, u13_first, u2_first, h2_core = now(smalls[r1], u13_first, u2_first, h2_core)
    u13, u2 = (u13_keep, u13_core, u13_first), (u2_keep, u2_core, u2_first)
    seconds, h1_core = hop_second(u13, u2), to_core(h1_send)
    units_of = {0: total(*u0, u0_second)}
    h3_keep, h3_send = back(r3, [t])
    t, h1_core, *seconds = now(smalls[r3], h1_core, *seconds)
    pair = total(*u13, seconds[0])
    rows = pair.shape[0] // len(near)
    for i, r in enumerate(near):
        units_of[r] = to_plane(pair[i * rows : (i + 1) * rows].astype(BF), r)
    units_of[r2] = to_plane(total(*u2, seconds[1]).astype(BF), r2)
    (h2_first, h1_first), h3_core = hop_first((h2_keep, h2_core), (h1_keep, h1_core)), to_core(h3_send)
    h0_keep, h0_send = back(0, [t])
    t, h2_first, h1_first, h3_core = now(smalls[0], h2_first, h1_first, h3_core)
    h2, h1 = (h2_keep, h2_core, h2_first), (h1_keep, h1_core, h1_first)
    seconds = hop_second(h2, h1)
    (h3_first,), h0_core = hop_first((h3_keep, h3_core)), to_core(h0_send)
    grad_tokens, small = call(
        partial(last_kernel, planes),
        "last",
        8,
        20,
        [(tokens, VMEM), (row(gain_attn), VMEM), (grad_mixed, VMEM), (sm1, VMEM)]
        + [(ds[r], VMEM) for r in range(planes)]
        + [(ws[r] if r else w_heads, VMEM) for r in range(planes)]
        + [(smalls[r], VMEM) for r in [0] + far],
        [(SDS((T, D), F32), HBM), (SDS((TAIL, D), F32), VMEM)],
        [VMEM((T, D), F32), VMEM((T, D), F32), sems(8)],
        after=[h2_first],
    )

    steps = [1 << i for i in range(places.bit_length() - 1)]
    hop_small = lambda v, step: v + lax.ppermute(v, "dp", [(a, a ^ step) for a in range(places)])
    small, h3_first, h0_core, *seconds = now(small, h3_first, h0_core, *seconds)
    h3, small = (h3_keep, h3_core, h3_first), hop_small(small, steps[0])
    (h0_first,), (h3_second,) = hop_first((h0_keep, h0_core)), hop_second(h3)
    heads_of = {r: to_plane(total(*h, v).astype(BF), r) for r, h, v in zip((r2, r1), (h2, h1), seconds)}
    small, h0_first, h3_second, *came = now(small, h0_first, h3_second, *(units_of[r] for r in far))
    units_of.update(zip(far, came))
    h0, small = (h0_keep, h0_core, h0_first), hop_small(small, steps[1])
    (h0_second,) = hop_second(h0)
    heads_of[r3] = to_plane(total(*h3, h3_second).astype(BF), r3)
    for step in steps[2:]:
        small = hop_small(small, step)
    tails = {0: small, **{r: to_plane(small, r) for r in far}}
    heads_of[0] = total(*h0, h0_second)

    m = D // places
    units = units_of[0] + sum(f32(units_of[r]) for r in far)
    hd = heads_of[0] + sum(f32(heads_of[r]) for r in far)
    grad_w_up, grad_w_down = units[:m], units[m:].T
    grad_w_qkv = hd[:, : 3 * e].reshape(m, 3, e).transpose(1, 0, 2)
    grad_w_out = hd[:, 3 * e :].T

    seat = {r: i for i, r in enumerate([0] + far)}
    size = D // (places * planes)
    spots = jnp.stack([(d * planes + z) * size, d * (H // places), d * (e // places)]).astype(jnp.int32)
    *vecs, grad_bias_up, grad_bias_qv = call(
        partial(cut_sums_kernel, [seat[r] for r in range(planes)]),
        "cutsums",
        1,
        16,
        [(spots, SMEM)] + [(tails[r], VMEM) for r in range(planes)],
        [(SDS((size,), F32), VMEM)] * 6 + [(SDS((H // places,), F32), VMEM), (SDS((2, e // places), F32), VMEM)],
        [],
    )
    return (
        result,
        grad_tokens,
        vecs[0],
        vecs[1],
        grad_w_qkv,
        grad_bias_qv,
        grad_w_out,
        vecs[2],
        vecs[3],
        vecs[4],
        grad_w_up,
        grad_bias_up,
        grad_w_down,
        vecs[5],
    )


def solution(mesh):
    return jax.shard_map(
        partial(on_device, mesh.shape["dp"], mesh.shape["mp"]),
        mesh=mesh,
        in_specs=(
            P(("dp", "mp"), None),
            P("dp", None),
            P(),
            P(),
            P(None, None, "mp"),
            P(None, "mp"),
            P("mp", None),
            P(),
            P(),
            P(),
            P(None, "mp"),
            P("mp"),
            P("mp", None),
            P(),
            P(("dp", "mp"), None),
        ),
        out_specs=(
            P(("dp", "mp"), None),
            P(("dp", "mp"), None),
            P(("dp", "mp")),
            P(("dp", "mp")),
            P(None, "dp", "mp"),
            P(None, ("mp", "dp")),
            P("mp", "dp"),
            P(("dp", "mp")),
            P(("dp", "mp")),
            P(("dp", "mp")),
            P("dp", "mp"),
            P(("mp", "dp")),
            P("mp", "dp"),
            P(("dp", "mp")),
        ),
        check_vma=False,
    )
```

```python
from functools import partial

import jax
import jax.numpy as jnp
import numpy as np
from jax import lax
from jax.experimental import pallas as pl
from jax.experimental.pallas import tpu as pltpu
from jax.sharding import PartitionSpec as P

F32, BF = jnp.float32, jnp.bfloat16
HEAD_DIM = 64
MOST = 256
EPSILON = 1e-06
MASKED = -1e30
LOG2E = 1.4426950408889634
ROOT_HALF = 0.7071067811865476
RSQRT_2PI = 0.3989422804014327
PARTS = 8
KEY_BLOCK = 128
TAIL = 16
GATHERED, EXCHANGED, PLACE = 8, 16, 24
VMEM, SMEM, HBM = pltpu.VMEM, pltpu.SMEM, pltpu.HBM
LANES = 128
SDS = jax.ShapeDtypeStruct


def _dot(a, b, i, j):
    return lax.dot_general(a, b, (((i,), (j,)), ((), ())), preferred_element_type=F32)


def nn(a, b):
    return _dot(a, b, 1, 0)


def nt(a, b):
    return _dot(a, b, 1, 1)


def tn(a, b):
    return _dot(a, b, 0, 0)


def tt(a, b):
    return _dot(a, b, 0, 1)


def call(body, name, us, megabytes, ins, outs, scratch, after=()):
    count, skip = len(ins), len(ins) + len(after)

    def kernel(*refs):
        body(*refs[:count], *refs[skip:])

    pinned = lambda o, m: HBM(o.shape, o.dtype) if m is HBM else o
    there = lambda a, m: pltpu.with_memory_space_constraint(a, HBM) if m is HBM else a
    return pl.pallas_call(
        kernel,
        out_shape=tuple(pinned(*o) for o in outs),
        in_specs=[pl.BlockSpec(memory_space=m) for _, m in ins] + [pl.BlockSpec(memory_space=pl.ANY)] * len(after),
        out_specs=tuple(pl.BlockSpec(memory_space=m) for _, m in outs),
        scratch_shapes=scratch,
        compiler_params=pltpu.CompilerParams(vmem_limit_bytes=megabytes << 20),
        cost_estimate=pl.CostEstimate(flops=int(us * 1.0e9), bytes_accessed=1 << 20, transcendentals=0),
        name=name,
    )(*(there(*a) for a in ins), *after)


class Mover:
    def __init__(self, sems):
        self.sems, self.used = sems, 0

    def __call__(self, src, dst):
        c = pltpu.make_async_copy(src, dst, self.sems.at[self.used])
        self.used += 1
        c.start()
        return c


def wait(*copies):
    for c in copies:
        c.wait()


def windows(slots, width=256):
    out = []
    for q0 in range(0, slots, width):
        qn = min(width, slots - q0)
        lo = max(0, (q0 - MOST + 1) // 128 * 128)
        hi = min(slots, -(-(q0 + qn + MOST - 1) // 128) * 128)
        out.append((q0, qn, lo, hi - lo))
    return out


def segments(info, clips, shape, axis):
    place = lax.broadcasted_iota(jnp.int32, shape, axis)
    seg = jnp.zeros(shape, jnp.int32)
    for c in range(clips):
        seg = seg + jnp.where(place >= info[c], 1, 0)
    return jnp.where(seg == clips - 1, place + clips, seg)


def fill_mask(bias_sc, segc, segr, q0, qn, k0, w):
    for b in range(0, w, KEY_BLOCK):
        same = segc[k0 + b : k0 + b + KEY_BLOCK, :] == segr[:, q0 : q0 + qn]
        bias_sc[b : b + KEY_BLOCK, :qn] = jnp.where(same, 0.0, MASKED)


def fold(x, f):
    return f(x.reshape(x.shape[0] // 8, 8, x.shape[1]), axis=0)


def attend(tl, heads, scale, qkvT, kn, segc, segr, oT, lse, bias_sc, s_sc, p_sc):
    e, hd = heads * HEAD_DIM, HEAD_DIM

    def scores(tile, h):
        q0, qn, k0, w = tl[tile]
        if h == 0:
            fill_mask(bias_sc.at[tile % 2], segc, segr, q0, qn, k0, w)
        q = qkvT[h * hd : (h + 1) * hd, q0 : q0 + qn]
        m = None
        for b in range(0, w, KEY_BLOCK):
            k = slice(b, b + KEY_BLOCK)
            s = nn(kn[h, k0 + b : k0 + b + KEY_BLOCK, :], q) * scale + bias_sc[tile % 2, k, :qn]
            s_sc[h, k, :qn] = s
            mb = fold(s, jnp.max)
            m = mb if m is None else jnp.maximum(m, mb)
        return jnp.max(m, axis=0, keepdims=True)

    def finish(tile, h, m):
        q0, qn, k0, w = tl[tile]
        total = None
        for b in range(0, w, KEY_BLOCK):
            p = jnp.exp2(s_sc[h, b : b + KEY_BLOCK, :qn] - m)
            p_sc[h, b : b + KEY_BLOCK, :qn] = p.astype(BF)
            lb = fold(p, jnp.sum)
            total = lb if total is None else total + lb
        total = jnp.sum(total, axis=0, keepdims=True)
        o = nn(qkvT[2 * e + h * hd : 2 * e + (h + 1) * hd, k0 : k0 + w], p_sc[h, :w, :qn])
        oT[h * hd : (h + 1) * hd, q0 : q0 + qn] = (o * (1.0 / total)).astype(BF)
        lse[h : h + 1, q0 : q0 + qn] = m + jnp.log2(total)

    steps = [(tile, h) for tile in range(len(tl)) for h in range(heads)]
    ahead = scores(*steps[0])
    for at, step in enumerate(steps):
        m = ahead
        if at + 1 < len(steps):
            ahead = scores(*steps[at + 1])
        finish(*step, m)


def unit(x):
    y = x - jnp.mean(x, axis=1, keepdims=True)
    inverse = lax.rsqrt(jnp.mean(y * y, axis=1, keepdims=True) + EPSILON)
    return y * inverse, inverse


def unit_back(up, n, inverse, gain):
    g = up * gain
    return inverse * (g - jnp.mean(g, axis=1, keepdims=True) - n * jnp.mean(g * n, axis=1, keepdims=True))


def normal(u):
    bell = jnp.exp2(u * u * (-0.5 * LOG2E))
    d = jnp.abs(u) * (0.3275911 * ROOT_HALF) + 1.0
    t = pl.reciprocal(d, approx=True)
    t = t * (2.0 - d * t)
    q = 0.5 * 1.061405429
    for c in (-1.453152027, 1.421413741, -0.284496736, 0.254829592):
        q = q * t + 0.5 * c
    q = q * t * bell
    return jnp.where(u >= 0.0, 1.0 - q, q), bell * RSQRT_2PI


def blocks_out(move, info, source, place, keep, send):
    n, half = source.shape[0] // PARTS, PARTS // 2
    copies = []
    for j in range(PARTS):
        row = pl.ds(pl.multiple_of(info[EXCHANGED + j] * n, n), n)
        out = keep if j < half else send
        if move is None:
            out[j % half, place : place + n, :] = source[row, :]
        else:
            copies.append(move(source.at[row], out.at[j % half, pl.ds(place, n)]))
    return copies


def cut_kernel(info, w_heads, w_out, w_up, w_down, bias_qv, bias_up, piece, units, tail_s, sems):
    e, H = w_out.shape[0], bias_up.shape[1]
    n = units.shape[0] // 2
    move = Mover(sems)
    at = info[PLACE]
    row = pl.ds(pl.multiple_of(at * n, n), n)
    edge = w_heads.shape[0] // n
    loads = [move(w_up.at[row], units.at[pl.ds(0, n)]), move(w_down.at[row], units.at[pl.ds(n, n)])]
    tail_s[...] = jnp.zeros_like(tail_s)
    tail_s[0:1, :H] = bias_up[...].astype(F32)
    for i in range(2):
        tail_s[1:2, 256 * i : 256 * i + e] = bias_qv[i : i + 1, :].astype(F32)
    piece[pl.ds(n, TAIL), :] = tail_s[...].astype(BF)

    @pl.when(at < edge)
    def _():
        src = w_heads.at[pl.ds(pl.multiple_of(jnp.minimum(at, edge - 1) * n, n), n)]
        wait(move(src, piece.at[pl.ds(0, n)]))

    @pl.when(at >= edge)
    def _():
        src = w_out.at[pl.ds(pl.multiple_of(jnp.maximum(at - edge, 0) * n, n), n)]
        wait(move(src, piece.at[pl.ds(0, n)]))

    wait(*loads)


def project(heads, n1, w, piece, qkvT):
    e = heads * HEAD_DIM
    n = piece.shape[0] - TAIL
    biases = piece[n : n + TAIL, :512].astype(F32)[1:2, :]
    for c in range(3):
        t = nt(w[c * e : (c + 1) * e, :], n1[...])
        if c != 1:
            at = 128 * c
            t = t + jnp.broadcast_to(biases[:, at : at + 256], (LANES, 256)).T[:e, :1]
        qkvT[c * e : (c + 1) * e, :] = t.astype(BF)


def attend_kernel(clips, tl, heads, scale, info, qkvT, oT, lse, kn, bias_sc, s_sc, p_sc):
    slots = qkvT.shape[1]
    segc = segments(info, clips, (slots, 1), 0)
    segr = segments(info, clips, (1, slots), 1)
    e = heads * HEAD_DIM
    for h in range(heads):
        kn[h] = qkvT[e + h * HEAD_DIM : e + (h + 1) * HEAD_DIM, :].T
    attend(tl, heads, scale, qkvT, kn, segc, segr, oT, lse, bias_sc, s_sc, p_sc)


def first_kernel(heads, x, gain, shift, w, piece, n1, qkvT):
    for i in range(0, x.shape[0], LANES):
        n, _ = unit(x[i : i + LANES, :].astype(F32))
        n1[i : i + LANES, :] = (n * gain[...].astype(F32) + shift[...].astype(F32)).astype(BF)
    project(heads, n1, w, piece, qkvT)


def attn_kernel(clips, tl, heads, scale, info, n1, piece, p4, r4, w, qkvT, oT, lse, *scratch):
    n = w.shape[0] // PARTS
    for i in range(PARTS):
        ref = (p4, r4)[i // 4]
        w[pl.ds(pl.multiple_of(info[GATHERED + i] * n, n), n), :] = ref[i % 4 * n : (i % 4 + 1) * n, :]
    project(heads, n1, w, piece, qkvT)
    attend_kernel(clips, tl, heads, scale, info, qkvT, oT, lse, *scratch)


def chunk_front(n2, cot, wup, wdn, piece, hid, gp, gb):
    n = piece.shape[0] - TAIL
    u = nn(n2[...], wup[...]) + piece[n : n + TAIL, :].astype(F32)[0:1, : wup.shape[1]]
    ga = nt(cot[...], wdn[...])
    dist, dens = normal(u)
    hid[...] = (u * dist).astype(BF)
    g = (ga * (dist + u * dens)).astype(BF)
    gp[...] = g
    gb[...] = jnp.sum(g.astype(F32), axis=0, keepdims=True)


def chunk_sums(hid, gp, wup, wdn, out_acc, g_acc, fresh):
    o = nn(hid[...], wdn[...])
    out_acc[...] = o if fresh else out_acc[...] + o
    g = nt(gp[...], wup[...])
    g_acc[...] = g if fresh else g_acc[...] + g


def chunk_grads(move, info, n2, cot, hid, gp, up_sc, dn_sc, k, keep, send):
    n = n2.shape[1] // PARTS
    dn_sc[...] = tn(cot[...], hid[...]).astype(BF)
    copies = blocks_out(move, info, dn_sc, (2 * k + 1) * n, keep, send)
    up_sc[...] = tn(n2[...], gp[...]).astype(BF)
    return copies + blocks_out(move, info, up_sc, 2 * k * n, keep, send)


def mid_kernel(x, bias_out, gain, shift, *refs):
    count = (len(refs) - 6) // 2
    o, w, refs = refs[:count], refs[count : 2 * count], refs[2 * count :]
    mixed, n2, o_s, wo_s, mixed_s, sems = refs
    e = o[0].shape[0]
    move = Mover(sems)
    for r in range(count):
        o_s[r * e : (r + 1) * e, :] = o[r][...]
        wo_s[r * e : (r + 1) * e, :] = w[r][w[r].shape[0] - e :, :]
    mixed_s[...] = tn(o_s[...], wo_s[...])
    done = []
    for i in range(0, x.shape[0], LANES):
        k = slice(i, i + LANES)
        m = mixed_s[k, :] + x[k, :].astype(F32) + bias_out[...].astype(F32)
        mixed_s[k, :] = m
        done.append(move(mixed_s.at[pl.ds(i, LANES)], mixed.at[pl.ds(i, LANES)]))
        n, _ = unit(m)
        n2[k, :] = (n * gain[...].astype(F32) + shift[...].astype(F32)).astype(BF)
    wait(*done)


def own_kernel(info, n2, cot, piece, wup, wdn, out, g, keep, send, gb, out_s, g_s, hid, gp, up_sc, dn_sc, sems):
    move = Mover(sems)
    chunk_front(n2, cot, wup, wdn, piece, hid, gp, gb)
    chunk_sums(hid, gp, wup, wdn, out_s, g_s, True)
    done = [move(out_s, out), move(g_s, g)]
    wait(*chunk_grads(move, info, n2, cot, hid, gp, up_sc, dn_sc, 0, keep, send), *done)


def units_here(info, refs, wup, wdn, k, count):
    n = wup.shape[0] // PARTS
    for i in range(PARTS):
        ref, at = refs[i // 2], (i % 2 * count + k) * 2 * n
        row = pl.ds(pl.multiple_of(info[GATHERED + i] * n, n), n)
        wup[row, :] = ref[at : at + n, :]
        wdn[row, :] = ref[at + n : at + 2 * n, :]


def mlp_kernel(count, info, n2, cot, out_in, g_in, own, own2, core, core2, *refs):
    piece, refs = refs[:count], refs[count:]
    out, g, keep, send, gb, out_s, g_s, hid, gp, up_sc, dn_sc, wup, wdn, sems = refs
    move = Mover(sems)
    sums = [move(out_in, out_s), move(g_in, g_s)]
    done = []
    for k in range(count):
        units_here(info, (own, own2, core, core2), wup, wdn, k, count)
        chunk_front(n2, cot, wup, wdn, piece[k], hid, gp, gb.at[pl.ds(k, 1)])
        if k == 0:
            wait(*sums)
        chunk_sums(hid, gp, wup, wdn, out_s, g_s, False)
        wait(*done)
        done = []
        if k == count - 1:
            done = [move(out_s, out), move(g_s, g)]
        done += chunk_grads(move, info, n2, cot, hid, gp, up_sc, dn_sc, k, keep, send)
    wait(*done)


def mlp_last_kernel(info, n2, cot, out_in, g_in, own, own2, core, core2, piece, mixed, bias_down, gain, *refs):
    gbs, refs = refs[: len(refs) - 17], refs[len(refs) - 17 :]
    result, grad_mixed, branch, keep, send, sm = refs[:6]
    out_s, g_s, hid, gp, up_sc, dn_sc, wup, wdn, mixed_s, result_s, sems = refs[6:]
    move = Mover(sems)
    sums = [move(out_in, out_s), move(g_in, g_s), move(mixed, mixed_s)]
    units_here(info, (own, own2, core, core2), wup, wdn, 0, 1)
    chunk_front(n2, cot, wup, wdn, piece, hid, gp, sm.at[pl.ds(7, 1)])
    wait(*sums)
    chunk_sums(hid, gp, wup, wdn, out_s, g_s, False)
    vecs = [0.0] * 4
    for i in range(0, n2.shape[0], LANES):
        k = slice(i, i + LANES)
        up, mid, c = g_s[k, :], mixed_s[k, :], cot[k, :].astype(F32)
        result_s[k, :] = (mid + out_s[k, :] + bias_down[...].astype(F32)).astype(BF)
        m, inverse = unit(mid)
        gm = c + unit_back(up, m, inverse, gain[...].astype(F32))
        mixed_s[k, :] = gm
        branch[k, :] = gm.astype(BF)
        for j, v in enumerate((gm, up * m, up, c)):
            vecs[j] = vecs[j] + fold(v, jnp.sum)
    done = [move(mixed_s, grad_mixed), move(result_s, result)]
    for j in range(4):
        sm[j : j + 1, :] = jnp.sum(vecs[j], axis=0, keepdims=True)
    at = 4
    for ref in gbs:
        sm[at : at + ref.shape[0], :] = ref[...]
        at += ref.shape[0]
    done += chunk_grads(move, info, n2, cot, hid, gp, up_sc, dn_sc, 0, keep, send)
    wait(*done)


def back_heads(clips, tl, heads, scale, part, info, gb, w, q_s, oT, lse, d_s, scratch):
    kn, vn, ga, bias_sc, pb_sc, ds_sc, dk, dv = scratch
    e, hd = heads * HEAD_DIM, HEAD_DIM
    slots = gb.shape[0]
    segc = segments(info, clips, (slots, 1), 0)
    segr = segments(info, clips, (1, slots), 1)
    ga[...] = nt(w[w.shape[0] - e :, :], gb[...]).astype(BF)
    for h in range(heads):
        kn[h] = q_s[e + h * hd : e + (h + 1) * hd, :].T
        vn[h] = q_s[2 * e + h * hd : 2 * e + (h + 1) * hd, :].T
    dk[...] = jnp.zeros_like(dk)
    dv[...] = jnp.zeros_like(dv)

    def scores(tile, h):
        q0, qn, k0, wide = tl[tile]
        if h == 0:
            fill_mask(bias_sc.at[tile % 2], segc, segr, q0, qn, k0, wide)
        hs = slice(h * hd, (h + 1) * hd)
        q, go = q_s[hs, q0 : q0 + qn], ga[hs, q0 : q0 + qn]
        total = lse[h : h + 1, q0 : q0 + qn]
        centre = jnp.sum(go.astype(F32) * oT[hs, q0 : q0 + qn].astype(F32), axis=0, keepdims=True)
        for b in range(0, wide, KEY_BLOCK):
            k, v = slice(b, b + KEY_BLOCK), slice(k0 + b, k0 + b + KEY_BLOCK)
            p = jnp.exp2(nn(kn[h, v, :], q) * scale + bias_sc[tile % 2, k, :qn] - total)
            pb_sc[h, k, :qn] = p.astype(BF)
            ds_sc[h, k, :qn] = (p * (nn(vn[h, v, :], go) - centre)).astype(BF)

    def finish(tile, h):
        q0, qn, k0, wide = tl[tile]
        hs = slice(h * hd, (h + 1) * hd)
        q, go = q_s[hs, q0 : q0 + qn], ga[hs, q0 : q0 + qn]
        ds = ds_sc[h, :wide, :qn]
        d_s[hs, q0 : q0 + qn] = (nn(q_s[e + h * hd : e + (h + 1) * hd, k0 : k0 + wide], ds) * part).astype(BF)
        dk[hs, k0 : k0 + wide] += nt(q, ds)
        dv[hs, k0 : k0 + wide] += nt(go, pb_sc[h, :wide, :qn])

    steps = [(tile, h) for tile in range(len(tl)) for h in range(heads)]
    scores(*steps[0])
    for at, step in enumerate(steps):
        if at + 1 < len(steps):
            scores(*steps[at + 1])
        finish(*step)
    d_s[e : 2 * e, :] = (dk[...] * part).astype(BF)
    d_s[2 * e : 3 * e, :] = dv[...].astype(BF)


def bias_rows(d_s, small, at, e):
    rows = nt(jnp.ones((8, d_s.shape[1]), BF), d_s[...])
    small[at : at + 1, 0:e] = rows[0:1, 0:e]
    small[at : at + 1, 256 : 256 + e] = rows[0:1, 2 * e : 3 * e]


def head_grads(move, info, gb, n1, oT, d_s, acc, keep, send):
    k = d_s.shape[0]
    acc[:, :k] = tt(n1[...], d_s[...]).astype(BF)
    acc[:, k:] = tt(gb[...], oT[...]).astype(BF)
    return blocks_out(move, info, acc, 0, keep, send)


def back_kernel(clips, tl, heads, scale, part, info, gb, n1, q, w, oT, lse, d, keep, send, small, acc, *scratch):
    small[...] = jnp.zeros_like(small)
    back_heads(clips, tl, heads, scale, part, info, gb, w, q, oT, lse, d, scratch)
    bias_rows(d, small, 0, heads * HEAD_DIM)
    head_grads(None, info, gb, n1, oT, d, acc, keep, send)


def last_kernel(planes, x, gain, grad_mixed, sm1, *refs):
    d, w, smalls = refs[:planes], refs[planes : 2 * planes], refs[2 * planes : 3 * planes]
    grad_tokens, sm, g_sc, gm_s, sems = refs[3 * planes :]
    rows = d[0].shape[0]
    move = Mover(sems)
    for r in range(planes):
        g = tn(d[r][...], w[r][:rows, :])
        g_sc[...] = g if r == 0 else g_sc[...] + g
    vecs, done = [0.0] * 2, []
    for i in range(0, x.shape[0], LANES):
        k = slice(i, i + LANES)
        up = g_sc[k, :]
        m, inverse = unit(x[k, :].astype(F32))
        gm_s[k, :] = grad_mixed[k, :] + unit_back(up, m, inverse, gain[...].astype(F32))
        done.append(move(gm_s.at[pl.ds(i, LANES)], grad_tokens.at[pl.ds(i, LANES)]))
        for j, v in enumerate((up * m, up)):
            vecs[j] = vecs[j] + fold(v, jnp.sum)
    sm[...] = jnp.zeros_like(sm)
    for j in range(2):
        sm[j : j + 1, :] = jnp.sum(vecs[j], axis=0, keepdims=True)
    for r in range(planes):
        sm[2 + r : 3 + r, :512] = smalls[r][...]
    sm[6:14, :] = sm1[...]
    wait(*done)


def on_device(
    places,
    planes,
    tokens,
    clip_lengths,
    gain_attn,
    shift_attn,
    w_qkv,
    bias_qv,
    w_out,
    bias_out,
    gain_mlp,
    shift_mlp,
    w_up,
    bias_up,
    w_down,
    bias_down,
    cotangent,
):
    T, D = tokens.shape
    clips = clip_lengths.shape[1]
    e = w_out.shape[0]
    heads = e // HEAD_DIM
    H = w_up.shape[1]
    n = D // PARTS
    rest = places // PARTS
    d, z = lax.axis_index("dp"), lax.axis_index("mp")
    hi = d // rest
    f32 = lambda v: v.astype(F32)
    row = lambda v: v.reshape(1, -1)

    core = hi % 2
    first, second = jnp.where(core == 0, 2, 4), jnp.where(core == 0, 4, 2)
    both = lambda a, f, s: [a, a ^ f, a ^ s, a ^ 6]
    order = lambda a, f, s: [a, a ^ s, a ^ f, a ^ 6]
    gathered = both(hi, first, second) + both(hi ^ 1, second, first)
    exchanged = order(hi, first, second) + order(hi ^ 1, second, first)
    ends = jnp.cumsum(lax.dynamic_index_in_dim(clip_lengths, z, 0, keepdims=False))
    ends = jnp.concatenate([ends, jnp.zeros((GATHERED - clips,), jnp.int32)])
    info = jnp.concatenate([ends, jnp.stack(gathered + exchanged + [hi]).astype(jnp.int32)])

    def over_plane(v, flip):
        to = lambda a: ((a // rest) ^ flip((a // rest) % 2)) * rest + a % rest
        return lax.ppermute(v, "dp", [(a, to(a)) for a in range(places)])

    to_core = lambda v: over_plane(v, lambda c: 1)
    to_first = lambda v: over_plane(v, lambda c: 4 if c else 2)
    to_second = lambda v: over_plane(v, lambda c: 2 if c else 4)
    to_both = lambda v: over_plane(v, lambda c: 6)
    shift = lambda v, r: lax.ppermute(v, "mp", [(a, (a + r) % planes) for a in range(planes)])
    from_plane = lambda v, r: shift(v, -r)
    to_plane = shift

    def now(*arrays):
        return lax.optimization_barrier(arrays)

    near, last_far = [1, 3], 2
    far = near + [last_far]

    sems = lambda k: pltpu.SemaphoreType.DMA((k,))
    w_heads = w_qkv.transpose(0, 2, 1).reshape(3 * e, D)
    piece, unit_piece = call(
        cut_kernel,
        "cut",
        2,
        16,
        [(info, SMEM), (w_heads, HBM), (w_out, HBM), (w_up, HBM), (w_down, HBM), (bias_qv, VMEM), (row(bias_up), VMEM)],
        [(SDS((n + TAIL, D), BF), VMEM), (SDS((2 * n, D), BF), VMEM)],
        [VMEM((TAIL, D), F32), sems(8)],
    )
    pieces = {0: piece, **{r: from_plane(piece, r) for r in far}}

    tl = windows(T)
    wm, qm = max(t[3] for t in tl), max(t[1] for t in tl)
    scale = HEAD_DIM**-0.5 * LOG2E
    attn_out = [(SDS((3 * e, T), BF), VMEM), (SDS((e, T), BF), VMEM), (SDS((8, T), F32), VMEM)]
    attn_sc = [VMEM((heads, T, HEAD_DIM), BF), VMEM((2, wm, qm), F32), VMEM((heads, wm, qm), F32), VMEM((heads, wm, qm), BF)]
    n1, q0 = call(
        partial(first_kernel, heads),
        "first",
        4,
        20,
        [(tokens, VMEM), (row(gain_attn), VMEM), (row(shift_attn), VMEM), (w_heads, VMEM), (piece, VMEM)],
        [(SDS((T, D), BF), VMEM), attn_out[0]],
        [],
    )
    ws, qs, os, ls = {0: w_out}, {0: q0}, {}, {}

    def join(*v):
        return jnp.concatenate(v)

    def attn(r, c4, r4, after, us=7):
        ws[r], qs[r], os[r], ls[r] = call(
            partial(attn_kernel, clips, tl, heads, scale),
            f"attn{r}",
            us,
            24,
            [(info, SMEM), (n1, VMEM), (pieces[r], VMEM), (c4, VMEM), (r4, VMEM)],
            [(SDS((4 * e, D), BF), VMEM)] + attn_out,
            attn_sc,
            after=after,
        )
        return ls[r]

    a1, a3, a2 = far
    q0, p1, p3 = now(q0, pieces[a1], pieces[a3])
    got1 = [p1, to_first(p1), to_second(p1), to_both(p1)]
    f3 = to_first(p3)
    os[0], ls[0] = call(
        partial(attend_kernel, clips, tl, heads, scale),
        "attend0",
        4,
        20,
        [(info, SMEM), (q0, VMEM)],
        attn_out[1:],
        attn_sc,
    )
    _, p3, f3, p2, *got1 = now(ls[0], p3, f3, pieces[a2], *got1)
    c1, c3 = join(*(v[:n] for v in got1)), join(p3[:n], f3[:n])
    core1, s3, f2 = to_core(c1), to_second(c3), to_first(p2)
    near_piece = now(unit_piece, c1)[0]
    near_z = [from_plane(near_piece, r) for r in near]
    t = attn(a1, c1, core1, [])
    _, s3, f2, *near_z = now(t, s3, f2, *near_z)
    c3, c2, near_b = join(c3, s3), join(p2[:n], f2[:n]), join(*near_z)
    core3, s2, near_f = to_core(c3), to_second(c2), to_first(near_b)
    far_b = from_plane(near_z[0], 1)
    t = attn(a3, c3, core3, [c2, near_b])
    _, s2, near_f, far_b = now(t, s2, near_f, far_b)
    c2, near_b = join(c2, s2), join(near_b, near_f)
    core2, near_s, far_f = to_core(c2), to_second(near_b), to_first(far_b)
    attn(a2, c2, core2, [near_b])

    def block(i, keep, core, first):
        return f32(keep[i]) + f32(core[i]) + f32(first[i])

    def hop_first(*had):
        half = PARTS // 4
        return apart(to_first, [(f32(keep[half:]) + f32(core[half:])).astype(BF) for keep, core in had], 1)

    def hop_second(*had):
        return apart(to_second, [block(1, *v).astype(BF) for v in had], 0)

    def apart(hop, v, axis):
        if len(v) == 1:
            return [hop(v[0])]
        return jnp.split(hop(jnp.concatenate(v, axis)), np.cumsum([a.shape[axis] for a in v])[:-1], axis)

    def total(keep, core, first, second):
        k = block(0, keep, core, first) + f32(second)
        if rest > 1:
            groups = [[a * rest + b for b in range(rest)] for a in range(PARTS)]
            k = k.reshape(-1, n, k.shape[-1])
            k = lax.psum_scatter(k, "dp", scatter_dimension=1, axis_index_groups=groups, tiled=True)
            k = k.reshape(-1, k.shape[-1])
        return k

    half = PARTS // 2
    acts = [VMEM((T, D), F32)] * 2 + [VMEM((T, H), BF)] * 2 + [VMEM((D, H), BF)] * 2
    weights = [VMEM((D, H), BF), VMEM((H, D), BF)]
    grads = lambda k: [(SDS((half, k * 2 * n, H), BF), HBM)] * 2
    sums = [(SDS((T, D), F32), HBM)] * 2
    mixed, n2 = call(
        mid_kernel,
        "mid",
        6,
        24,
        [(tokens, VMEM), (row(bias_out), VMEM), (row(gain_mlp), VMEM), (row(shift_mlp), VMEM)]
        + [(os[r], VMEM) for r in range(planes)]
        + [(ws[r], VMEM) for r in range(planes)],
        [(SDS((T, D), F32), HBM), (SDS((T, D), BF), VMEM)],
        [VMEM((planes * e, T), BF), VMEM((planes * e, D), BF), VMEM((T, D), F32), sems(8)],
    )
    near_r = to_core(now(near_b, n2)[0])
    out_acc, g_acc, u0_keep, u0_send, gb0 = call(
        own_kernel,
        "own",
        2,
        40,
        [(info, SMEM), (n2, VMEM), (cotangent, VMEM), (piece, VMEM), (w_up, VMEM), (w_down, VMEM)],
        sums + grads(1) + [(SDS((1, H), F32), VMEM)],
        acts + [sems(24)],
    )
    gb0, near_r, near_s, far_f = now(gb0, near_r, near_s, far_f)
    far_b = join(far_b, far_f)
    near_r2, far_s, far_r, u0_core = to_core(near_s), to_second(far_b), to_core(far_b), to_core(u0_send)
    k = len(near)
    out_acc, g_acc, u13_keep, u13_send, gb13 = call(
        partial(mlp_kernel, k),
        "mlp",
        22,
        40,
        [(info, SMEM), (n2, VMEM), (cotangent, VMEM), (out_acc, HBM), (g_acc, HBM)]
        + [(v, VMEM) for v in (near_b, near_s, near_r, near_r2)]
        + [(pieces[r], VMEM) for r in near],
        sums + grads(k) + [(SDS((k, H), F32), VMEM)],
        acts + weights + [sems(40)],
        after=[far_b],
    )
    gb13, far_s, far_r, u0_core = now(gb13, far_s, far_r, u0_core)
    far_r2 = to_core(far_s)
    (u0_first,), u13_core = hop_first((u0_keep, u0_core)), to_core(u13_send)
    result, grad_mixed, branch, u2_keep, u2_send, sm1 = call(
        mlp_last_kernel,
        "mlplast",
        15,
        42,
        [(info, SMEM), (n2, VMEM), (cotangent, VMEM), (out_acc, HBM), (g_acc, HBM)]
        + [(v, VMEM) for v in (far_b, far_s, far_r, far_r2)]
        + [(pieces[last_far], VMEM), (mixed, HBM), (row(bias_down), VMEM), (row(gain_mlp), VMEM), (gb0, VMEM), (gb13, VMEM)],
        [(SDS((T, D), BF), HBM), (SDS((T, D), F32), HBM), (SDS((T, D), BF), VMEM)]
        + grads(1)
        + [(SDS((8, H), F32), VMEM)],
        acts + weights + [VMEM((T, D), F32), VMEM((T, D), BF), sems(32)],
    )

    back_sc = (
        [VMEM((heads, T, HEAD_DIM), BF)] * 2
        + [VMEM((e, T), BF)]
        + [VMEM((2, wm, qm), F32)]
        + [VMEM((heads, wm, qm), BF)] * 2
        + [VMEM((e, T), F32)] * 2
    )
    spec = (clips, tl, heads, scale, HEAD_DIM**-0.5)
    ins = lambda r: [(v, VMEM) for v in (branch, n1, qs[r], ws[r], os[r], ls[r])]
    ds, smalls = {}, {}

    def back(r, after):
        ds[r], keep, send, smalls[r] = call(
            partial(back_kernel, *spec),
            f"back{r}",
            11,
            30,
            [(info, SMEM)] + ins(r),
            [(SDS((3 * e, T), BF), VMEM)] + [(SDS((half, n, 4 * e), BF), VMEM)] * 2 + [(SDS((1, 512), F32), VMEM)],
            [VMEM((D, 4 * e), BF)] + back_sc,
            after=after,
        )
        return keep, send

    r2, r1, r3 = last_far, *near
    sm1, u0_first, u13_core = now(sm1, u0_first, u13_core)
    u0 = u0_keep, u0_core, u0_first
    (u0_second,), (u13_first,), u2_core = hop_second(u0), hop_first((u13_keep, u13_core)), to_core(u2_send)
    h2_keep, h2_send = back(r2, [sm1])
    t, u0_second, u2_core = now(smalls[r2], u0_second, u2_core)
    (u2_first,), h2_core = hop_first((u2_keep, u2_core)), to_core(h2_send)
    h1_keep, h1_send = back(r1, [t])
    t, u13_first, u2_first, h2_core = now(smalls[r1], u13_first, u2_first, h2_core)
    u13, u2 = (u13_keep, u13_core, u13_first), (u2_keep, u2_core, u2_first)
    seconds, h1_core = hop_second(u13, u2), to_core(h1_send)
    units_of = {0: total(*u0, u0_second)}
    h3_keep, h3_send = back(r3, [t])
    t, h1_core, *seconds = now(smalls[r3], h1_core, *seconds)
    pair = total(*u13, seconds[0])
    rows = pair.shape[0] // len(near)
    for i, r in enumerate(near):
        units_of[r] = to_plane(pair[i * rows : (i + 1) * rows].astype(BF), r)
    units_of[r2] = to_plane(total(*u2, seconds[1]).astype(BF), r2)
    (h2_first, h1_first), h3_core = hop_first((h2_keep, h2_core), (h1_keep, h1_core)), to_core(h3_send)
    h0_keep, h0_send = back(0, [t])
    t, h2_first, h1_first, h3_core = now(smalls[0], h2_first, h1_first, h3_core)
    h2, h1 = (h2_keep, h2_core, h2_first), (h1_keep, h1_core, h1_first)
    seconds = hop_second(h2, h1)
    (h3_first,), h0_core = hop_first((h3_keep, h3_core)), to_core(h0_send)
    grad_tokens, small = call(
        partial(last_kernel, planes),
        "last",
        8,
        20,
        [(tokens, VMEM), (row(gain_attn), VMEM), (grad_mixed, VMEM), (sm1, VMEM)]
        + [(ds[r], VMEM) for r in range(planes)]
        + [(ws[r] if r else w_heads, VMEM) for r in range(planes)]
        + [(smalls[r], VMEM) for r in [0] + far],
        [(SDS((T, D), F32), HBM), (SDS((TAIL, D), F32), VMEM)],
        [VMEM((T, D), F32), VMEM((T, D), F32), sems(8)],
        after=[h2_first],
    )

    steps = [1 << i for i in range(places.bit_length() - 1)]
    hop_small = lambda v, step: v + lax.ppermute(v, "dp", [(a, a ^ step) for a in range(places)])
    small, h3_first, h0_core, *seconds = now(small, h3_first, h0_core, *seconds)
    h3, small = (h3_keep, h3_core, h3_first), hop_small(small, steps[0])
    (h0_first,), (h3_second,) = hop_first((h0_keep, h0_core)), hop_second(h3)
    heads_of = {r: to_plane(total(*h, v).astype(BF), r) for r, h, v in zip((r2, r1), (h2, h1), seconds)}
    small, h0_first, h3_second, *came = now(small, h0_first, h3_second, *(units_of[r] for r in far))
    units_of.update(zip(far, came))
    h0, small = (h0_keep, h0_core, h0_first), hop_small(small, steps[1])
    (h0_second,) = hop_second(h0)
    heads_of[r3] = to_plane(total(*h3, h3_second).astype(BF), r3)
    for step in steps[2:]:
        small = hop_small(small, step)
    tails = {0: small, **{r: to_plane(small, r) for r in far}}
    heads_of[0] = total(*h0, h0_second)

    m = D // places
    units = units_of[0] + sum(f32(units_of[r]) for r in far)
    hd = heads_of[0] + sum(f32(heads_of[r]) for r in far)
    grad_w_up, grad_w_down = units[:m], units[m:].T
    grad_w_qkv = hd[:, : 3 * e].reshape(m, 3, e).transpose(1, 0, 2)
    grad_w_out = hd[:, 3 * e :].T

    seat = {r: i for i, r in enumerate([0] + far)}
    g_ga, g_sa, g_bo, g_gm, g_sm, g_bd = [sum(v[j] for v in tails.values()) for j in (0, 1, 6, 7, 8, 9)]
    bu = sum(tails[r][10 + seat[r]] for r in range(planes))
    qv = sum(tails[r][2 + seat[r]] for r in range(planes))
    slice_of = lambda v, at, size: lax.dynamic_slice_in_dim(v, at, size, v.ndim - 1)
    size = D // (places * planes)
    vecs = [slice_of(v, (d * planes + z) * size, size) for v in (g_ga, g_sa, g_bo, g_gm, g_sm, g_bd)]
    grad_bias_up = slice_of(bu, d * (H // places), H // places)
    qv = jnp.stack([qv[:e], qv[256 : 256 + e]])
    grad_bias_qv = slice_of(qv, d * (e // places), e // places)
    return (
        result,
        grad_tokens,
        vecs[0],
        vecs[1],
        grad_w_qkv,
        grad_bias_qv,
        grad_w_out,
        vecs[2],
        vecs[3],
        vecs[4],
        grad_w_up,
        grad_bias_up,
        grad_w_down,
        vecs[5],
    )


def solution(mesh):
    return jax.shard_map(
        partial(on_device, mesh.shape["dp"], mesh.shape["mp"]),
        mesh=mesh,
        in_specs=(
            P(("dp", "mp"), None),
            P("dp", None),
            P(),
            P(),
            P(None, None, "mp"),
            P(None, "mp"),
            P("mp", None),
            P(),
            P(),
            P(),
            P(None, "mp"),
            P("mp"),
            P("mp", None),
            P(),
            P(("dp", "mp"), None),
        ),
        out_specs=(
            P(("dp", "mp"), None),
            P(("dp", "mp"), None),
            P(("dp", "mp")),
            P(("dp", "mp")),
            P(None, "dp", "mp"),
            P(None, ("mp", "dp")),
            P("mp", "dp"),
            P(("dp", "mp")),
            P(("dp", "mp")),
            P(("dp", "mp")),
            P("dp", "mp"),
            P(("mp", "dp")),
            P("mp", "dp"),
            P(("dp", "mp")),
        ),
        check_vma=False,
    )
```
